32 devices in a mesh: section: 2 (over y), dp: 16 (over z, x, core).
Axes of the slice: x: 2, y: 2, z: 4, core: 2. Of those that a mesh axis runs over, the one named last changes fastest.
Arguments:
- features: bfloat16 [32, 1024, 512], P('dp', None, 'section'), may hold values from -6 to 6
- conv_weight: bfloat16 [1024, 512], P(('section', 'dp')), may hold values from -0.1875 to 0.1875
- ln0_gain: bfloat16 [512], P(('section', 'dp')), may hold values from 0.25 to 1.75
- ln0_bias: bfloat16 [512], P(('section', 'dp')), may hold values from -1.75 to 1.75
- proj0_weight: bfloat16 [512, 768], P(('section', 'dp')), may hold values from -0.25 to 0.25
- proj0_bias: bfloat16 [768], P(('section', 'dp')), may hold values from -1.75 to 1.75
- mask_emb: bfloat16 [768], P(('section', 'dp')), may hold values from -6 to 6
- qkv_weight: bfloat16 [768, 2304], P(('section', 'dp')), may hold values from -0.21875 to 0.21875
- qv_bias: bfloat16 [1536], P(('section', 'dp')), may hold values from -1.75 to 1.75
- out_weight: bfloat16 [768, 768], P(('section', 'dp')), may hold values from -1.75 to 1.75
- out_bias: bfloat16 [768], P(('section', 'dp')), may hold values from -1.75 to 1.75
- ln1_gain: bfloat16 [768], P(('section', 'dp')), may hold values from 0.25 to 1.75
- ln1_bias: bfloat16 [768], P(('section', 'dp')), may hold values from -1.75 to 1.75
- up_weight: bfloat16 [768, 3072], P(('section', 'dp')), may hold values from -0.21875 to 0.21875
- up_bias: bfloat16 [3072], P(('section', 'dp')), may hold values from -1.75 to 1.75
- down_weight: bfloat16 [3072, 768], P(('section', 'dp')), may hold values from -0.109375 to 0.109375
- down_bias: bfloat16 [768], P(('section', 'dp')), may hold values from -1.75 to 1.75
- ln2_gain: bfloat16 [768], P(('section', 'dp')), may hold values from 0.25 to 1.75
- ln2_bias: bfloat16 [768], P(('section', 'dp')), may hold values from -1.75 to 1.75
- final_weight: bfloat16 [768, 256], P(('section', 'dp')), may hold values from -0.21875 to 0.21875
- final_bias: bfloat16 [256], P(('section', 'dp')), may hold values from -1.75 to 1.75
- codebook: bfloat16 [2, 320, 128], replicated, may hold values from -6 to 6
- lengths: int32 [32, 3], P('dp'), may hold values from 32 to 384, as said below
- mask_pos: int32 [32, 256], P('dp'), may hold values from 0 to 511, as said below
- distractors: int32 [32, 256, 100], P('dp'), may hold values from 0 to 511, as said below
- target_ids: int32 [32, 2, 512], P('dp'), may hold values from 0 to 319
Outputs:
- loss: float32 [32], P('dp')
- features_grad: float32 [32, 1024, 512], P('dp', None, 'section')
- conv_weight_grad: float32 [1024, 512], P(('section', 'dp'))
- ln0_gain_grad: float32 [512], P(('section', 'dp'))
- ln0_bias_grad: float32 [512], P(('section', 'dp'))
- proj0_weight_grad: float32 [512, 768], P(('section', 'dp'))
- proj0_bias_grad: float32 [768], P(('section', 'dp'))
- mask_emb_grad: float32 [768], P(('section', 'dp'))
- qkv_weight_grad: float32 [768, 2304], P(('section', 'dp'))
- qv_bias_grad: float32 [1536], P(('section', 'dp'))
- out_weight_grad: float32 [768, 768], P(('section', 'dp'))
- out_bias_grad: float32 [768], P(('section', 'dp'))
- ln1_gain_grad: float32 [768], P(('section', 'dp'))
- ln1_bias_grad: float32 [768], P(('section', 'dp'))
- up_weight_grad: float32 [768, 3072], P(('section', 'dp'))
- up_bias_grad: float32 [3072], P(('section', 'dp'))
- down_weight_grad: float32 [3072, 768], P(('section', 'dp'))
- down_bias_grad: float32 [768], P(('section', 'dp'))
- ln2_gain_grad: float32 [768], P(('section', 'dp'))
- ln2_bias_grad: float32 [768], P(('section', 'dp'))
- final_weight_grad: float32 [768, 256], P(('section', 'dp'))
- final_bias_grad: float32 [256], P(('section', 'dp'))
The draws below stay inside these ranges and needn't reach their ends.
Inputs may be any that keep to these rules, and one draw needn't show every extreme that they name: Each row holds the lengths of the 3 utterances of one micro-batch in frame order; they sum to 512. `mask_pos`: each row holds 256 distinct frames of one micro-batch. distractors[b, k] are frames of the utterance of mask_pos[b, k], never that frame itself.
All inputs are finite; a program needn't handle non-finite values.
Results may differ from the reference program's by a relative error of at most 0.022.
Values may be sent and summed in bfloat16 or wider, within the bound.
No kernel may reach another device: no remote copies, remote signals or barrier semaphores. Data moves between devices by JAX's collectives and lax.ppermute only.
A program may use at most 320 MiB of HBM per device.

```python
import math
import jax
import jax.numpy as jnp
from jax import lax

D = 768
H = 12
HD = 64
FF = 3072
C = 512
PD = 256
V = 320
NEG = 100
UTTS = 3
FMB = 512
UMAX = 384
LMIN = 32
NMASK = 256
NMB = 32


def layout(key):
    key = jax.random.fold_in(key, 17)
    key_first, key_second, key_order, key_offsets = jax.random.split(key, 4)
    first_len = jax.random.randint(key_first, (NMB,), LMIN, UMAX + 1)
    first_len = first_len.at[0].set(UMAX)
    lower_bound = jnp.maximum(LMIN, FMB - first_len - UMAX)
    upper_bound = jnp.minimum(UMAX, FMB - first_len - LMIN)
    second = jax.random.randint(key_second, (NMB,), lower_bound, upper_bound + 1)
    third_len = FMB - first_len - second
    utterance_lens = jnp.stack([first_len, second, third_len], axis=1).astype(jnp.int32)
    row_keys = jax.random.split(key_order, NMB)
    orders = jax.vmap(lambda row_key: jax.random.permutation(row_key, FMB))(row_keys)
    positions = orders[:, :NMASK].astype(jnp.int32)
    stop_positions = jnp.cumsum(utterance_lens, axis=1)
    starts = stop_positions - utterance_lens
    owner_index = jnp.sum((positions[:, :, None] >= stop_positions[:, None, :]).astype(jnp.int32), axis=2)
    start_position = jnp.take_along_axis(starts, owner_index, axis=1)
    extent = jnp.take_along_axis(utterance_lens, owner_index, axis=1)
    offsets = jax.random.randint(key_offsets, (NMB, NMASK, NEG), 0, extent[:, :, None] - 1)
    chosen = start_position[:, :, None] + offsets + (offsets >= (positions - start_position)[:, :, None]).astype(jnp.int32)
    return (utterance_lens, positions, chosen.astype(jnp.int32))


def draw_lengths(key, part):
    shared = layout(key)
    return shared[0]


def draw_mask_pos(key, part):
    shared = layout(key)
    return shared[1]


def draw_distractors(key, part):
    shared = layout(key)
    return shared[2]


def plant(array, key, smallest, top_value):
    longest = array.shape.index(max(array.shape))
    spots = []
    for shift in (0, 1):
        where = [jax.random.randint(jax.random.fold_in(key, axis), (), 0, length) for axis, length in enumerate(array.shape)]
        where[longest] = (where[longest] + shift) % array.shape[longest]
        spots.append(tuple(where))
    return array.at[spots[0]].set(smallest).at[spots[1]].set(top_value)


def strengthened(result, key, source, target, parts, factor):
    def block_of(axis_at):
        return (jnp.arange(result.shape[axis_at]) // (result.shape[axis_at] // parts)).reshape((-1,) + (1,) * (result.ndim - 1 - axis_at))

    first = jax.random.permutation(key, parts)[block_of(target)]
    second = (block_of(target) + parts // 2) % parts
    return jnp.where((block_of(source) == first) | (block_of(source) == second), factor * result, result)


def block_scale(own_key, shape, cuts, least, top_value):
    loudness, own = 1.0, jax.random.fold_in(own_key, 6)
    for position, shards_of in cuts:
        draws = jnp.exp(jax.random.uniform(jax.random.fold_in(own, position), (shards_of,), jnp.float32, least / len(cuts), top_value / len(cuts)))
        loudness = loudness * jnp.repeat(draws, shape[position] // shards_of).reshape([-1 if axis == position else 1 for axis in range(len(shape))])
    return loudness


def noise(key, shape, scale, limit, shards=(), held_as=jnp.bfloat16):
    result = scale * jax.random.normal(key, shape, jnp.float32)
    if shards:
        result = result * block_scale(key, shape, shards, -0.22, 0.18)
    return jnp.clip(result, -limit, limit).astype(held_as)


def heavy_noise(key, shape, deviation, reach, cuts, heavy, held_as=jnp.bfloat16):
    result = deviation * jax.random.normal(key, shape, jnp.float32)
    if cuts:
        result = result * block_scale(key, shape, cuts, -0.22, 0.18)
    return jnp.clip(strengthened(result, jax.random.fold_in(key, 3), *heavy), -reach, reach).astype(held_as)


def setup_inputs(seed: int = 0) -> dict:
    key_of = jax.random.split(jax.random.key(seed), 27)
    features = heavy_noise(key_of[0], (NMB, 2 * FMB, C), 1.0, 6.0, ((0, 16), (2, 2)), (0, 2, 16, 2.0))
    conv_weight = noise(key_of[1], (2 * C, C), (2 * C) ** -0.5, 0.1875, ((0, 32),))
    ln0_gain = jnp.clip(1.0 + 0.15 * jax.random.normal(key_of[2], (C,), jnp.float32), 0.25, 1.75).astype(jnp.bfloat16)
    ln0_bias = noise(key_of[3], (C,), 0.3, 1.75, ((0, 32),))
    proj0_weight = noise(key_of[4], (C, D), C ** -0.5, 0.25, ((0, 32),))
    proj0_bias = noise(key_of[5], (D,), 0.3, 1.75, ((0, 32),))
    mask_emb = noise(key_of[6], (D,), 1.0, 6.0, ((0, 32),))
    qkv_weight = noise(key_of[7], (D, 3 * D), D ** -0.5, 0.21875, ((0, 32),))
    qv_bias = noise(key_of[8], (2 * D,), 0.3, 1.75, ((0, 32),))
    out_weight = noise(key_of[9], (D, D), (D // 64) ** -0.5, 1.75, ((0, 32),))
    out_bias = noise(key_of[10], (D,), 0.3, 1.75, ((0, 32),))
    ln1_gain = jnp.clip(1.0 + 0.15 * jax.random.normal(key_of[11], (D,), jnp.float32), 0.25, 1.75).astype(jnp.bfloat16)
    ln1_bias = noise(key_of[12], (D,), 0.3, 1.75, ((0, 32),))
    up_weight = noise(key_of[13], (D, FF), D ** -0.5, 0.21875, ((0, 32),))
    up_bias = noise(key_of[14], (FF,), 0.3, 1.75, ((0, 32),))
    down_weight = noise(key_of[15], (FF, D), FF ** -0.5, 0.109375, ((0, 32),))
    down_bias = noise(key_of[16], (D,), 0.3, 1.75, ((0, 32),))
    ln2_gain = jnp.clip(1.0 + 0.15 * jax.random.normal(key_of[17], (D,), jnp.float32), 0.25, 1.75).astype(jnp.bfloat16)
    ln2_bias = noise(key_of[18], (D,), 0.3, 1.75, ((0, 32),))
    final_weight = noise(key_of[19], (D, PD), D ** -0.5, 0.21875, ((0, 32),))
    final_bias = noise(key_of[20], (PD,), 0.3, 1.75, ((0, 32),))
    codebook = noise(key_of[21], (2, V, PD // 2), 1.0, 6.0)
    lengths = draw_lengths(jax.random.fold_in(key_of[26], 71), 0)
    mask_pos = draw_mask_pos(jax.random.fold_in(key_of[26], 71), 0)
    distractors = draw_distractors(jax.random.fold_in(key_of[26], 71), 0)
    target_ids = plant(jax.random.randint(key_of[25], (NMB, 2, FMB), 0, V), jax.random.fold_in(key_of[25], 1), 0, V - 1).astype(jnp.int32)
    return dict(features=features, conv_weight=conv_weight, ln0_gain=ln0_gain, ln0_bias=ln0_bias, proj0_weight=proj0_weight, proj0_bias=proj0_bias, mask_emb=mask_emb, qkv_weight=qkv_weight, qv_bias=qv_bias, out_weight=out_weight, out_bias=out_bias, ln1_gain=ln1_gain, ln1_bias=ln1_bias, up_weight=up_weight, up_bias=up_bias, down_weight=down_weight, down_bias=down_bias, ln2_gain=ln2_gain, ln2_bias=ln2_bias, final_weight=final_weight, final_bias=final_bias, codebook=codebook, lengths=lengths, mask_pos=mask_pos, distractors=distractors, target_ids=target_ids)


@jax.custom_vjp
def low(v):
    return lax.optimization_barrier(v.astype(jnp.bfloat16)).astype(jnp.float32)

@jax.custom_vjp
def low_back(v):
    return v

def low_keep(v):
    return (low(v), None)

def low_pass(kept, grad):
    return (grad,)

def back_keep(v):
    return (v, None)

def back_low(kept, grad):
    return (low(grad),)
low.defvjp(low_keep, low_pass)
low_back.defvjp(back_keep, back_low)
norm_eps = 1e-05
unit_eps = 1e-06
sharpness_divisor = 0.1
masked_score = -1000000000.0
precise = lax.Precision.HIGHEST

def matrix_product(left_side, right_side):
    return jnp.dot(left_side, right_side, precision=precise, preferred_element_type=jnp.float32)

def layer_normalize(values, norm_gain, norm_shift):
    center = values - lax.optimization_barrier(jnp.mean(values, axis=-1, keepdims=True))
    spread = lax.optimization_barrier(jnp.mean(center * center, axis=-1, keepdims=True))
    return center * lax.rsqrt(spread + norm_eps) * norm_gain + norm_shift

def exact_gelu(values):
    return jax.nn.gelu(values, approximate=False)

def contrastive(projected, code_table, target_rows, positions, chosen):
    entries = jnp.arange(code_table.shape[1], dtype=jnp.int32)
    first_pick = (target_rows[0][:, None] == entries[None, :]).astype(jnp.float32)
    second_pick = (target_rows[1][:, None] == entries[None, :]).astype(jnp.float32)
    targets = jnp.concatenate([matrix_product(first_pick, code_table[0]), matrix_product(second_pick, code_table[1])], axis=1)
    targets = targets * lax.rsqrt(lax.optimization_barrier(jnp.sum(targets * targets, axis=1, keepdims=True)) + unit_eps)
    picked = jnp.take(projected, positions, axis=0)
    picked = picked * lax.rsqrt(lax.optimization_barrier(jnp.sum(picked * picked, axis=1, keepdims=True)) + unit_eps)
    angular_agreement = matrix_product(picked, targets.T)
    contender_entries = jnp.concatenate([positions[:, None], chosen], axis=1).astype(jnp.int32)
    agreement_scores_raw = jnp.take_along_axis(angular_agreement, contender_entries, axis=1) / sharpness_divisor
    return jnp.mean(jax.nn.logsumexp(agreement_scores_raw, axis=1) - agreement_scores_raw[:, 0])

def encoder(feature_rows, front_params):
    conv_weight, gain_zero, shift_zero, proj_weight, proj_shift = front_params
    frame_pairs = feature_rows.reshape(FMB, 2 * C)
    conv_out = low_back(matrix_product(frame_pairs, conv_weight))
    normed = low(layer_normalize(exact_gelu(conv_out), gain_zero, shift_zero))
    return low_back(low(matrix_product(normed, proj_weight) + proj_shift))

def block(block_in, mask_rows, segment, encoder_coefficients):
    mask_vector, qkv_weight, qv_bias, out_weight, out_shift, gain_one, shift_one, up_weight, up_shift, down_weight, down_shift, gain_two, shift_two, final_weight, final_shift = encoder_coefficients
    inputs = jnp.where(mask_rows[:, None], low(mask_vector)[None, :], block_in)
    bias_three = jnp.concatenate([qv_bias[:D], jnp.zeros((D,), jnp.float32), qv_bias[D:]])
    qkv_rows = low(low_back(matrix_product(inputs, qkv_weight) + bias_three))
    queries = qkv_rows[:, :D].reshape(FMB, H, HD)
    key_rows = qkv_rows[:, D:2 * D].reshape(FMB, H, HD)
    value_rows = qkv_rows[:, 2 * D:].reshape(FMB, H, HD)
    raw_scores = low_back(jnp.einsum('qhd,khd->hqk', queries, key_rows, precision=precise) * (1.0 / math.sqrt(HD)))
    same_utt = (segment[:, None] == segment[None, :])[None]
    attention = jax.nn.softmax(jnp.where(same_utt, raw_scores, masked_score), axis=-1)
    mixed_heads = jnp.einsum('hqk,khd->qhd', low(attention), value_rows, precision=precise).reshape(FMB, D)
    attn_out = low_back(matrix_product(low(low_back(mixed_heads)), out_weight) + out_shift)
    first_norm = low(layer_normalize(inputs + attn_out, gain_one, shift_one))
    hidden_pre = low_back(matrix_product(first_norm, up_weight) + up_shift)
    hidden_act = low(exact_gelu(hidden_pre))
    ffn_out = low_back(matrix_product(hidden_act, down_weight) + down_shift)
    second_norm = low(layer_normalize(first_norm + ffn_out, gain_two, shift_two))
    return low_back(matrix_product(second_norm, final_weight) + final_shift)

def reference(features, conv_weight, ln0_gain, ln0_bias, proj0_weight, proj0_bias, mask_emb, qkv_weight, qv_bias, out_weight, out_bias, ln1_gain, ln1_bias, up_weight, up_bias, down_weight, down_bias, ln2_gain, ln2_bias, final_weight, final_bias, codebook, lengths, mask_pos, distractors, target_ids):
    front_params = tuple((member.astype(jnp.float32) for member in (conv_weight, ln0_gain, ln0_bias, proj0_weight, proj0_bias)))
    encoder_coefficients = tuple((member.astype(jnp.float32) for member in (mask_emb, qkv_weight, qv_bias, out_weight, out_bias, ln1_gain, ln1_bias, up_weight, up_bias, down_weight, down_bias, ln2_gain, ln2_bias, final_weight, final_bias)))
    code_table = codebook.astype(jnp.float32)
    feature_data = features.astype(jnp.float32)

    def objective(front_params, encoder_coefficients, feature_data):

        def micro_step(running, slices):
            feature_rows, utterance_lens, positions, chosen, target_rows = slices
            frame_ids = jnp.arange(FMB, dtype=jnp.int32)
            stop_positions = jnp.cumsum(utterance_lens)
            segment = lax.optimization_barrier(jnp.sum((frame_ids[:, None] >= stop_positions[None, :UTTS - 1]).astype(jnp.int32), axis=1))
            mask_rows = jnp.any(frame_ids[:, None] == positions[None, :], axis=1)
            projected = block(encoder(feature_rows, front_params), mask_rows, segment, encoder_coefficients)
            micro_loss = contrastive(projected, code_table, target_rows, positions, chosen)
            return (running + micro_loss, micro_loss)
        loss_total, per_micro = lax.scan(jax.checkpoint(micro_step), jnp.zeros((), jnp.float32), (feature_data, lengths, mask_pos, distractors, target_ids))
        return (loss_total, per_micro)
    loss_total, pullback, per_micro = jax.vjp(objective, front_params, encoder_coefficients, feature_data, has_aux=True)
    grad_front, grad_block, grad_features = pullback(jnp.ones((), loss_total.dtype))
    return (per_micro, grad_features, grad_front[0], grad_front[1], grad_front[2], grad_front[3], grad_front[4], grad_block[0], grad_block[1], grad_block[2], grad_block[3], grad_block[4], grad_block[5], grad_block[6], grad_block[7], grad_block[8], grad_block[9], grad_block[10], grad_block[11], grad_block[12], grad_block[13], grad_block[14])
```

```python
import math

import jax
import jax.numpy as jnp
from jax import lax
from jax.experimental import pallas as pl
from jax.experimental.pallas import tpu as pltpu
from jax.sharding import PartitionSpec as P

D = 768
H = 12
HD = 64
FF = 3072
C = 512
PD = 256
UTTS = 3
FMB = 512
NEG = 100
NMASK = 256
SPARE = 256

BOTH = ("section", "dp")
norm_eps = 1e-05
unit_eps = 1e-06
sharpness = 10.0
masked_score = -1000000000.0
precise = lax.Precision.HIGHEST
low = jnp.bfloat16
full = jnp.float32

VECTORS = (
    ("ln0_gain", C),
    ("ln0_bias", C),
    ("proj0_bias", D),
    ("mask_emb", D),
    ("qv_bias", 2 * D),
    ("out_bias", D),
    ("ln1_gain", D),
    ("ln1_bias", D),
    ("up_bias", FF),
    ("down_bias", D),
    ("ln2_gain", D),
    ("ln2_bias", D),
    ("final_bias", PD),
)
VECTOR_TOTAL = sum(size for _, size in VECTORS)


def plain_dot(left_side, right_side):
    return jnp.dot(left_side, right_side, preferred_element_type=full)


def left_dot(left_side, right_side):
    return lax.dot_general(
        left_side, right_side, (((0,), (0,)), ((), ())), preferred_element_type=full
    )


def right_dot(left_side, right_side):
    return lax.dot_general(
        left_side, right_side, (((1,), (1,)), ((), ())), preferred_element_type=full
    )


def layer_normalize(values, norm_gain, norm_shift):
    center = values - jnp.mean(values, axis=-1, keepdims=True)
    spread = jnp.mean(center * center, axis=-1, keepdims=True)
    return center * lax.rsqrt(spread + norm_eps) * norm_gain + norm_shift


def exact_gelu(values):
    return jax.nn.gelu(values, approximate=False)


def front_norm(conv_out, norm_gain, norm_shift):
    return layer_normalize(exact_gelu(conv_out), norm_gain, norm_shift)


class Links:
    def __init__(self):
        self.per_section = lax.axis_size("dp")
        self.depth = self.per_section // 4
        place = lax.axis_index("dp")
        self.core = place % 2
        self.x = (place // 2) % 2
        self.z = place // 4
        self.y = lax.axis_index("section")

    def move(self, value, where):
        pairs = []
        for y in range(2):
            for z in range(self.depth):
                for x in range(2):
                    for core in range(2):
                        ty, tz, tx, tcore = where(y, z, x, core)
                        pairs.append(
                            (
                                y * self.per_section + z * 4 + x * 2 + core,
                                ty * self.per_section + tz * 4 + tx * 2 + tcore,
                            )
                        )
        return lax.ppermute(value, BOTH, pairs)

    def over_x(self, value):
        return self.move(value, lambda y, z, x, core: (y, z, 1 - x, core))

    def over_y(self, value):
        return self.move(value, lambda y, z, x, core: (1 - y, z, x, core))

    def over_core(self, value):
        return self.move(value, lambda y, z, x, core: (y, z, x, 1 - core))

    def over_z(self, value, steps):
        return self.move(value, lambda y, z, x, core: (y, (z + steps) % self.depth, x, core))


def pick(value, index, axis):
    return lax.squeeze(lax.dynamic_slice_in_dim(value, index, 1, axis), (axis,))


def in_order(index, own, got, axis):
    return jnp.where(
        index == 0, jnp.stack([own, got], axis=axis), jnp.stack([got, own], axis=axis)
    )


def gather_shares(links, share):
    rows, cols = share.shape
    depth = links.depth
    turns = [share] + [links.over_z(share, k) for k in range(1, depth)]
    doubled = jnp.stack([turns[(depth - 1 - i) % depth] for i in range(2 * depth - 1)], 0)
    line = lax.dynamic_slice_in_dim(doubled, depth - 1 - links.z, depth, 0)
    half = cols // 2
    first, second = line[..., :half], line[..., half:]
    first_got, second_got = links.over_x(first), links.over_y(second)
    first = in_order(links.x, first, first_got, 1)
    second = in_order(links.y, second, second_got, 0)
    first_got, second_got = links.over_y(first), links.over_x(second)
    first = in_order(links.y, first, first_got, 0)
    second = in_order(links.x, second, second_got, 2)
    lane = jnp.concatenate([first, second], -1)
    whole = in_order(links.core, lane, links.over_core(lane), 3)
    return whole.reshape(2 * links.per_section, rows, cols)


def sum_shares(links, terms):
    devices, rows, cols = terms.shape
    depth = links.depth
    terms = terms.reshape(2, depth, 2, 2, rows, cols)
    got = links.over_core(pick(terms, 1 - links.core, 3).astype(low))
    lane = pick(terms, links.core, 3) + got.astype(full)
    half = cols // 2
    first, second = lane[..., :half], lane[..., half:]
    first_got = links.over_x(pick(first, 1 - links.x, 2).astype(low))
    second_got = links.over_y(pick(second, 1 - links.y, 0).astype(low))
    first = pick(first, links.x, 2) + first_got.astype(full)
    second = pick(second, links.y, 0) + second_got.astype(full)
    first_got = links.over_y(pick(first, 1 - links.y, 0).astype(low))
    second_got = links.over_x(pick(second, 1 - links.x, 1).astype(low))
    first = pick(first, links.y, 0) + first_got.astype(full)
    second = pick(second, links.x, 1) + second_got.astype(full)
    line = jnp.concatenate([first, second], -1)
    total = pick(line, links.z, 0)
    for k in range(1, depth):
        sent = pick(line, (links.z + k) % depth, 0).astype(low)
        total = total + links.over_z(sent, k).astype(full)
    return total


def vector_maps(devices):
    owner, place = [], []
    start = 0
    for _, size in VECTORS:
        part = size // devices
        for device in range(devices):
            owner += [device] * part
            place += list(range(start, start + part))
        start += part
    return jnp.array(owner, jnp.int32), jnp.array(place, jnp.int32)


def spread_vectors(parts, devices):
    owner, place = vector_maps(devices)
    lanes = (jnp.arange(parts.shape[1], dtype=jnp.int32)[:, None] == place[None, :]).astype(low)
    rows = jnp.arange(devices, dtype=jnp.int32)[:, None] == owner[None, :]
    return jnp.sum(jnp.where(rows, plain_dot(parts, lanes), 0.0), axis=0, keepdims=True)


def split_vectors(vectors, devices, width):
    owner, place = vector_maps(devices)
    lanes = (jnp.arange(width, dtype=jnp.int32)[:, None] == place[None, :]).astype(low)
    rows = jnp.arange(devices, dtype=jnp.int32)[:, None] == owner[None, :]
    return right_dot(jnp.where(rows, vectors.astype(low), 0).astype(low), lanes)


def count_kernel(chosen_ref, count_ref):
    rows = 64
    for block in range(FMB // rows):
        frames = block * rows + lax.broadcasted_iota(jnp.int32, (rows, NMASK), 0)

        def add_one(j, seen):
            return seen + jnp.where(frames == chosen_ref[pl.ds(j, 1), :], 1.0, 0.0)

        seen = lax.fori_loop(0, NEG, add_one, jnp.zeros((rows, NMASK), full), unroll=10)
        count_ref[pl.ds(block * rows, rows), :] = seen.astype(low)


def count_distractors(chosen):
    return pl.pallas_call(
        count_kernel,
        out_shape=jax.ShapeDtypeStruct((FMB, NMASK), low),
        in_specs=[pl.BlockSpec(memory_space=pltpu.VMEM)],
        out_specs=pl.BlockSpec(memory_space=pltpu.VMEM),
        cost_estimate=pl.CostEstimate(flops=2 * FMB * NMASK * NEG, bytes_accessed=400000, transcendentals=0),
    )(chosen.T)


def body(
    features,
    conv_weight,
    ln0_gain,
    ln0_bias,
    proj0_weight,
    proj0_bias,
    mask_emb,
    qkv_weight,
    qv_bias,
    out_weight,
    out_bias,
    ln1_gain,
    ln1_bias,
    up_weight,
    up_bias,
    down_weight,
    down_bias,
    ln2_gain,
    ln2_bias,
    final_weight,
    final_bias,
    codebook,
    lengths,
    mask_pos,
    distractors,
    target_ids,
):
    links = Links()
    section = links.y
    devices = 2 * links.per_section
    rows = C // devices

    own_rows = pick(features, section, 0)
    got_rows = links.over_y(pick(features, 1 - section, 0))
    lens = pick(lengths, section, 0)
    positions = pick(mask_pos, section, 0)
    chosen = pick(distractors, section, 0)
    target_rows = pick(target_ids, section, 0)

    vector_part = jnp.concatenate(
        [
            ln0_gain,
            ln0_bias,
            proj0_bias,
            mask_emb,
            qv_bias,
            out_bias,
            ln1_gain,
            ln1_bias,
            up_bias,
            down_bias,
            ln2_gain,
            ln2_bias,
            final_bias,
        ]
    )
    vector_part = jnp.pad(vector_part, (0, (rows // 2) * SPARE - vector_part.shape[0]))
    misc = jnp.concatenate(
        [
            proj0_weight,
            conv_weight[:rows],
            conv_weight[rows:],
            final_weight[:rows],
            jnp.concatenate([final_weight[rows:], vector_part.reshape(rows // 2, SPARE)], 0),
        ],
        axis=1,
    )
    misc_all = gather_shares(links, misc)
    heads_all = gather_shares(links, jnp.concatenate([qkv_weight, out_weight], axis=1))
    up_all = gather_shares(links, up_weight)
    down_all = gather_shares(links, down_weight)

    proj_full = misc_all[..., :D].reshape(C, D)
    conv_full = jnp.concatenate(
        [misc_all[..., D : D + C], misc_all[..., D + C : D + 2 * C]], axis=1
    ).reshape(2 * C, C)
    last = misc_all[..., D + 2 * C + PD :]
    final_full = jnp.concatenate(
        [misc_all[..., D + 2 * C : D + 2 * C + PD], last[:, : rows // 2]], axis=1
    ).reshape(D, PD)
    vectors = spread_vectors(last[:, rows // 2 :].reshape(devices, -1), devices)
    vec = {}
    start = 0
    for name, size in VECTORS:
        vec[name] = vectors[:, start : start + size]
        start += size
    heads_all = heads_all.reshape(D, 4 * D)
    qkv_full, out_full = heads_all[:, : 3 * D], heads_all[:, 3 * D :]
    up_full = up_all.reshape(D, FF)
    down_full = down_all.reshape(FF, D)

    frame_ids = jnp.arange(FMB, dtype=jnp.int32)
    at_frame = positions[:, None] == frame_ids[None, :]
    is_masked = jnp.any(at_frame, axis=0)
    counts = plain_dot(count_distractors(chosen), at_frame.astype(low))
    own_frame = (frame_ids[:, None] == frame_ids[None, :]) & is_masked[None, :]
    counts = counts + own_frame.astype(full)
    entries = jnp.arange(codebook.shape[1], dtype=jnp.int32)
    targets = jnp.concatenate(
        [
            plain_dot((target_rows[0][:, None] == entries[None, :]).astype(low), codebook[0]),
            plain_dot((target_rows[1][:, None] == entries[None, :]).astype(low), codebook[1]),
        ],
        axis=1,
    )
    targets = targets * lax.rsqrt(jnp.sum(targets * targets, axis=1, keepdims=True) + unit_eps)
    stops = jnp.cumsum(lens)
    segment = jnp.sum(
        (frame_ids[:, None] >= stops[None, : UTTS - 1]).astype(jnp.int32), axis=1
    )
    same_utt = (segment[:, None] == segment[None, :])[None]
    mask_rows = is_masked[:, None]

    own_pairs = own_rows.reshape(FMB, C)
    got_pairs = got_rows.reshape(FMB, C)
    half = C // 2
    taps = conv_full.reshape(2, 2, half, C)
    own_taps = pick(taps, section, 1).reshape(C, C)
    got_taps = pick(taps, 1 - section, 1).reshape(C, C)
    conv_out = plain_dot(own_pairs, own_taps) + plain_dot(got_pairs, got_taps)
    normed, norm_back = jax.vjp(front_norm, conv_out, vec["ln0_gain"], vec["ln0_bias"])
    normed = normed.astype(low)
    encoded = (plain_dot(normed, proj_full) + vec["proj0_bias"]).astype(low)
    inputs = jnp.where(mask_rows, vec["mask_emb"].astype(low), encoded)

    scale = 1.0 / math.sqrt(HD)
    bias_three = jnp.concatenate(
        [vec["qv_bias"][:, :D], jnp.zeros((1, D), full), vec["qv_bias"][:, D:]], axis=1
    )
    qkv_rows = (plain_dot(inputs, qkv_full) + bias_three).astype(low)
    queries = qkv_rows[:, :D].reshape(FMB, H, HD)
    key_rows = qkv_rows[:, D : 2 * D].reshape(FMB, H, HD)
    value_rows = qkv_rows[:, 2 * D :].reshape(FMB, H, HD)
    scores = jnp.einsum("qhd,khd->hqk", queries, key_rows, preferred_element_type=full) * scale
    scores = jnp.where(same_utt, scores, masked_score)
    top_score = jnp.max(scores, axis=-1, keepdims=True)
    exp_scores = jnp.exp(scores - top_score)
    row_total = jnp.sum(exp_scores, axis=-1, keepdims=True)
    attention = exp_scores / row_total
    attention_low = attention.astype(low)
    mixed = (
        jnp.einsum("hqk,khd->qhd", attention_low, value_rows, preferred_element_type=full)
        .reshape(FMB, D)
        .astype(low)
    )
    first, first_back = jax.vjp(
        layer_normalize,
        inputs.astype(full) + plain_dot(mixed, out_full) + vec["out_bias"],
        vec["ln1_gain"],
        vec["ln1_bias"],
    )
    first_low = first.astype(low)
    hidden, gelu_back = jax.vjp(exact_gelu, plain_dot(first_low, up_full) + vec["up_bias"])
    hidden_low = hidden.astype(low)
    second, second_back = jax.vjp(
        layer_normalize,
        first_low.astype(full) + plain_dot(hidden_low, down_full) + vec["down_bias"],
        vec["ln2_gain"],
        vec["ln2_bias"],
    )
    second_low = second.astype(low)
    projected = plain_dot(second_low, final_full) + vec["final_bias"]

    inverse = lax.rsqrt(jnp.sum(projected * projected, axis=1, keepdims=True) + unit_eps)
    unit = projected * inverse
    agreement = sharpness * lax.dot_general(
        targets, unit, (((1,), (1,)), ((), ())), precision=precise, preferred_element_type=full
    )
    drawn = counts > 0
    highest = jnp.max(jnp.where(drawn, agreement, masked_score), axis=0, keepdims=True)
    weights = counts * jnp.exp(jnp.where(drawn, agreement - highest, 0.0))
    weight_total = jnp.sum(weights, axis=0, keepdims=True)
    log_total = highest + jnp.log(jnp.where(is_masked[None, :], weight_total, 1.0))
    own_score = jnp.sum(jnp.where(own_frame, agreement, 0.0), axis=0, keepdims=True)
    loss = jnp.sum(jnp.where(is_masked[None, :], log_total - own_score, 0.0)) / NMASK
    d_agreement = jnp.where(
        is_masked[None, :],
        weights / jnp.where(is_masked[None, :], weight_total, 1.0) - own_frame.astype(full),
        0.0,
    ) * (sharpness / NMASK)
    d_unit = lax.dot_general(
        d_agreement, targets, (((0,), (0,)), ((), ())), precision=precise, preferred_element_type=full
    )
    d_projected = inverse * (d_unit - unit * jnp.sum(d_unit * unit, axis=1, keepdims=True))
    loss_got = links.over_y(loss.reshape(1, 1))
    loss_each = in_order(section, loss.reshape(1, 1), loss_got, 0).reshape(2)

    grad = {}
    d_proj_low = d_projected.astype(low)
    g_final = left_dot(second_low, d_proj_low)
    grad["final_bias"] = jnp.sum(d_proj_low.astype(full), axis=0, keepdims=True)
    d_second, grad["ln2_gain"], grad["ln2_bias"] = second_back(right_dot(d_proj_low, final_full))
    d_ffn_low = d_second.astype(low)
    g_down = left_dot(hidden_low, d_ffn_low)
    down_sum = sum_shares(links, g_down.reshape(devices, FF // devices, D))
    grad["down_bias"] = jnp.sum(d_ffn_low.astype(full), axis=0, keepdims=True)
    (d_hidden,) = gelu_back(right_dot(d_ffn_low, down_full))
    d_pre_low = d_hidden.astype(low)
    g_up = left_dot(first_low, d_pre_low)
    up_sum = sum_shares(links, g_up.reshape(devices, D // devices, FF))
    grad["up_bias"] = jnp.sum(d_pre_low.astype(full), axis=0, keepdims=True)
    d_first, grad["ln1_gain"], grad["ln1_bias"] = first_back(
        right_dot(d_pre_low, up_full) + d_second
    )
    d_attn_low = d_first.astype(low)
    g_out = left_dot(mixed, d_attn_low)
    grad["out_bias"] = jnp.sum(d_attn_low.astype(full), axis=0, keepdims=True)
    d_mixed = right_dot(d_attn_low, out_full).astype(low).reshape(FMB, H, HD)
    d_values = jnp.einsum("hqk,qhd->khd", attention_low, d_mixed, preferred_element_type=full)
    d_attention = jnp.einsum("qhd,khd->hqk", d_mixed, value_rows, preferred_element_type=full)
    d_scores = (
        attention * (d_attention - jnp.sum(attention * d_attention, axis=-1, keepdims=True))
    ).astype(low)
    d_queries = jnp.einsum("hqk,khd->qhd", d_scores, key_rows, preferred_element_type=full) * scale
    d_keys = jnp.einsum("hqk,qhd->khd", d_scores, queries, preferred_element_type=full) * scale
    d_qkv = jnp.concatenate(
        [d_queries.reshape(FMB, D), d_keys.reshape(FMB, D), d_values.reshape(FMB, D)], axis=1
    ).astype(low)
    g_qkv = left_dot(inputs, d_qkv)
    heads_sum = sum_shares(
        links,
        jnp.concatenate([g_qkv, g_out], axis=1).reshape(devices, D // devices, 4 * D),
    )
    qkv_sums = jnp.sum(d_qkv.astype(full), axis=0, keepdims=True)
    grad["qv_bias"] = jnp.concatenate([qkv_sums[:, :D], qkv_sums[:, 2 * D :]], axis=1)
    d_inputs = right_dot(d_qkv, qkv_full) + d_first
    grad["mask_emb"] = jnp.sum(jnp.where(mask_rows, d_inputs, 0.0), axis=0, keepdims=True)
    d_encoded = jnp.where(mask_rows, 0.0, d_inputs).astype(low)
    g_proj = left_dot(normed, d_encoded)
    grad["proj0_bias"] = jnp.sum(d_encoded.astype(full), axis=0, keepdims=True)
    d_conv, grad["ln0_gain"], grad["ln0_bias"] = norm_back(right_dot(d_encoded, proj_full))
    d_conv_low = d_conv.astype(low)
    got_d = links.over_y(right_dot(d_conv_low, got_taps).astype(low).reshape(2 * FMB, half))
    own_d = right_dot(d_conv_low, own_taps).reshape(2 * FMB, half)
    features_grad = in_order(section, own_d, got_d.astype(full), 0)
    own_g = left_dot(own_pairs, d_conv_low).reshape(2, half, C)
    got_g = left_dot(got_pairs, d_conv_low).reshape(2, half, C)
    g_conv = in_order(section, own_g, got_g, 1).reshape(devices, 2 * rows, C)
    g_final = g_final.reshape(devices, D // devices, PD)
    g_vectors = split_vectors(
        jnp.concatenate([grad[name] for name, _ in VECTORS], axis=1),
        devices,
        (rows // 2) * SPARE,
    ).reshape(devices, rows // 2, SPARE)
    misc_sum = sum_shares(
        links,
        jnp.concatenate(
            [
                g_proj.reshape(devices, rows, D),
                g_conv[:, :rows],
                g_conv[:, rows:],
                g_final[:, :rows],
                jnp.concatenate([g_final[:, rows:], g_vectors], axis=1),
            ],
            axis=2,
        ),
    )
    proj_sum = misc_sum[:, :D]
    conv_sum = jnp.concatenate([misc_sum[:, D : D + C], misc_sum[:, D + C : D + 2 * C]], axis=0)
    last = misc_sum[:, D + 2 * C + PD :]
    final_sum = jnp.concatenate(
        [misc_sum[:, D + 2 * C : D + 2 * C + PD], last[: rows // 2]], axis=0
    )
    vector_sum = last[rows // 2 :].reshape(-1)
    share = {}
    start = 0
    for name, size in VECTORS:
        share[name] = vector_sum[start : start + size // devices]
        start += size // devices
    return (
        loss_each,
        features_grad,
        conv_sum,
        share["ln0_gain"],
        share["ln0_bias"],
        proj_sum,
        share["proj0_bias"],
        share["mask_emb"],
        heads_sum[:, : 3 * D],
        share["qv_bias"],
        heads_sum[:, 3 * D :],
        share["out_bias"],
        share["ln1_gain"],
        share["ln1_bias"],
        up_sum,
        share["up_bias"],
        down_sum,
        share["down_bias"],
        share["ln2_gain"],
        share["ln2_bias"],
        final_sum,
        share["final_bias"],
    )


def solution(mesh):
    rows = P(BOTH, None)
    part = P(BOTH)
    weights = (rows, part, part, rows, part, part, rows, part, rows, part, part, part)
    weights += (rows, part, rows, part, part, part, rows, part)
    return jax.shard_map(
        body,
        mesh=mesh,
        in_specs=(P("dp", None, "section"),)
        + weights
        + (P(), P("dp", None), P("dp", None), P("dp", None, None), P("dp", None, None)),
        out_specs=(P("dp"), P("dp", None, "section")) + weights,
        check_vma=False,
    )
```

```python
import functools
import math

import jax
import jax.numpy as jnp
from jax import lax
from jax.experimental import pallas as pl
from jax.experimental.pallas import tpu as pltpu
from jax.sharding import PartitionSpec as P

D = 768
H = 12
HD = 64
FF = 3072
C = 512
PD = 256
UTTS = 3
PAIR = 2 * HD
FMB = 512
NEG = 100
NMASK = 256
SPARE = 256
SLOTS = 16

SPLIT = ("z", "x", "core")
BOTH = ("section",) + SPLIT
norm_eps = 1e-05
unit_eps = 1e-06
sharpness = 10.0
masked_score = -1000000000.0
precise = lax.Precision.HIGHEST
low = jnp.bfloat16
full = jnp.float32

VECTORS = (
    ("up_bias", FF),
    ("ln0_gain", C),
    ("ln0_bias", C),
    ("proj0_bias", D),
    ("mask_emb", D),
    ("qv_bias", 2 * D),
    ("out_bias", D),
    ("ln1_gain", D),
    ("ln1_bias", D),
    ("down_bias", D),
    ("ln2_gain", D),
    ("ln2_bias", D),
    ("final_bias", PD),
)
VECTOR_TOTAL = sum(size for _, size in VECTORS)
start_of = {name: sum(size for _, size in VECTORS[:i]) for i, (name, _) in enumerate(VECTORS)}
QV_START = start_of["qv_bias"]


def plain_dot(left_side, right_side):
    return jnp.dot(left_side, right_side, preferred_element_type=full)


def left_dot(left_side, right_side):
    return lax.dot_general(
        left_side, right_side, (((0,), (0,)), ((), ())), preferred_element_type=full
    )


def right_dot(left_side, right_side):
    return lax.dot_general(
        left_side, right_side, (((1,), (1,)), ((), ())), preferred_element_type=full
    )


def gelu_and_slope(x):
    size = jnp.abs(x)
    bell = jnp.exp(-0.5 * x * x)
    t = 1.0 / (1.0 + 0.23164189 * size)
    poly = t * (0.127414796 + t * (-0.142248368 + t * (0.7107068705 + t * (-0.7265760135 + t * 0.5307027145))))
    tail = poly * bell
    below = jnp.where(x >= 0, 1.0 - tail, tail)
    return x * below, below + x * (0.3989422804 * bell)


class Links:
    def __init__(self):
        self.depth = lax.axis_size("z")
        self.per_section = 4 * self.depth
        self.core = lax.axis_index("core")
        self.x = lax.axis_index("x")
        self.z = lax.axis_index("z")
        self.y = lax.axis_index("section")
        self.sizes, self.upper = [], []
        size, place = self.depth, self.z
        while size > 1:
            self.sizes.append(size)
            self.upper.append((place >= size // 2).astype(jnp.int32))
            place = jnp.where(place >= size // 2, size - 1 - place, place)
            size //= 2

    def move(self, value, where):
        pairs = []
        for y in range(2):
            for z in range(self.depth):
                for x in range(2):
                    for core in range(2):
                        ty, tz, tx, tcore = where(y, z, x, core)
                        pairs.append(
                            (
                                y * self.per_section + z * 4 + x * 2 + core,
                                ty * self.per_section + tz * 4 + tx * 2 + tcore,
                            )
                        )
        return lax.ppermute(value, BOTH, pairs)

    def over_x(self, value):
        return self.move(value, lambda y, z, x, core: (y, z, 1 - x, core))

    def over_y(self, value):
        return self.move(value, lambda y, z, x, core: (1 - y, z, x, core))

    def over_core(self, value):
        return self.move(value, lambda y, z, x, core: (y, z, x, 1 - core))

    def over_both(self, value):
        return self.move(value, lambda y, z, x, core: (1 - y, z, 1 - x, core))

    def along_z(self, value, steps):
        return self.move(value, lambda y, z, x, core: (y, (z + steps) % self.depth, x, core))

    def over_z(self, value, size):
        def where(y, z, x, core):
            return (y, z - z % size + size - 1 - z % size, x, core)

        return self.move(value, where)


def pick(value, index, axis):
    axis = axis % value.ndim
    return lax.squeeze(lax.dynamic_slice_in_dim(value, index, 1, axis), (axis,))


def in_order(index, own, got, axis):
    axis = axis % own.ndim
    own, got = jnp.expand_dims(own, axis), jnp.expand_dims(got, axis)
    shape = own.shape[:axis] + (2,) + own.shape[axis + 1 :]
    return jnp.where(lax.broadcasted_iota(jnp.int32, shape, axis) == index, own, got)


def in_line(uppers, own, got):
    shape = (own.shape[0], 2) + own.shape[1:]
    turn = (
        lax.broadcasted_iota(jnp.int32, shape, 0) + lax.broadcasted_iota(jnp.int32, shape, 1)
    ) % 2
    line = jnp.where(turn == uppers[-1], jnp.expand_dims(own, 1), jnp.expand_dims(got, 1))
    line = line.reshape((-1,) + own.shape[1:])
    for _ in range(2, len(uppers)):
        line = jnp.concatenate([line[:, 0], jnp.flip(line[:, 1], 0)], axis=0)
    return line


class Gather:
    def __init__(self, links, line, cut, parts=1):
        self.links, self.line, self.cut, self.parts = links, line, cut, parts
        self.got = []

    def start_z(self):
        self.got = [self.links.over_z(self.line, self.links.sizes[0])]

    def start_z_rest(self):
        links = self.links
        for step in range(1, len(links.sizes)):
            self.line = in_order(links.upper[step - 1], self.line, self.got[0], 0)
            self.got = [links.over_z(self.line, links.sizes[step])]

    def start_first(self):
        links = self.links
        line = in_line(links.upper, self.line, self.got[0])
        self.first, self.second = line[..., : self.cut], line[..., self.cut :]
        if self.parts > 1:
            shape = self.second.shape
            self.second = self.second.reshape(shape[:2] + (self.parts, -1)).swapaxes(1, 2)
            self.second = self.second.reshape(shape[0], -1, shape[2] // self.parts)
        self.got = [links.over_x(self.first), links.over_y(self.second)]

    def start_second(self):
        links = self.links
        self.first = in_order(links.x, self.first, self.got[0], -2)
        self.second = in_order(links.y, self.second, self.got[1], -3)
        self.got = [links.over_y(self.first), links.over_x(self.second)]

    def start_core(self):
        links = self.links
        self.lanes = [
            in_order(links.y, self.first, self.got[0], -4),
            in_order(links.x, self.second, self.got[1], -2),
        ]
        self.lanes = lax.optimization_barrier(self.lanes)
        self.got = [links.over_core(lane) for lane in self.lanes]

    def whole(self):
        core = self.links.core
        return [
            in_order(core, own, got, -2).reshape(-1, own.shape[-1])
            for own, got in zip(self.lanes, self.got)
        ]

    def apart(self):
        lanes = [x for pair in zip(self.lanes, self.got) for x in pair]
        return [x.reshape(-1, x.shape[-1]) for x in lanes]


class Line:
    def __init__(self, links, line):
        self.links, self.line = links, line

    def start_z(self):
        self.start_line(self.line)

    def start_line(self, line):
        links = self.links
        for size in links.sizes[:-1]:
            line = jnp.stack([line[: size // 2], jnp.flip(line[size // 2 :], 0)], axis=1)
        self.line = line
        self.got = [links.over_z(pick(line, 1 - links.upper[-1], 0), links.sizes[-1])]

    def start_z_rest(self):
        links = self.links
        for step in range(len(links.sizes) - 2, -1, -1):
            self.line = added(pick(self.line, links.upper[step + 1], 0), self.got[0])
            away = pick(self.line, 1 - links.upper[step], 0)
            self.got = [links.over_z(away, links.sizes[step])]

    def total(self):
        return pick(self.line, self.links.upper[0], 0).astype(full) + self.got[0].astype(full)


class Sum(Line):
    def __init__(self, links, keep, send, cut):
        self.links, self.cut = links, cut
        self.grid = (2, links.depth, 2, -1, keep.shape[-1])
        self.keep, self.send = keep.reshape(self.grid), send
        self.got = []

    def start_core(self):
        self.got = [self.links.over_core(self.send)]

    def start_first(self):
        links = self.links
        lane = added(self.keep, self.got[0].reshape(self.grid))
        self.first, self.second = lane[..., : self.cut], lane[..., self.cut :]
        self.got = [
            links.over_x(pick(self.first, 1 - links.x, -3)),
            links.over_y(pick(self.second, 1 - links.y, -5)),
        ]

    def start_plane(self):
        links = self.links
        lane = added(self.keep, self.got[0].reshape(self.grid))

        def part(y, x):
            return pick(pick(lane, x, -3), y, 0)

        self.line = part(links.y, links.x)
        self.got = [
            links.over_x(part(links.y, 1 - links.x)),
            links.over_y(part(1 - links.y, links.x)),
            links.over_both(part(1 - links.y, 1 - links.x)),
        ]

    def line_of(self):
        links = self.links
        if len(self.got) == 3:
            return total_of(self.line, self.got).astype(low)
        first = added(pick(self.first, links.y, -4), self.got[0])
        second = added(pick(self.second, links.x, -3), self.got[1])
        return jnp.concatenate([first, second], -1)

    def start_straight_z(self):
        links, line = self.links, self.line_of()
        self.line = pick(line, links.z, 0)
        self.got = [
            links.along_z(pick(line, (links.z + k) % links.depth, 0), k)
            for k in range(1, links.depth)
        ]

    def straight_total(self):
        return total_of(self.line, self.got)

    def start_second(self):
        links = self.links
        self.first = added(pick(self.first, links.x, -3), self.got[0])
        self.second = added(pick(self.second, links.y, -5), self.got[1])
        self.got = [
            links.over_y(pick(self.first, 1 - links.y, -4)),
            links.over_x(pick(self.second, 1 - links.x, -3)),
        ]

    def start_z(self):
        self.start_line(self.line_of())


def by_core(links, terms):
    lanes = terms.reshape(links.per_section, 2, -1, terms.shape[-1])
    return [
        pick(lanes, core, 1).reshape(-1, terms.shape[-1]) for core in (links.core, 1 - links.core)
    ]


def total_of(own, others):
    out = own.astype(full)
    for got in others:
        out = out + got.astype(full)
    return out


def added(own, got):
    return (own.astype(full) + got.astype(full)).astype(low)


def after(moves, *values):
    bound = lax.optimization_barrier((tuple(tuple(m.got) for m in moves), values))
    for move, got in zip(moves, bound[0]):
        move.got = list(got)
    return bound[1]


def owner_of(columns, part):
    factor = -(-(1 << 20) // part)
    assert all((n * factor) >> 20 == n // part for n in range(columns))
    lane = lax.broadcasted_iota(jnp.int32, (1, columns), 1)
    return lax.shift_right_logical(lane * factor, 20)


def spread_parts(rows, parts_ref, out_ref):
    start = 0
    devices = C // rows
    slot = (rows // 2) * SPARE // SLOTS
    each_row = SPARE // slot
    shape = (devices, C)
    across = lax.broadcasted_iota(jnp.int32, shape, 1)
    first = lax.broadcasted_iota(jnp.int32, shape, 0) * rows + rows // 2
    held = [
        plain_dot(jnp.where(across == first + k, 1.0, 0.0).astype(low), parts_ref[:, PD:]).astype(low)
        for k in range(rows // 2)
    ]
    for index, (_, size) in enumerate(VECTORS):
        part = size // devices
        owner = owner_of(size, part)
        place = lax.broadcasted_iota(jnp.int32, (1, size), 1) - owner * part
        lanes = jnp.where(lax.broadcasted_iota(jnp.int32, (slot, size), 0) == place, 1.0, 0.0)
        at = lax.broadcasted_iota(jnp.int32, (devices, size), 0) == owner
        begin = (index % each_row) * slot
        mine = held[index // each_row][:, begin : begin + slot]
        out_ref[:, start : start + size] = jnp.sum(
            jnp.where(at, plain_dot(mine, lanes.astype(low)), 0.0), axis=0, keepdims=True
        )
        start += size


def split_kernel(devices, *refs):
    out_ref = refs[-1]
    slot = out_ref.shape[2]
    for index, (_, size) in enumerate(VECTORS):
        part = size // devices
        owner = owner_of(size, part)
        place = lax.broadcasted_iota(jnp.int32, (1, size), 1) - owner * part
        lanes = jnp.where(lax.broadcasted_iota(jnp.int32, (slot, size), 0) == place, 1.0, 0.0)
        lanes = lanes.astype(low)
        rows = lax.broadcasted_iota(jnp.int32, (devices, size), 0) == owner
        values = refs[index][...]
        high = values.astype(low)
        rest = (values - high.astype(full)).astype(low)
        out_ref[index] = right_dot(
            jnp.where(rows, high.astype(full), 0.0).astype(low), lanes
        ) + right_dot(jnp.where(rows, rest.astype(full), 0.0).astype(low), lanes)
    for index in range(len(VECTORS), SLOTS):
        out_ref[index] = jnp.zeros((devices, slot), full)


def split_vectors(vectors, devices, slot):
    return pl.pallas_call(
        functools.partial(split_kernel, devices),
        out_shape=jax.ShapeDtypeStruct((SLOTS, devices, slot), full),
        compiler_params=pltpu.CompilerParams(vmem_limit_bytes=8 * 1024 * 1024),
        name="split_vectors",
    )(*vectors)


def count_kernel(chosen_ref, count_ref):
    rows = 64
    for block in range(FMB // rows):
        frames = block * rows + lax.broadcasted_iota(jnp.int32, (rows, NMASK), 0)

        def add_one(j, seen):
            return seen + jnp.where(frames == chosen_ref[pl.ds(j, 1), :], 1.0, 0.0)

        seen = lax.fori_loop(0, NEG, add_one, jnp.zeros((rows, NMASK), full), unroll=10)
        count_ref[pl.ds(block * rows, rows), :] = seen.astype(low)


def count_distractors(chosen):
    return pl.pallas_call(
        count_kernel,
        out_shape=jax.ShapeDtypeStruct((FMB, NMASK), low),
        in_specs=[pl.BlockSpec(memory_space=pltpu.VMEM)],
        out_specs=pl.BlockSpec(memory_space=pltpu.VMEM),
        cost_estimate=pl.CostEstimate(flops=1, bytes_accessed=1, transcendentals=0),
    )(chosen.T)


def head_lanes(rows, which):
    lane = lax.broadcasted_iota(jnp.int32, (rows, PAIR), 1)
    return (lane < HD) if which == 0 else (lane >= HD)
def fill_mask(row_ref, col_ref, mask_ref):
    mask_ref[...] = jnp.where(col_ref[...] == row_ref[...], 0.0, masked_score)
def spare_lanes(which):
    lane = lax.broadcasted_iota(jnp.int32, (FMB, PAIR), 1)
    return lane - HD if which == 0 else jnp.where(lane >= HD, -1, lane)


def lane_value(spare, columns):
    value = jnp.zeros((FMB, PAIR), full)
    for place, column in columns:
        value = jnp.where(spare == place, column, value)
    return value


def score_sides(q_ref, k_ref, col_ref, which):
    spare = spare_lanes(which)
    segment = col_ref[...]
    same = [(u, jnp.where(segment == u, 1.0, 0.0)) for u in range(UTTS)]
    keys = [(u, 1.0 - value) for u, value in same]
    queries = [(u, masked_score * value) for u, value in same]
    scaled = q_ref[...] * jnp.asarray(1.0 / math.sqrt(HD), low)
    keys = jnp.where(spare < 0, k_ref[...], lane_value(spare, keys).astype(low))
    queries = jnp.where(spare < 0, scaled, lane_value(spare, queries).astype(low))
    return keys, queries


def attention_kernel(col_ref, q_ref, k_ref, v_ref, mixed_ref, log_ref):
    parts, logs = [], []
    for which in range(2):
        keys, queries = score_sides(q_ref, k_ref, col_ref, which)
        scores = right_dot(queries, keys)
        top = jnp.max(scores, axis=1, keepdims=True)
        shares = jnp.exp(scores - top)
        total = jnp.sum(shares, axis=1, keepdims=True)
        parts.append(plain_dot(shares.astype(low), v_ref[...]) * (1.0 / total))
        logs.append(top + jnp.log(total))
    mixed_ref[...] = jnp.where(spare_lanes(0) < 0, parts[0], parts[1]).astype(low)
    log_ref[0] = jnp.concatenate(logs + [jnp.zeros((FMB, 6), full)], 1).T


def attention_forward(qk, values, seg):
    pairs = H // 2

    def spec(first):
        return pl.BlockSpec((FMB, PAIR), lambda i: (0, i + first))

    return pl.pallas_call(
        attention_kernel,
        grid=(pairs,),
        in_specs=[pl.BlockSpec((FMB, 1), lambda i: (0, 0)), spec(0), spec(pairs), spec(0)],
        out_specs=[spec(0), pl.BlockSpec((1, 8, FMB), lambda i: (i, 0, 0))],
        out_shape=[
            jax.ShapeDtypeStruct((FMB, D), low),
            jax.ShapeDtypeStruct((pairs, 8, FMB), full),
        ],
        compiler_params=pltpu.CompilerParams(vmem_limit_bytes=14 * 1024 * 1024),
        cost_estimate=pl.CostEstimate(flops=1, bytes_accessed=1, transcendentals=0),
        name="attention_forward",
    )(seg.reshape(FMB, 1), qk, qk, values)


def attention_back_kernel(row_ref, col_ref, q_ref, k_ref, v_ref, dm_ref, log_ref, out_ref, d_values_ref, mask_ref):
    i = pl.program_id(0)
    @pl.when(i == 0)
    def _():
        fill_mask(row_ref, col_ref, mask_ref)
    queries = q_ref[...] * jnp.asarray(1.0/math.sqrt(HD), low)
    d_mixed = dm_ref[...]
    keys_t = (k_ref[...] * jnp.asarray(1.0/math.sqrt(HD), low)).T
    d_keys = d_values = None
    d_queries = []
    for which in range(2):
        lanes = head_lanes(FMB, which)
        keys = jnp.where(lanes, k_ref[...], 0).astype(low)
        values = jnp.where(lanes, v_ref[...], 0).astype(low)
        shares = jnp.exp(right_dot(keys, queries) + mask_ref[...] - log_ref[0, which:which+1, :])
        d_shares = right_dot(values, d_mixed)
        inner = jnp.sum(shares * d_shares, axis=0, keepdims=True)
        d_scores = (shares * (d_shares - inner)).astype(low)
        dv = plain_dot(shares.astype(low), d_mixed)
        dk = plain_dot(d_scores, queries)
        d_queries.append(plain_dot(keys_t[which*HD:(which+1)*HD], d_scores))
        if which == 0:
            d_values, d_keys = dv, dk
        else:
            d_values, d_keys = jnp.where(lanes, dv, d_values), jnp.where(lanes, dk, d_keys)
    out_ref[:, pl.ds(pl.multiple_of(i*PAIR, PAIR), PAIR)] = jnp.concatenate(d_queries, 0).T.astype(low)
    out_ref[:, pl.ds(pl.multiple_of(D + i*PAIR, PAIR), PAIR)] = d_keys.astype(low)
    d_values_ref[...] = d_values.astype(low)
def attention_backward(qk, values, seg, d_mixed, logs):
    pairs = H//2
    spec = lambda off: pl.BlockSpec((FMB, PAIR), lambda i: (0, i+off))
    return pl.pallas_call(attention_back_kernel, grid=(pairs,),
        in_specs=[pl.BlockSpec((1,FMB), lambda i:(0,0)), pl.BlockSpec((FMB,1), lambda i:(0,0)), spec(0), spec(pairs), spec(0), spec(0), pl.BlockSpec((1,8,FMB), lambda i:(i,0,0))],
        out_specs=[pl.BlockSpec((FMB,2*D), lambda i:(0,0)), spec(0)],
        out_shape=[jax.ShapeDtypeStruct((FMB,2*D),low), jax.ShapeDtypeStruct((FMB,D),low)],
        scratch_shapes=[pltpu.VMEM((FMB,FMB),full)],
        compiler_params=pltpu.CompilerParams(vmem_limit_bytes=56 * 1024 * 1024),
        cost_estimate=pl.CostEstimate(flops=1, bytes_accessed=1, transcendentals=0),
        name="attention_backward")(seg.reshape(1,FMB), seg.reshape(FMB,1), qk, qk, values, d_mixed, logs)


def column_sum(value):
    return jnp.sum(value, axis=0, keepdims=True)
def middle_kernel(each, hidden_ref, slope_ref, blocks_ref, first_ref, final_ref, down_bias_ref, gain_ref, shift_ref, final_bias_ref,
                  targets_ref, counts_ref, masked_ref,
                  second_ref, d_proj_ref, d_ffn_ref, d_pre_ref, loss_ref, g_down_bias_ref, g_gain_ref, g_shift_ref, g_final_bias_ref, g_up_bias_ref,
                  res_ref, inv_ref, proj_ref, down_ref, d_second_ref, held_ref, sem):
    rows = 128
    steps = FMB // rows
    blocks = FF // D
    copy = pltpu.make_async_copy(blocks_ref.at[1], held_ref, sem)
    copy.start()
    copy.wait()
    for r in range(0, D, 2 * each):
        pair = [held_ref[r : r + 2 * each, j * D : (j + 1) * D].astype(full) for j in range(blocks)]
        for k in range(2):
            part = jnp.concatenate([p[k * each : (k + 1) * each] for p in pair], 0).astype(low)
            begin = (r + k * each) * blocks
            down_ref[begin : begin + blocks * each, :] = part
    res_ref[...] = plain_dot(hidden_ref[...], down_ref[...])
    for r in range(steps):
        at = slice(r*rows, (r+1)*rows)
        value = first_ref[at, :].astype(full) + res_ref[at, :] + down_bias_ref[...]
        center = value - jnp.mean(value, axis=1, keepdims=True)
        inverse = lax.rsqrt(jnp.mean(center*center, axis=1, keepdims=True) + norm_eps)
        hat = center * inverse
        res_ref[at, :] = hat
        inv_ref[at, :] = inverse
        second_ref[at, :] = (hat * gain_ref[...] + shift_ref[...]).astype(low)
    proj_ref[...] = plain_dot(second_ref[...], final_ref[...].astype(low)) + final_bias_ref[...]
    loss = jnp.zeros((1, 1), full)
    g_final_bias = jnp.zeros((1, PD), full)
    for r in range(steps):
        at = slice(r*rows, (r+1)*rows)
        value = proj_ref[at, :]
        inverse = lax.rsqrt(jnp.sum(value*value, axis=1, keepdims=True) + unit_eps)
        unit = value * inverse
        agreement = sharpness * lax.dot_general(unit, targets_ref[...], (((1,), (1,)), ((), ())), precision=precise, preferred_element_type=full)
        counts = counts_ref[at, :]
        masked = masked_ref[at, :] > 0
        drawn = counts > 0
        own = (lax.broadcasted_iota(jnp.int32, (rows, FMB), 0) + r*rows) == lax.broadcasted_iota(jnp.int32, (rows, FMB), 1)
        highest = jnp.max(jnp.where(drawn, agreement, masked_score), axis=1, keepdims=True)
        weights = counts * jnp.exp(jnp.where(drawn, agreement - highest, 0.0))
        total = jnp.where(masked, jnp.sum(weights, axis=1, keepdims=True), 1.0)
        own_score = jnp.sum(jnp.where(own, agreement, 0.0), axis=1, keepdims=True)
        loss += column_sum(jnp.where(masked, highest + jnp.log(total) - own_score, 0.0))
        d_agreement = jnp.where(masked, weights * (1.0 / total) - jnp.where(own, 1.0, 0.0), 0.0) * (sharpness / NMASK)
        d_unit = jnp.dot(d_agreement, targets_ref[...], precision=precise, preferred_element_type=full)
        d_proj = (inverse * (d_unit - unit * jnp.sum(d_unit*unit, axis=1, keepdims=True))).astype(low)
        d_proj_ref[at, :] = d_proj
        g_final_bias += column_sum(d_proj.astype(full))
    loss_ref[...] = loss * (1.0 / NMASK)
    g_final_bias_ref[...] = g_final_bias
    d_second_ref[...] = right_dot(d_proj_ref[...], final_ref[...].astype(low))
    g_gain = g_shift = g_down_bias = jnp.zeros((1, D), full)
    for r in range(steps):
        at = slice(r*rows, (r+1)*rows)
        grad = d_second_ref[at, :]
        hat = res_ref[at, :]
        g_gain += column_sum(grad * hat)
        g_shift += column_sum(grad)
        grad = grad * gain_ref[...]
        grad = inv_ref[at, :] * (grad - jnp.mean(grad, axis=1, keepdims=True) - hat * jnp.mean(grad*hat, axis=1, keepdims=True))
        d_ffn_ref[at, :] = grad.astype(low)
        g_down_bias += column_sum(grad.astype(low).astype(full))
    g_gain_ref[...] = g_gain
    g_shift_ref[...] = g_shift
    g_down_bias_ref[...] = g_down_bias
    for j in range(blocks):
        part = right_dot(d_ffn_ref[...], down_ref[j*D:(j+1)*D, :]) * slope_ref[:, j*D:(j+1)*D].astype(full)
        part = part.astype(low)
        d_pre_ref[:, j*D:(j+1)*D] = part
        g_up_bias_ref[:, j*D:(j+1)*D] = column_sum(part.astype(full))
def middle(each, hidden, slope, down, first_low, final, down_bias, gain, shift, final_bias, targets, counts, masked):
    def out(shape, dtype): return jax.ShapeDtypeStruct(shape, dtype)
    return pl.pallas_call(functools.partial(middle_kernel, each),
        grid=(1,),
        in_specs=[pl.BlockSpec(memory_space=pltpu.VMEM)] * 2 + [pl.BlockSpec(memory_space=pltpu.HBM)] + [pl.BlockSpec(memory_space=pltpu.VMEM)] * 9,
        out_specs=[pl.BlockSpec(memory_space=pltpu.VMEM)] * 10,
        out_shape=[out((FMB,D),low), out((FMB,PD),low), out((FMB,D),low), out((FMB,FF),low), out((1,1),full),
                   out((1,D),full), out((1,D),full), out((1,D),full), out((1,PD),full), out((1,FF),full)],
        scratch_shapes=[pltpu.VMEM((FMB,D),full), pltpu.VMEM((FMB,1),full), pltpu.VMEM((FMB,PD),full), pltpu.VMEM((FF,D),low), pltpu.VMEM((FMB,D),full), pltpu.VMEM((D,FF),low), pltpu.SemaphoreType.DMA(())],
        compiler_params=pltpu.CompilerParams(vmem_limit_bytes=34*1024*1024),
        cost_estimate=pl.CostEstimate(flops=1, bytes_accessed=1, transcendentals=0),
        name="middle")(hidden, slope, down, first_low, final, down_bias, gain, shift, final_bias, targets, counts, masked)


def normalized(value):
    center = value - jnp.mean(value, axis=1, keepdims=True)
    inverse = lax.rsqrt(jnp.mean(center * center, axis=1, keepdims=True) + norm_eps)
    return center * inverse, inverse


def normalize_back(grad, hat, inverse):
    shift = jnp.mean(grad, axis=1, keepdims=True)
    return inverse * (grad - shift - hat * jnp.mean(grad * hat, axis=1, keepdims=True))


def vector(ref, name):
    start = 0
    for known, size in VECTORS:
        if known == name:
            return ref[:, start : start + size]
        start += size


def row_steps(rows=128):
    return [slice(r, r + rows) for r in range(0, FMB, rows)]


def join_rows(own_ref, got_ref, whole_ref, core, rows, to=slice(None), at=slice(None)):
    for value in range(2):
        @pl.when(core == value)
        def _():
            for r in range(0, own_ref.shape[0], rows):
                for c, ref in enumerate((own_ref, got_ref)):
                    begin = 2 * r + ((value + c) % 2) * rows
                    part = ref[r : r + rows, at].astype(whole_ref.dtype)
                    whole_ref[begin : begin + rows, to] = part


def front_kernel(
    rows, own_ref, got_ref, left_own_ref, left_got_ref, right_own_ref, right_got_ref, masked_ref,
    place_ref,
    inputs_ref, normed_ref, hat_ref, slope_ref, inverse_ref, taps_ref, proj_ref, vec_ref,
    final_ref, parts_ref, total_ref,
):
    core, section = place_ref[0, 0], place_ref[0, 1]
    half = C // 2
    join_rows(right_own_ref, right_got_ref, taps_ref, core, 2 * rows)
    join_rows(left_own_ref, left_got_ref, proj_ref, core, rows, at=slice(0, D))
    more = slice(D, D + PD + SPARE)
    join_rows(left_own_ref, left_got_ref, parts_ref, core, rows, at=more)
    spread_parts(rows, parts_ref, vec_ref)
    for d in range(C // rows):
        at = slice(d * rows, (d + 1) * rows)
        head, tail = parts_ref[at, :PD], parts_ref[d * rows : d * rows + rows // 2, PD:]
        to = d * (rows + rows // 2)
        final_ref[to : to + rows, :] = head.astype(full)
        final_ref[to + rows : to + rows + rows // 2, :] = tail.astype(full)
    for tap in range(2):
        cols = slice(tap * half, (tap + 1) * half)
        own_taps = taps_ref[pl.ds(pl.multiple_of(tap * C + section * half, half), half), :]
        got_taps = taps_ref[pl.ds(pl.multiple_of(tap * C + (1 - section) * half, half), half), :]
        part = plain_dot(own_ref[:, cols], own_taps) + plain_dot(got_ref[:, cols], got_taps)
        if tap == 0:
            total_ref[...] = part
        else:
            total_ref[...] += part
    for at in row_steps():
        lifted, slope = gelu_and_slope(total_ref[at, :])
        hat, inverse = normalized(lifted)
        slope_ref[at, :] = slope.astype(low)
        hat_ref[at, :] = hat.astype(low)
        inverse_ref[at, :] = inverse
        normed = hat * vector(vec_ref, "ln0_gain") + vector(vec_ref, "ln0_bias")
        normed_ref[at, :] = normed.astype(low)
    for at in row_steps():
        encoded = plain_dot(normed_ref[at, :], proj_ref[...]) + vector(vec_ref, "proj0_bias")
        encoded = jnp.where(masked_ref[at, :] > 0, vector(vec_ref, "mask_emb"), encoded)
        inputs_ref[at, :] = encoded.astype(low)


def first_kernel(
    inputs_ref, mixed_ref, out_ref, vec_ref, first_ref, hat_ref, inverse_ref, total_ref
):
    total_ref[...] = plain_dot(mixed_ref[...], out_ref[:, D:])
    for at in row_steps():
        value = inputs_ref[at, :].astype(full) + total_ref[at, :] + vector(vec_ref, "out_bias")
        hat, inverse = normalized(value)
        hat_ref[at, :] = hat.astype(low)
        inverse_ref[at, :] = inverse
        value = hat * vector(vec_ref, "ln1_gain") + vector(vec_ref, "ln1_bias")
        first_ref[at, :] = value.astype(low)


def first_back_kernel(
    d_pre_ref, up_ref, d_ffn_ref, hat_ref, inverse_ref, out_ref, vec_ref,
    d_attn_ref, d_mixed_ref, g_gain_ref, g_shift_ref, g_out_bias_ref, d_first_ref, held_ref, sems,
):
    part = right_dot(d_pre_ref[...], fetched(up_ref, held_ref, sems))

    @pl.when(pl.program_id(0) == 0)
    def _():
        d_first_ref[...] = d_ffn_ref[...].astype(full) + part

    @pl.when(pl.program_id(0) > 0)
    def _():
        d_first_ref[...] += part

    @pl.when(pl.program_id(0) == pl.num_programs(0) - 1)
    def _():
        g_gain = g_shift = g_out_bias = jnp.zeros((1, D), full)
        for at in row_steps():
            grad = d_first_ref[at, :]
            hat = hat_ref[at, :].astype(full)
            g_gain += column_sum(grad * hat)
            g_shift += column_sum(grad)
            grad = normalize_back(grad * vector(vec_ref, "ln1_gain"), hat, inverse_ref[at, :])
            grad = grad.astype(low)
            d_attn_ref[at, :] = grad
            g_out_bias += column_sum(grad.astype(full))
        g_gain_ref[...] = g_gain
        g_shift_ref[...] = g_shift
        g_out_bias_ref[...] = g_out_bias
        d_mixed_ref[...] = right_dot(d_attn_ref[...], out_ref[:, D:]).astype(low)


def first_backward(d_pre, ffn, d_ffn, hat, inverse, vo, vectors):
    def held(*shape):
        return pl.BlockSpec(shape, lambda i: (0, 0))

    return pl.pallas_call(
        first_back_kernel,
        grid=(FF // D,),
        in_specs=[
            pl.BlockSpec((FMB, D), lambda i: (0, i)),
            pl.BlockSpec(memory_space=pltpu.HBM),
            held(FMB, D),
            held(FMB, D),
            held(FMB, 1),
            held(D, 2 * D),
            held(1, VECTOR_TOTAL),
        ],
        out_specs=[held(FMB, D)] * 2 + [held(1, D)] * 3,
        out_shape=[jax.ShapeDtypeStruct((FMB, D), low)] * 2
        + [jax.ShapeDtypeStruct((1, D), full)] * 3,
        scratch_shapes=[
            pltpu.VMEM((FMB, D), full),
            pltpu.VMEM((FF // D, D, D), low),
            pltpu.SemaphoreType.DMA((FF // D,)),
        ],
        compiler_params=pltpu.CompilerParams(vmem_limit_bytes=28 * 1024 * 1024),
        cost_estimate=pl.CostEstimate(flops=1, bytes_accessed=1, transcendentals=0),
        name="first_backward",
    )(d_pre, ffn, d_ffn, hat, inverse, vo, vectors)


def inputs_back_kernel(
    d_qk_ref, d_values_ref, qk_ref, v_ref, d_attn_ref, masked_ref,
    d_encoded_ref, g_mask_ref, g_proj_bias_ref, g_query_ref, g_value_ref, total_ref,
):
    total_ref[...] = right_dot(d_qk_ref[...], qk_ref[...])
    total_ref[...] += right_dot(d_values_ref[...], v_ref[:, :D])
    g_mask = g_proj_bias = g_query = g_value = jnp.zeros((1, D), full)
    for at in row_steps():
        grad = total_ref[at, :] + d_attn_ref[at, :].astype(full)
        masked = masked_ref[at, :] > 0
        g_mask += column_sum(jnp.where(masked, grad, 0.0))
        grad = jnp.where(masked, 0.0, grad).astype(low)
        d_encoded_ref[at, :] = grad
        g_proj_bias += column_sum(grad.astype(full))
        g_query += column_sum(d_qk_ref[at, :D].astype(full))
        g_value += column_sum(d_values_ref[at, :].astype(full))
    g_mask_ref[...] = g_mask
    g_proj_bias_ref[...] = g_proj_bias
    g_query_ref[...] = g_query
    g_value_ref[...] = g_value


def front_back_kernel(
    d_encoded_ref, proj_ref, hat_ref, slope_ref, inverse_ref, vec_ref,
    d_conv_ref, g_gain_ref, g_shift_ref, total_ref,
):
    total_ref[...] = right_dot(d_encoded_ref[...], proj_ref[...])
    g_gain = g_shift = jnp.zeros((1, C), full)
    for at in row_steps():
        grad = total_ref[at, :]
        hat = hat_ref[at, :].astype(full)
        g_gain += column_sum(grad * hat)
        g_shift += column_sum(grad)
        grad = normalize_back(grad * vector(vec_ref, "ln0_gain"), hat, inverse_ref[at, :])
        d_conv_ref[at, :] = (grad * slope_ref[at, :].astype(full)).astype(low)
    g_gain_ref[...] = g_gain
    g_shift_ref[...] = g_shift


def each_pair(rows, each):
    step = 2 * each if rows % (2 * each) == 0 else each
    return [(slice(r, r + step), slice(2 * r, 2 * r + 2 * step)) for r in range(0, rows, step)]


def join_cores(own_ref, got_ref, whole_ref, core, each, width=512):
    cols = own_ref.shape[1]
    for c in range(0, cols, width):
        at = slice(c, min(c + width, cols))
        for lane, whole in each_pair(own_ref.shape[0], each):
            own, got = own_ref[lane, at].astype(full), got_ref[lane, at].astype(full)
            zero = jnp.where(core == 0, own, got)
            one = jnp.where(core == 0, got, own)
            parts = []
            for r in range(0, own.shape[0], each):
                parts += [zero[r : r + each], one[r : r + each]]
            whole_ref[whole, at] = jnp.concatenate(parts, 0).astype(low)


def split_cores(whole_ref, keep_ref, send_ref, core, each, begin=0, width=384):
    cols = whole_ref.shape[1]
    for c in range(0, cols, width):
        at = slice(c, min(c + width, cols))
        to = slice(begin + at.start, begin + at.stop)
        for lane, whole in each_pair(whole_ref.shape[0] // 2, each):
            zero, one = [], []
            for r in range(whole.start, whole.stop, 2 * each):
                zero.append(whole_ref[r : r + each, at])
                one.append(whole_ref[r + each : r + 2 * each, at])
            zero, one = jnp.concatenate(zero, 0), jnp.concatenate(one, 0)
            keep_ref[lane, to] = jnp.where(core == 0, zero, one).astype(low)
            send_ref[lane, to] = jnp.where(core == 0, one, zero).astype(low)


def qkv_kernel(
    each, inputs_ref, qk_own_ref, qk_got_ref, vo_own_ref, vo_got_ref, vec_ref, core_ref,
    qk_ref, vo_ref, qk_rows_ref, values_ref,
):
    core = core_ref[0, 0]
    join_cores(qk_own_ref, qk_got_ref, qk_ref, core, each)
    join_cores(vo_own_ref, vo_got_ref, vo_ref, core, each)
    bias = vector(vec_ref, "qv_bias")
    rows = plain_dot(inputs_ref[...], qk_ref[:, :D]) + bias[:, :D]
    qk_rows_ref[:, :D] = rows.astype(low)
    qk_rows_ref[:, D:] = plain_dot(inputs_ref[...], qk_ref[:, D:]).astype(low)
    rows = plain_dot(inputs_ref[...], vo_ref[:, :D]) + bias[:, D:]
    values_ref[...] = rows.astype(low)


def lanes_kernel(each, up_ref, up_got_ref, down_ref, down_got_ref, out_ref):
    out_ref[0, 0, 0, :each, :] = added(up_ref[0], up_got_ref[0])
    for j in range(FF // D):
        rows = slice(j * each, (j + 1) * each)
        part = added(down_ref[0, rows, :], down_got_ref[0, rows, :])
        out_ref[0, 0, 0, each:, j * D : (j + 1) * D] = part


def add_lanes(each, depth, up, up_got, down, down_got):
    def where(i):
        return (i // (2 * depth), i % 2, (i // 2) % depth, 0, 0)

    up_rows = pl.BlockSpec((1, each, FF), lambda i: (i, 0, 0))
    down_rows = pl.BlockSpec((1, each * FF // D, D), lambda i: (i, 0, 0))
    up, up_got = [t.reshape(4 * depth, each, FF) for t in (up, up_got)]
    down, down_got = [t.reshape(4 * depth, each * FF // D, D) for t in (down, down_got)]
    return pl.pallas_call(
        functools.partial(lanes_kernel, each),
        grid=(4 * depth,),
        in_specs=[up_rows, up_rows, down_rows, down_rows],
        out_specs=pl.BlockSpec((1, 1, 1, 2 * each, FF), where),
        out_shape=jax.ShapeDtypeStruct((2, 2, depth, 2 * each, FF), low),
        compiler_params=pltpu.CompilerParams(vmem_limit_bytes=8 * 1024 * 1024),
        cost_estimate=pl.CostEstimate(flops=1, bytes_accessed=1, transcendentals=0),
        name="add_lanes",
    )(up, up_got, down, down_got)


def heads_grad_kernel(
    each, inputs_ref, mixed_ref, d_qk_ref, d_values_ref, d_attn_ref, core_ref,
    keep_ref, send_ref, turned_ref, total_ref,
):
    core = core_ref[0, 0]
    turned_ref[...] = inputs_ref[...].T
    for begin, rhs in (
        (0, d_qk_ref[:, :D]),
        (D, d_qk_ref[:, D:]),
        (2 * D, d_values_ref[...]),
        (3 * D, d_attn_ref[...]),
    ):
        if begin == 3 * D:
            turned_ref[...] = mixed_ref[...].T
        total_ref[...] = plain_dot(turned_ref[...], rhs)
        split_cores(total_ref, keep_ref, send_ref, core, each, begin)


def misc_grad_kernel(
    rows, each, normed_ref, d_encoded_ref, second_ref, d_proj_ref, own_ref, got_ref, d_conv_ref,
    vectors_ref, section_ref, terms_ref, final_ref, taps_ref,
):
    section = section_ref[0, 0]
    half = C // 2
    terms_ref[:, :D] = plain_dot(normed_ref[...].T, d_encoded_ref[...]).astype(low)
    final_ref[...] = plain_dot(second_ref[...].T, d_proj_ref[...])
    for d in range(C // rows):
        to = slice(d * rows, d * rows + rows)
        terms_ref[to, D : D + PD] = final_ref[d * each : d * each + rows, :].astype(low)
        last = [final_ref[d * each + rows : (d + 1) * each, :]]
        last.append(vectors_ref[d * (rows // 2) : (d + 1) * (rows // 2), :])
        terms_ref[to, D + PD : D + PD + SPARE] = jnp.concatenate(last, 0).astype(low)
    taps_ref[:C, :] = plain_dot(own_ref[...].T, d_conv_ref[...])
    taps_ref[C:, :] = plain_dot(got_ref[...].T, d_conv_ref[...])
    for tap in range(2):
        for side in range(2):
            for r in range(0, half, 2 * rows):
                at = tap * half + r
                own, got = taps_ref[at : at + 2 * rows, :], taps_ref[C + at : C + at + 2 * rows, :]
                value = jnp.where(section == side, own, got).astype(low)
                d = (tap * C + side * half + r) // (2 * rows)
                begin = D + PD + SPARE
                terms_ref[d * rows : (d + 1) * rows, begin : begin + C] = value[:rows]
                terms_ref[d * rows : (d + 1) * rows, begin + C :] = value[rows:]


def local_kernel(kernel, outs, scratch=(), scalars=0, static=(), far_in=(), far_out=()):
    def call(*args):
        near = len(args) - scalars
        held = [(args[i].shape, args[i].dtype) for i in far_in] + [outs[i] for i in far_out]
        first_held = len(args) + len(outs) + len(scratch)

        def run(*refs):
            refs, held_refs, sems = list(refs[:first_held]), refs[first_held:-2], refs[-2:]
            ins = [
                pltpu.make_async_copy(refs[i], held_refs[k], sems[0].at[k])
                for k, i in enumerate(far_in)
            ]
            ends = [
                pltpu.make_async_copy(
                    held_refs[len(far_in) + k], refs[len(args) + i], sems[1].at[k]
                )
                for k, i in enumerate(far_out)
            ]
            for copy in ins:
                copy.start()
            for copy in ins:
                copy.wait()
            for k, i in enumerate(list(far_in) + [len(args) + i for i in far_out]):
                refs[i] = held_refs[k]
            kernel(*static, *refs)
            for copy in ends:
                copy.start()
            for copy in ends:
                copy.wait()

        def space(index, far):
            return pl.BlockSpec(memory_space=pltpu.HBM if index in far else pltpu.VMEM)

        everything = [(a.shape, a.dtype) for a in args] + list(outs) + list(scratch)
        size = sum(math.prod(shape) * jnp.dtype(dtype).itemsize for shape, dtype in everything)
        return pl.pallas_call(
            run,
            out_shape=[jax.ShapeDtypeStruct(shape, dtype) for shape, dtype in outs],
            in_specs=[space(i, far_in) for i in range(near)]
            + [pl.BlockSpec(memory_space=pltpu.SMEM)] * scalars,
            out_specs=[space(i, far_out) for i in range(len(outs))],
            scratch_shapes=[pltpu.VMEM(shape, dtype) for shape, dtype in list(scratch) + held]
            + [pltpu.SemaphoreType.DMA((max(len(far), 1),)) for far in (far_in, far_out)],
            compiler_params=pltpu.CompilerParams(vmem_limit_bytes=56 * 1024 * 1024 if kernel.__name__ in ('front_kernel',) else size + 4 * 1024 * 1024),
            cost_estimate=pl.CostEstimate(flops=1, bytes_accessed=1, transcendentals=0),
            name=kernel.__name__,
        )(*args)

    return call


def fetched(ffn_ref, held_ref, sems):
    step, width = pl.program_id(0), held_ref.shape[2]

    def copy(k):
        source = ffn_ref.at[0, :, k * width : (k + 1) * width]
        return pltpu.make_async_copy(source, held_ref.at[k], sems.at[k])

    for k in range(held_ref.shape[0]):
        @pl.when(step == 0)
        def _():
            copy(k).start()

    for k in range(held_ref.shape[0]):
        @pl.when(step == k)
        def _():
            copy(k).wait()

    return held_ref[step]


def up_kernel(x_ref, ffn_ref, bias_ref, hidden_ref, slope_ref, pre_ref, held_ref, sems):
    pre_ref[...] = plain_dot(x_ref[...], fetched(ffn_ref, held_ref, sems))
    bias = bias_ref[...]
    rows = 32

    def step(r, carry):
        at = pl.ds(pl.multiple_of(r * rows, rows), rows)
        value, slope = gelu_and_slope(pre_ref[at, :] + bias)
        hidden_ref[at, :] = value.astype(low)
        slope_ref[at, :] = slope.astype(low)
        return carry

    lax.fori_loop(0, FMB // rows, step, 0)


def up_forward(x, ffn, vectors, tile=1024):
    begin = start_of["up_bias"] // tile
    columns = pl.BlockSpec((FMB, tile), lambda i: (0, i))
    return pl.pallas_call(
        up_kernel,
        grid=(FF // tile,),
        in_specs=[
            pl.BlockSpec((FMB, D), lambda i: (0, 0)),
            pl.BlockSpec(memory_space=pltpu.HBM),
            pl.BlockSpec((1, tile), lambda i: (0, begin + i)),
        ],
        out_specs=[columns, columns],
        out_shape=[jax.ShapeDtypeStruct((FMB, FF), low)] * 2,
        scratch_shapes=[
            pltpu.VMEM((FMB, tile), full),
            pltpu.VMEM((FF // tile, D, tile), low),
            pltpu.SemaphoreType.DMA((FF // tile,)),
        ],
        compiler_params=pltpu.CompilerParams(vmem_limit_bytes=22 * 1024 * 1024),
        cost_estimate=pl.CostEstimate(flops=1, bytes_accessed=1, transcendentals=0),
        name="up_forward",
    )(x, ffn, vectors)


def body(
    features,
    conv_weight,
    ln0_gain,
    ln0_bias,
    proj0_weight,
    proj0_bias,
    mask_emb,
    qkv_weight,
    qv_bias,
    out_weight,
    out_bias,
    ln1_gain,
    ln1_bias,
    up_weight,
    up_bias,
    down_weight,
    down_bias,
    ln2_gain,
    ln2_bias,
    final_weight,
    final_bias,
    codebook,
    lengths,
    mask_pos,
    distractors,
    target_ids,
):
    links = Links()
    section = links.y
    core = links.core.reshape(1, 1).astype(jnp.int32)
    place = jnp.stack([links.core, links.y]).reshape(1, 2).astype(jnp.int32)
    devices = 2 * links.per_section
    rows = C // devices

    own_rows = pick(features, section, 0)
    lens = pick(lengths, section, 0)
    positions = pick(mask_pos, section, 0)
    chosen = pick(distractors, section, 0)
    target_rows = pick(target_ids, section, 0)

    each = D // devices
    slot = (rows // 2) * SPARE // SLOTS
    blocks = FF // D
    down_blocks = down_weight.reshape(blocks, each, D).transpose(1, 0, 2).reshape(each, FF)
    ffn_full = lax.all_gather(jnp.stack([up_weight, down_blocks]), BOTH, axis=1, tiled=True)
    heads = Gather(links, jnp.concatenate([qkv_weight, out_weight], axis=1), 2 * D)
    heads.start_z()
    got_rows = links.over_y(pick(features, 1 - section, 0))
    late = (up_bias, proj0_weight, chosen)
    late = after([heads], *late)
    up_bias, proj0_weight, chosen = late
    heads.start_z_rest()
    vector_parts = [
        up_bias,
        ln0_gain,
        ln0_bias,
        proj0_bias,
        mask_emb,
        qv_bias,
        out_bias,
        ln1_gain,
        ln1_bias,
        down_bias,
        ln2_gain,
        ln2_bias,
        final_bias,
    ]
    vector_parts += [vector_parts[0]] * (SLOTS - len(vector_parts))
    vector_part = jnp.stack([jnp.pad(v, (0, slot - v.shape[0])) for v in vector_parts])
    misc = Gather(
        links,
        jnp.concatenate(
            [
                proj0_weight,
                final_weight[:rows],
                jnp.concatenate([final_weight[rows:], vector_part.reshape(rows // 2, SPARE)], 0),
                conv_weight[:rows],
                conv_weight[rows:],
            ],
            axis=1,
        ),
        D + PD + SPARE,
        parts=2,
    )
    misc.start_z()
    drawn = count_distractors(chosen)
    (drawn,) = after([heads, misc], drawn)

    heads.start_first()
    misc.start_z_rest()
    frame_ids = jnp.arange(FMB, dtype=jnp.int32)
    at_frame = positions[:, None] == frame_ids[None, :]
    is_masked = jnp.any(at_frame, axis=0)
    own_frame = (frame_ids[:, None] == frame_ids[None, :]) & is_masked[:, None]
    counts = lax.dot_general(
        at_frame.astype(low), drawn, (((0,), (1,)), ((), ())), preferred_element_type=full
    ) + own_frame.astype(full)
    entries = jnp.arange(codebook.shape[1], dtype=jnp.int32)
    targets = jnp.concatenate(
        [
            plain_dot((target_rows[0][:, None] == entries[None, :]).astype(low), codebook[0]),
            plain_dot((target_rows[1][:, None] == entries[None, :]).astype(low), codebook[1]),
        ],
        axis=1,
    )
    targets = targets * lax.rsqrt(jnp.sum(targets * targets, axis=1, keepdims=True) + unit_eps)
    stops = jnp.cumsum(lens)
    segment = jnp.sum(
        (frame_ids[:, None] >= stops[None, : UTTS - 1]).astype(jnp.int32), axis=1
    )
    masked = is_masked[:, None].astype(full)
    own_pairs = own_rows.reshape(FMB, C)
    counts, targets, got_rows, own_pairs, segment = after(
        [heads, misc], counts, targets, got_rows, own_pairs, segment
    )

    heads.start_second()
    misc.start_first()
    got_pairs = got_rows.reshape(FMB, C)
    (got_pairs,) = after([heads, misc], got_pairs)

    misc.start_second()
    heads.start_core()
    (got_pairs,) = after([misc, heads], got_pairs)

    misc.start_core()
    (got_pairs,) = after([misc], got_pairs)
    half = C // 2
    (
        inputs, normed, hat_zero, conv_slope, inverse_zero, conv_full, proj_full, vectors, final_full
    ) = local_kernel(
        front_kernel,
        [
            ((FMB, D), low),
            ((FMB, C), low),
            ((FMB, C), low),
            ((FMB, C), low),
            ((FMB, 1), full),
            ((2 * C, C), low),
            ((C, D), low),
            ((1, VECTOR_TOTAL), full),
            ((D, PD), full),
        ],
        [((C, PD + SPARE), low), ((FMB, C), full)],
        scalars=1,
        static=(rows,),
        far_in=(0, 1),
        far_out=(1, 2, 3, 4, 5, 6, 8),
    )(own_pairs, got_pairs, *misc.apart(), masked, place)
    taps = conv_full.reshape(2, 2, half, C)
    own_taps = pick(taps, section, 1).reshape(C, C)
    got_taps = pick(taps, 1 - section, 1).reshape(C, C)
    qk_full, vo_full, qk_rows, value_rows = local_kernel(
        qkv_kernel,
        [((D, 2 * D), low), ((D, 2 * D), low), ((FMB, 2 * D), low), ((FMB, D), low)],
        scalars=1,
        static=(each,),
        far_out=(0,),
    )(inputs, *heads.apart(), vectors, core)
    mixed, logs = attention_forward(qk_rows, value_rows, segment)
    first_low, hat_one, inverse_one = local_kernel(
        first_kernel, [((FMB, D), low), ((FMB, D), low), ((FMB, 1), full)], [((FMB, D), full)],
        far_out=(1, 2),
    )(inputs, mixed, vo_full, vectors)
    hidden_low, slope = up_forward(first_low, ffn_full, vectors)
    grad = {}
    (
        second_low,
        d_proj_low,
        d_ffn_low,
        d_pre_low,
        loss,
        grad["down_bias"],
        grad["ln2_gain"],
        grad["ln2_bias"],
        grad["final_bias"],
        grad["up_bias"],
    ) = middle(
        each,
        hidden_low,
        slope,
        ffn_full,
        first_low,
        final_full,
        *[
            vectors[:, start_of[name] : start_of[name] + size]
            for name, size in VECTORS
            if name in ("down_bias", "ln2_gain", "ln2_bias", "final_bias")
        ],
        targets,
        counts,
        masked,
    )

    loss = jnp.where(jnp.arange(2) == section, loss[0], 0.0)
    loss_got = links.over_y(loss)
    g_down = left_dot(hidden_low, d_ffn_low).astype(low)
    down = Sum(links, *by_core(links, g_down), D // 2)
    down.start_core()
    g_up = left_dot(first_low, d_pre_low).astype(low)
    up = Sum(links, *by_core(links, g_up), FF // 2)
    up.start_core()
    d_attn_low, d_mixed, grad["ln1_gain"], grad["ln1_bias"], grad["out_bias"] = (
        first_backward(d_pre_low, ffn_full, d_ffn_low, hat_one, inverse_one, vo_full, vectors)
    )
    d_mixed, d_attn_low, loss_got = after([down, up], d_mixed, d_attn_low, loss_got)

    lanes = add_lanes(
        each, links.depth, up.keep.reshape(-1, FF), up.got[0], down.keep.reshape(-1, D), down.got[0]
    )
    line = lax.psum_scatter(
        lanes.reshape(-1, FF), ("section", "x"), scatter_dimension=0, tiled=True
    ).reshape(links.depth, 2 * each, FF)
    d_qk, d_values = attention_backward(qk_rows, value_rows, segment, d_mixed, logs)
    keep, send = local_kernel(
        heads_grad_kernel,
        [((D // 2, 4 * D), low)] * 2,
        [((D, FMB), low), ((D, D), full)],
        scalars=1,
        static=(each,),
        far_in=(0, 1),
    )(inputs, mixed, d_qk, d_values, d_attn_low, core)

    heads = Sum(links, keep, send, 2 * D)
    heads.start_core()
    d_encoded, grad["mask_emb"], grad["proj0_bias"], g_query, g_value = local_kernel(
        inputs_back_kernel, [((FMB, D), low)] + [((1, D), full)] * 4, [((FMB, D), full)], far_in=(2, 3)
    )(d_qk, d_values, qk_full, vo_full, d_attn_low, masked)
    grad["qv_bias"] = jnp.concatenate([g_query, g_value], axis=1)
    (d_encoded,) = after([heads], d_encoded)

    heads.start_first()
    d_conv_low, grad["ln0_gain"], grad["ln0_bias"] = local_kernel(
        front_back_kernel,
        [((FMB, C), low), ((1, C), full), ((1, C), full)],
        [((FMB, C), full)],
        far_in=(1, 2, 3, 4),
    )(d_encoded, proj_full, hat_zero, conv_slope, inverse_zero, vectors)
    g_vectors = split_vectors([grad[name] for name, _ in VECTORS], devices, slot)
    g_vectors = g_vectors.transpose(1, 0, 2).reshape(devices * (rows // 2), SPARE)
    (terms,) = local_kernel(
        misc_grad_kernel,
        [((C, D + PD + SPARE + 2 * C), low)],
        [((D, PD), full), ((2 * C, C), full)],
        scalars=1,
        static=(rows, each),
        far_in=(0, 2, 3, 4, 5),
    )(
        normed, d_encoded, second_low, d_proj_low, own_pairs, got_pairs, d_conv_low, g_vectors,
        section.reshape(1, 1).astype(jnp.int32),
    )
    misc = Sum(links, *by_core(links, terms), D + PD + SPARE)
    misc.start_core()
    got_d = right_dot(d_conv_low, got_taps).astype(low).reshape(2 * FMB, half)
    own_d = right_dot(d_conv_low, own_taps).reshape(2 * FMB, half)
    own_d, got_d, line = after([misc, heads], own_d, got_d, line)

    heads.start_second()
    misc.start_first()
    ffn = Line(links, line)
    ffn.start_z()
    (got_d,) = after([heads, misc], got_d)

    heads.start_z()
    misc.start_second()
    ffn.start_z_rest()
    (got_d,) = after([heads, misc], got_d)

    heads.start_z_rest()
    misc.start_z()
    got_d = links.over_y(got_d)
    after([misc])
    misc.start_z_rest()
    features_grad = in_order(section, own_d, got_d.astype(full), -2)
    loss_each = loss + loss_got
    ffn_sum, heads_sum, misc_sum = ffn.total(), heads.total(), misc.total()
    up_sum = ffn_sum[:each]
    down_sum = jnp.concatenate(jnp.split(ffn_sum[each:], blocks, axis=1), axis=0)
    qkv_sum, out_sum = heads_sum[:, : 3 * D], heads_sum[:, 3 * D :]
    proj_sum = misc_sum[:, :D]
    left, right = misc_sum[:, D : D + PD + SPARE], misc_sum[:, D + PD + SPARE :]
    conv_sum = jnp.concatenate([right[:, :C], right[:, C:]], axis=0)
    final_sum = jnp.concatenate([left[:, :PD], left[: rows // 2, PD:]], axis=0)
    vector_sum = left[rows // 2 :, PD:].reshape(SLOTS, slot)
    share = {}
    for index, (name, size) in enumerate(VECTORS):
        share[name] = vector_sum[index, : size // devices]
    return (
        loss_each,
        features_grad,
        conv_sum,
        share["ln0_gain"],
        share["ln0_bias"],
        proj_sum,
        share["proj0_bias"],
        share["mask_emb"],
        qkv_sum,
        share["qv_bias"],
        out_sum,
        share["out_bias"],
        share["ln1_gain"],
        share["ln1_bias"],
        up_sum,
        share["up_bias"],
        down_sum,
        share["down_bias"],
        share["ln2_gain"],
        share["ln2_bias"],
        final_sum,
        share["final_bias"],
    )


def solution(mesh):
    grid = mesh.devices.reshape(2, -1, 2, 2)
    rows = P(BOTH, None)
    part = P(BOTH)
    weights = (rows, part, part, rows, part, part, rows, part, rows, part, part, part)
    weights += (rows, part, rows, part, part, part, rows, part)
    batch = [P(SPLIT, *[None] * more) for more in (1, 1, 2, 2)]
    return jax.shard_map(
        body,
        mesh=jax.sharding.Mesh(grid, BOTH),
        in_specs=(P(SPLIT, None, "section"),) + weights + (P(), *batch),
        out_specs=(P(SPLIT), P(SPLIT, None, "section")) + weights,
        check_vma=False,
    )
```

```python
import functools
import math

import jax
import jax.numpy as jnp
from jax import lax
from jax.experimental import pallas as pl
from jax.experimental.pallas import tpu as pltpu
from jax.sharding import PartitionSpec as P

D = 768
H = 12
HD = 64
FF = 3072
C = 512
PD = 256
UTTS = 3
PAIR = 2 * HD
FMB = 512
NEG = 100
NMASK = 256
SPARE = 256
SLOTS = 16

SPLIT = ("z", "x", "core")
BOTH = ("section",) + SPLIT
norm_eps = 1e-05
unit_eps = 1e-06
sharpness = 10.0
masked_score = -1000000000.0
precise = lax.Precision.HIGHEST
low = jnp.bfloat16
full = jnp.float32

VECTORS = (
    ("up_bias", FF),
    ("ln0_gain", C),
    ("ln0_bias", C),
    ("proj0_bias", D),
    ("mask_emb", D),
    ("qv_bias", 2 * D),
    ("out_bias", D),
    ("ln1_gain", D),
    ("ln1_bias", D),
    ("down_bias", D),
    ("ln2_gain", D),
    ("ln2_bias", D),
    ("final_bias", PD),
)
VECTOR_TOTAL = sum(size for _, size in VECTORS)
start_of = {name: sum(size for _, size in VECTORS[:i]) for i, (name, _) in enumerate(VECTORS)}
QV_START = start_of["qv_bias"]


def plain_dot(left_side, right_side):
    return jnp.dot(left_side, right_side, preferred_element_type=full)


def left_dot(left_side, right_side):
    return lax.dot_general(
        left_side, right_side, (((0,), (0,)), ((), ())), preferred_element_type=full
    )


def right_dot(left_side, right_side):
    return lax.dot_general(
        left_side, right_side, (((1,), (1,)), ((), ())), preferred_element_type=full
    )


def gelu_and_slope(x):
    size = jnp.abs(x)
    bell = jnp.exp(-0.5 * x * x)
    t = 1.0 / (1.0 + 0.23164189 * size)
    poly = t * (0.127414796 + t * (-0.142248368 + t * (0.7107068705 + t * (-0.7265760135 + t * 0.5307027145))))
    tail = poly * bell
    below = jnp.where(x >= 0, 1.0 - tail, tail)
    return x * below, below + x * (0.3989422804 * bell)


class Links:
    def __init__(self):
        self.depth = lax.axis_size("z")
        self.per_section = 4 * self.depth
        self.core = lax.axis_index("core")
        self.x = lax.axis_index("x")
        self.z = lax.axis_index("z")
        self.y = lax.axis_index("section")
        self.sizes, self.upper = [], []
        size, place = self.depth, self.z
        while size > 1:
            self.sizes.append(size)
            self.upper.append((place >= size // 2).astype(jnp.int32))
            place = jnp.where(place >= size // 2, size - 1 - place, place)
            size //= 2

    def move(self, value, where):
        pairs = []
        for y in range(2):
            for z in range(self.depth):
                for x in range(2):
                    for core in range(2):
                        ty, tz, tx, tcore = where(y, z, x, core)
                        pairs.append(
                            (
                                y * self.per_section + z * 4 + x * 2 + core,
                                ty * self.per_section + tz * 4 + tx * 2 + tcore,
                            )
                        )
        return lax.ppermute(value, BOTH, pairs)

    def over_x(self, value):
        return self.move(value, lambda y, z, x, core: (y, z, 1 - x, core))

    def over_y(self, value):
        return self.move(value, lambda y, z, x, core: (1 - y, z, x, core))

    def over_core(self, value):
        return self.move(value, lambda y, z, x, core: (y, z, x, 1 - core))

    def over_both(self, value):
        return self.move(value, lambda y, z, x, core: (1 - y, z, 1 - x, core))

    def along_z(self, value, steps):
        return self.move(value, lambda y, z, x, core: (y, (z + steps) % self.depth, x, core))

    def over_z(self, value, size):
        def where(y, z, x, core):
            return (y, z - z % size + size - 1 - z % size, x, core)

        return self.move(value, where)


def pick(value, index, axis):
    axis = axis % value.ndim
    return lax.squeeze(lax.dynamic_slice_in_dim(value, index, 1, axis), (axis,))


def in_order(index, own, got, axis):
    axis = axis % own.ndim
    own, got = jnp.expand_dims(own, axis), jnp.expand_dims(got, axis)
    shape = own.shape[:axis] + (2,) + own.shape[axis + 1 :]
    return jnp.where(lax.broadcasted_iota(jnp.int32, shape, axis) == index, own, got)


def in_line(uppers, own, got):
    shape = (own.shape[0], 2) + own.shape[1:]
    turn = (
        lax.broadcasted_iota(jnp.int32, shape, 0) + lax.broadcasted_iota(jnp.int32, shape, 1)
    ) % 2
    line = jnp.where(turn == uppers[-1], jnp.expand_dims(own, 1), jnp.expand_dims(got, 1))
    line = line.reshape((-1,) + own.shape[1:])
    for _ in range(2, len(uppers)):
        line = jnp.concatenate([line[:, 0], jnp.flip(line[:, 1], 0)], axis=0)
    return line


class Gather:
    def __init__(self, links, line, cut, parts=1):
        self.links, self.line, self.cut, self.parts = links, line, cut, parts
        self.got = []

    def start_z(self):
        self.got = [self.links.over_z(self.line, self.links.sizes[0])]

    def start_z_rest(self):
        links = self.links
        for step in range(1, len(links.sizes)):
            self.line = in_order(links.upper[step - 1], self.line, self.got[0], 0)
            self.got = [links.over_z(self.line, links.sizes[step])]

    def start_first(self):
        links = self.links
        line = in_line(links.upper, self.line, self.got[0])
        self.first, self.second = line[..., : self.cut], line[..., self.cut :]
        if self.parts > 1:
            shape = self.second.shape
            self.second = self.second.reshape(shape[:2] + (self.parts, -1)).swapaxes(1, 2)
            self.second = self.second.reshape(shape[0], -1, shape[2] // self.parts)
        self.got = [links.over_x(self.first), links.over_y(self.second)]

    def start_second(self):
        links = self.links
        self.first = in_order(links.x, self.first, self.got[0], -2)
        self.second = in_order(links.y, self.second, self.got[1], -3)
        self.got = [links.over_y(self.first), links.over_x(self.second)]

    def start_core(self):
        links = self.links
        self.lanes = [
            in_order(links.y, self.first, self.got[0], -4),
            in_order(links.x, self.second, self.got[1], -2),
        ]
        self.lanes = lax.optimization_barrier(self.lanes)
        self.got = [links.over_core(lane) for lane in self.lanes]

    def whole(self):
        core = self.links.core
        return [
            in_order(core, own, got, -2).reshape(-1, own.shape[-1])
            for own, got in zip(self.lanes, self.got)
        ]

    def apart(self):
        lanes = [x for pair in zip(self.lanes, self.got) for x in pair]
        return [x.reshape(-1, x.shape[-1]) for x in lanes]


class Line:
    def __init__(self, links, line):
        self.links, self.line = links, line

    def start_z(self):
        self.start_line(self.line)

    def start_line(self, line):
        links = self.links
        for size in links.sizes[:-1]:
            line = jnp.stack([line[: size // 2], jnp.flip(line[size // 2 :], 0)], axis=1)
        self.line = line
        self.got = [links.over_z(pick(line, 1 - links.upper[-1], 0), links.sizes[-1])]

    def start_z_rest(self):
        links = self.links
        for step in range(len(links.sizes) - 2, -1, -1):
            self.line = added(pick(self.line, links.upper[step + 1], 0), self.got[0])
            away = pick(self.line, 1 - links.upper[step], 0)
            self.got = [links.over_z(away, links.sizes[step])]

    def total(self):
        return pick(self.line, self.links.upper[0], 0).astype(full) + self.got[0].astype(full)


class Sum(Line):
    def __init__(self, links, keep, send, cut):
        self.links, self.cut = links, cut
        self.grid = (2, links.depth, 2, -1, keep.shape[-1])
        self.keep, self.send = keep.reshape(self.grid), send
        self.got = []

    def start_core(self):
        self.got = [self.links.over_core(self.send)]

    def start_first(self):
        links = self.links
        lane = added(self.keep, self.got[0].reshape(self.grid))
        self.first, self.second = lane[..., : self.cut], lane[..., self.cut :]
        self.got = [
            links.over_x(pick(self.first, 1 - links.x, -3)),
            links.over_y(pick(self.second, 1 - links.y, -5)),
        ]

    def start_plane(self):
        links = self.links
        lane = added(self.keep, self.got[0].reshape(self.grid))

        def part(y, x):
            return pick(pick(lane, x, -3), y, 0)

        self.line = part(links.y, links.x)
        self.got = [
            links.over_x(part(links.y, 1 - links.x)),
            links.over_y(part(1 - links.y, links.x)),
            links.over_both(part(1 - links.y, 1 - links.x)),
        ]

    def line_of(self):
        links = self.links
        if len(self.got) == 3:
            return total_of(self.line, self.got).astype(low)
        first = added(pick(self.first, links.y, -4), self.got[0])
        second = added(pick(self.second, links.x, -3), self.got[1])
        return jnp.concatenate([first, second], -1)

    def start_straight_z(self):
        links, line = self.links, self.line_of()
        self.line = pick(line, links.z, 0)
        self.got = [
            links.along_z(pick(line, (links.z + k) % links.depth, 0), k)
            for k in range(1, links.depth)
        ]

    def straight_total(self):
        return total_of(self.line, self.got)

    def start_second(self):
        links = self.links
        self.first = added(pick(self.first, links.x, -3), self.got[0])
        self.second = added(pick(self.second, links.y, -5), self.got[1])
        self.got = [
            links.over_y(pick(self.first, 1 - links.y, -4)),
            links.over_x(pick(self.second, 1 - links.x, -3)),
        ]

    def start_z(self):
        self.start_line(self.line_of())


def by_core(links, terms):
    lanes = terms.reshape(links.per_section, 2, -1, terms.shape[-1])
    return [
        pick(lanes, core, 1).reshape(-1, terms.shape[-1]) for core in (links.core, 1 - links.core)
    ]


def total_of(own, others):
    out = own.astype(full)
    for got in others:
        out = out + got.astype(full)
    return out


def added(own, got):
    return (own.astype(full) + got.astype(full)).astype(low)


def after(moves, *values):
    bound = lax.optimization_barrier((tuple(tuple(m.got) for m in moves), values))
    for move, got in zip(moves, bound[0]):
        move.got = list(got)
    return bound[1]


def owner_of(columns, part):
    factor = -(-(1 << 20) // part)
    assert all((n * factor) >> 20 == n // part for n in range(columns))
    lane = lax.broadcasted_iota(jnp.int32, (1, columns), 1)
    return lax.shift_right_logical(lane * factor, 20)


def spread_parts(rows, parts_ref, out_ref):
    start = 0
    devices = C // rows
    slot = (rows // 2) * SPARE // SLOTS
    each_row = SPARE // slot
    shape = (devices, C)
    across = lax.broadcasted_iota(jnp.int32, shape, 1)
    first = lax.broadcasted_iota(jnp.int32, shape, 0) * rows + rows // 2
    held = [
        plain_dot(jnp.where(across == first + k, 1.0, 0.0).astype(low), parts_ref[:, PD:]).astype(low)
        for k in range(rows // 2)
    ]
    for index, (_, size) in enumerate(VECTORS):
        part = size // devices
        owner = owner_of(size, part)
        place = lax.broadcasted_iota(jnp.int32, (1, size), 1) - owner * part
        lanes = jnp.where(lax.broadcasted_iota(jnp.int32, (slot, size), 0) == place, 1.0, 0.0)
        at = lax.broadcasted_iota(jnp.int32, (devices, size), 0) == owner
        begin = (index % each_row) * slot
        mine = held[index // each_row][:, begin : begin + slot]
        out_ref[:, start : start + size] = jnp.sum(
            jnp.where(at, plain_dot(mine, lanes.astype(low)), 0.0), axis=0, keepdims=True
        )
        start += size


def split_kernel(devices, *refs):
    out_ref = refs[-1]
    slot = out_ref.shape[2]
    for index, (_, size) in enumerate(VECTORS):
        part = size // devices
        owner = owner_of(size, part)
        place = lax.broadcasted_iota(jnp.int32, (1, size), 1) - owner * part
        lanes = jnp.where(lax.broadcasted_iota(jnp.int32, (slot, size), 0) == place, 1.0, 0.0)
        lanes = lanes.astype(low)
        rows = lax.broadcasted_iota(jnp.int32, (devices, size), 0) == owner
        values = refs[index][...]
        high = values.astype(low)
        rest = (values - high.astype(full)).astype(low)
        out_ref[index] = right_dot(
            jnp.where(rows, high.astype(full), 0.0).astype(low), lanes
        ) + right_dot(jnp.where(rows, rest.astype(full), 0.0).astype(low), lanes)
    for index in range(len(VECTORS), SLOTS):
        out_ref[index] = jnp.zeros((devices, slot), full)


def split_vectors(vectors, devices, slot):
    return pl.pallas_call(
        functools.partial(split_kernel, devices),
        out_shape=jax.ShapeDtypeStruct((SLOTS, devices, slot), full),
        compiler_params=pltpu.CompilerParams(vmem_limit_bytes=8 * 1024 * 1024),
        name="split_vectors",
    )(*vectors)


def count_kernel(chosen_ref, count_ref):
    rows = 64
    for block in range(FMB // rows):
        frames = block * rows + lax.broadcasted_iota(jnp.int32, (rows, NMASK), 0)

        def add_one(j, seen):
            return seen + jnp.where(frames == chosen_ref[pl.ds(j, 1), :], 1.0, 0.0)

        seen = lax.fori_loop(0, NEG, add_one, jnp.zeros((rows, NMASK), full), unroll=10)
        count_ref[pl.ds(block * rows, rows), :] = seen.astype(low)


def count_distractors(chosen):
    return pl.pallas_call(
        count_kernel,
        out_shape=jax.ShapeDtypeStruct((FMB, NMASK), low),
        in_specs=[pl.BlockSpec(memory_space=pltpu.VMEM)],
        out_specs=pl.BlockSpec(memory_space=pltpu.VMEM),
        cost_estimate=pl.CostEstimate(flops=1, bytes_accessed=1, transcendentals=0),
    )(chosen.T)


def head_lanes(rows, which):
    lane = lax.broadcasted_iota(jnp.int32, (rows, PAIR), 1)
    return (lane < HD) if which == 0 else (lane >= HD)
def fill_mask(row_ref, col_ref, mask_ref):
    mask_ref[...] = jnp.where(col_ref[...] == row_ref[...], 0.0, masked_score)
def spare_lanes(which):
    lane = lax.broadcasted_iota(jnp.int32, (FMB, PAIR), 1)
    return lane - HD if which == 0 else jnp.where(lane >= HD, -1, lane)


def lane_value(spare, columns):
    value = jnp.zeros((FMB, PAIR), full)
    for place, column in columns:
        value = jnp.where(spare == place, column, value)
    return value


def score_sides(q_ref, k_ref, col_ref, which):
    spare = spare_lanes(which)
    segment = col_ref[...]
    same = [(u, jnp.where(segment == u, 1.0, 0.0)) for u in range(UTTS)]
    keys = [(u, 1.0 - value) for u, value in same]
    queries = [(u, masked_score * value) for u, value in same]
    scaled = q_ref[...] * jnp.asarray(1.0 / math.sqrt(HD), low)
    keys = jnp.where(spare < 0, k_ref[...], lane_value(spare, keys).astype(low))
    queries = jnp.where(spare < 0, scaled, lane_value(spare, queries).astype(low))
    return keys, queries


def attention_kernel(col_ref, q_ref, k_ref, v_ref, mixed_ref, log_ref):
    parts, logs = [], []
    for which in range(2):
        keys, queries = score_sides(q_ref, k_ref, col_ref, which)
        scores = right_dot(queries, keys)
        top = jnp.max(scores, axis=1, keepdims=True)
        shares = jnp.exp(scores - top)
        total = jnp.sum(shares, axis=1, keepdims=True)
        parts.append(plain_dot(shares.astype(low), v_ref[...]) * (1.0 / total))
        logs.append(top + jnp.log(total))
    mixed_ref[...] = jnp.where(spare_lanes(0) < 0, parts[0], parts[1]).astype(low)
    log_ref[0] = jnp.concatenate(logs + [jnp.zeros((FMB, 6), full)], 1).T


def attention_forward(qk, values, seg):
    pairs = H // 2

    def spec(first):
        return pl.BlockSpec((FMB, PAIR), lambda i: (0, i + first))

    return pl.pallas_call(
        attention_kernel,
        grid=(pairs,),
        in_specs=[pl.BlockSpec((FMB, 1), lambda i: (0, 0)), spec(0), spec(pairs), spec(0)],
        out_specs=[spec(0), pl.BlockSpec((1, 8, FMB), lambda i: (i, 0, 0))],
        out_shape=[
            jax.ShapeDtypeStruct((FMB, D), low),
            jax.ShapeDtypeStruct((pairs, 8, FMB), full),
        ],
        compiler_params=pltpu.CompilerParams(vmem_limit_bytes=14 * 1024 * 1024),
        cost_estimate=pl.CostEstimate(flops=1, bytes_accessed=1, transcendentals=0),
        name="attention_forward",
    )(seg.reshape(FMB, 1), qk, qk, values)


def attention_back_kernel(row_ref, col_ref, q_ref, k_ref, v_ref, dm_ref, log_ref, out_ref, d_values_ref, mask_ref):
    i = pl.program_id(0)
    @pl.when(i == 0)
    def _():
        fill_mask(row_ref, col_ref, mask_ref)
    queries = q_ref[...] * jnp.asarray(1.0/math.sqrt(HD), low)
    d_mixed = dm_ref[...]
    keys_t = (k_ref[...] * jnp.asarray(1.0/math.sqrt(HD), low)).T
    d_keys = d_values = None
    d_queries = []
    for which in range(2):
        lanes = head_lanes(FMB, which)
        keys = jnp.where(lanes, k_ref[...], 0).astype(low)
        values = jnp.where(lanes, v_ref[...], 0).astype(low)
        shares = jnp.exp(right_dot(keys, queries) + mask_ref[...] - log_ref[0, which:which+1, :])
        d_shares = right_dot(values, d_mixed)
        inner = jnp.sum(shares * d_shares, axis=0, keepdims=True)
        d_scores = (shares * (d_shares - inner)).astype(low)
        dv = plain_dot(shares.astype(low), d_mixed)
        dk = plain_dot(d_scores, queries)
        d_queries.append(plain_dot(keys_t[which*HD:(which+1)*HD], d_scores))
        if which == 0:
            d_values, d_keys = dv, dk
        else:
            d_values, d_keys = jnp.where(lanes, dv, d_values), jnp.where(lanes, dk, d_keys)
    out_ref[:, pl.ds(pl.multiple_of(i*PAIR, PAIR), PAIR)] = jnp.concatenate(d_queries, 0).T.astype(low)
    out_ref[:, pl.ds(pl.multiple_of(D + i*PAIR, PAIR), PAIR)] = d_keys.astype(low)
    d_values_ref[...] = d_values.astype(low)
def attention_backward(qk, values, seg, d_mixed, logs):
    pairs = H//2
    spec = lambda off: pl.BlockSpec((FMB, PAIR), lambda i: (0, i+off))
    return pl.pallas_call(attention_back_kernel, grid=(pairs,),
        in_specs=[pl.BlockSpec((1,FMB), lambda i:(0,0)), pl.BlockSpec((FMB,1), lambda i:(0,0)), spec(0), spec(pairs), spec(0), spec(0), pl.BlockSpec((1,8,FMB), lambda i:(i,0,0))],
        out_specs=[pl.BlockSpec((FMB,2*D), lambda i:(0,0)), spec(0)],
        out_shape=[jax.ShapeDtypeStruct((FMB,2*D),low), jax.ShapeDtypeStruct((FMB,D),low)],
        scratch_shapes=[pltpu.VMEM((FMB,FMB),full)],
        compiler_params=pltpu.CompilerParams(vmem_limit_bytes=56 * 1024 * 1024),
        cost_estimate=pl.CostEstimate(flops=1, bytes_accessed=1, transcendentals=0),
        name="attention_backward")(seg.reshape(1,FMB), seg.reshape(FMB,1), qk, qk, values, d_mixed, logs)


def column_sum(value):
    return jnp.sum(value, axis=0, keepdims=True)
def middle_kernel(each, hidden_ref, slope_ref, blocks_ref, first_ref, final_ref, down_bias_ref, gain_ref, shift_ref, final_bias_ref,
                  targets_ref, counts_ref, masked_ref,
                  second_ref, d_proj_ref, d_ffn_ref, d_pre_ref, loss_ref, g_down_bias_ref, g_gain_ref, g_shift_ref, g_final_bias_ref, g_up_bias_ref,
                  res_ref, inv_ref, proj_ref, down_ref, d_second_ref, held_ref, sem):
    rows = 128
    steps = FMB // rows
    blocks = FF // D
    copy = pltpu.make_async_copy(blocks_ref.at[1], held_ref, sem)
    copy.start()
    copy.wait()
    for r in range(0, D, 2 * each):
        pair = [held_ref[r : r + 2 * each, j * D : (j + 1) * D].astype(full) for j in range(blocks)]
        for k in range(2):
            part = jnp.concatenate([p[k * each : (k + 1) * each] for p in pair], 0).astype(low)
            begin = (r + k * each) * blocks
            down_ref[begin : begin + blocks * each, :] = part
    res_ref[...] = plain_dot(hidden_ref[...], down_ref[...])
    for r in range(steps):
        at = slice(r*rows, (r+1)*rows)
        value = first_ref[at, :].astype(full) + res_ref[at, :] + down_bias_ref[...]
        center = value - jnp.mean(value, axis=1, keepdims=True)
        inverse = lax.rsqrt(jnp.mean(center*center, axis=1, keepdims=True) + norm_eps)
        hat = center * inverse
        res_ref[at, :] = hat
        inv_ref[at, :] = inverse
        second_ref[at, :] = (hat * gain_ref[...] + shift_ref[...]).astype(low)
    proj_ref[...] = plain_dot(second_ref[...], final_ref[...].astype(low)) + final_bias_ref[...]
    loss = jnp.zeros((1, 1), full)
    g_final_bias = jnp.zeros((1, PD), full)
    for r in range(steps):
        at = slice(r*rows, (r+1)*rows)
        value = proj_ref[at, :]
        inverse = lax.rsqrt(jnp.sum(value*value, axis=1, keepdims=True) + unit_eps)
        unit = value * inverse
        agreement = sharpness * lax.dot_general(unit, targets_ref[...], (((1,), (1,)), ((), ())), precision=precise, preferred_element_type=full)
        counts = counts_ref[at, :]
        masked = masked_ref[at, :] > 0
        drawn = counts > 0
        own = (lax.broadcasted_iota(jnp.int32, (rows, FMB), 0) + r*rows) == lax.broadcasted_iota(jnp.int32, (rows, FMB), 1)
        highest = jnp.max(jnp.where(drawn, agreement, masked_score), axis=1, keepdims=True)
        weights = counts * jnp.exp(jnp.where(drawn, agreement - highest, 0.0))
        total = jnp.where(masked, jnp.sum(weights, axis=1, keepdims=True), 1.0)
        own_score = jnp.sum(jnp.where(own, agreement, 0.0), axis=1, keepdims=True)
        loss += column_sum(jnp.where(masked, highest + jnp.log(total) - own_score, 0.0))
        d_agreement = jnp.where(masked, weights * (1.0 / total) - jnp.where(own, 1.0, 0.0), 0.0) * (sharpness / NMASK)
        d_unit = jnp.dot(d_agreement, targets_ref[...], precision=precise, preferred_element_type=full)
        d_proj = (inverse * (d_unit - unit * jnp.sum(d_unit*unit, axis=1, keepdims=True))).astype(low)
        d_proj_ref[at, :] = d_proj
        g_final_bias += column_sum(d_proj.astype(full))
    loss_ref[...] = loss * (1.0 / NMASK)
    g_final_bias_ref[...] = g_final_bias
    d_second_ref[...] = right_dot(d_proj_ref[...], final_ref[...].astype(low))
    g_gain = g_shift = g_down_bias = jnp.zeros((1, D), full)
    for r in range(steps):
        at = slice(r*rows, (r+1)*rows)
        grad = d_second_ref[at, :]
        hat = res_ref[at, :]
        g_gain += column_sum(grad * hat)
        g_shift += column_sum(grad)
        grad = grad * gain_ref[...]
        grad = inv_ref[at, :] * (grad - jnp.mean(grad, axis=1, keepdims=True) - hat * jnp.mean(grad*hat, axis=1, keepdims=True))
        d_ffn_ref[at, :] = grad.astype(low)
        g_down_bias += column_sum(grad.astype(low).astype(full))
    g_gain_ref[...] = g_gain
    g_shift_ref[...] = g_shift
    g_down_bias_ref[...] = g_down_bias
    for j in range(blocks):
        part = right_dot(d_ffn_ref[...], down_ref[j*D:(j+1)*D, :]) * slope_ref[:, j*D:(j+1)*D].astype(full)
        part = part.astype(low)
        d_pre_ref[:, j*D:(j+1)*D] = part
        g_up_bias_ref[:, j*D:(j+1)*D] = column_sum(part.astype(full))
def middle(each, hidden, slope, down, first_low, final, down_bias, gain, shift, final_bias, targets, counts, masked):
    def out(shape, dtype): return jax.ShapeDtypeStruct(shape, dtype)
    return pl.pallas_call(functools.partial(middle_kernel, each),
        grid=(1,),
        in_specs=[pl.BlockSpec(memory_space=pltpu.VMEM)] * 2 + [pl.BlockSpec(memory_space=pltpu.HBM)] + [pl.BlockSpec(memory_space=pltpu.VMEM)] * 9,
        out_specs=[pl.BlockSpec(memory_space=pltpu.VMEM)] * 10,
        out_shape=[out((FMB,D),low), out((FMB,PD),low), out((FMB,D),low), out((FMB,FF),low), out((1,1),full),
                   out((1,D),full), out((1,D),full), out((1,D),full), out((1,PD),full), out((1,FF),full)],
        scratch_shapes=[pltpu.VMEM((FMB,D),full), pltpu.VMEM((FMB,1),full), pltpu.VMEM((FMB,PD),full), pltpu.VMEM((FF,D),low), pltpu.VMEM((FMB,D),full), pltpu.VMEM((D,FF),low), pltpu.SemaphoreType.DMA(())],
        compiler_params=pltpu.CompilerParams(vmem_limit_bytes=34*1024*1024),
        cost_estimate=pl.CostEstimate(flops=1, bytes_accessed=1, transcendentals=0),
        name="middle")(hidden, slope, down, first_low, final, down_bias, gain, shift, final_bias, targets, counts, masked)


def normalized(value):
    center = value - jnp.mean(value, axis=1, keepdims=True)
    inverse = lax.rsqrt(jnp.mean(center * center, axis=1, keepdims=True) + norm_eps)
    return center * inverse, inverse


def normalize_back(grad, hat, inverse):
    shift = jnp.mean(grad, axis=1, keepdims=True)
    return inverse * (grad - shift - hat * jnp.mean(grad * hat, axis=1, keepdims=True))


def vector(ref, name):
    start = 0
    for known, size in VECTORS:
        if known == name:
            return ref[:, start : start + size]
        start += size


def row_steps(rows=128):
    return [slice(r, r + rows) for r in range(0, FMB, rows)]


def join_rows(own_ref, got_ref, whole_ref, core, rows, to=slice(None), at=slice(None)):
    for value in range(2):
        @pl.when(core == value)
        def _():
            for r in range(0, own_ref.shape[0], rows):
                for c, ref in enumerate((own_ref, got_ref)):
                    begin = 2 * r + ((value + c) % 2) * rows
                    part = ref[r : r + rows, at].astype(whole_ref.dtype)
                    whole_ref[begin : begin + rows, to] = part


def front_kernel(
    rows, own_ref, got_ref, left_own_ref, left_got_ref, right_own_ref, right_got_ref, masked_ref,
    place_ref,
    inputs_ref, normed_ref, hat_ref, slope_ref, inverse_ref, taps_ref, proj_ref, vec_ref,
    final_ref, parts_ref, total_ref,
):
    core, section = place_ref[0, 0], place_ref[0, 1]
    half = C // 2
    join_rows(right_own_ref, right_got_ref, taps_ref, core, 2 * rows)
    join_rows(left_own_ref, left_got_ref, proj_ref, core, rows, at=slice(0, D))
    more = slice(D, D + PD + SPARE)
    join_rows(left_own_ref, left_got_ref, parts_ref, core, rows, at=more)
    spread_parts(rows, parts_ref, vec_ref)
    for d in range(C // rows):
        at = slice(d * rows, (d + 1) * rows)
        head, tail = parts_ref[at, :PD], parts_ref[d * rows : d * rows + rows // 2, PD:]
        to = d * (rows + rows // 2)
        final_ref[to : to + rows, :] = head.astype(full)
        final_ref[to + rows : to + rows + rows // 2, :] = tail.astype(full)
    for tap in range(2):
        cols = slice(tap * half, (tap + 1) * half)
        own_taps = taps_ref[pl.ds(pl.multiple_of(tap * C + section * half, half), half), :]
        got_taps = taps_ref[pl.ds(pl.multiple_of(tap * C + (1 - section) * half, half), half), :]
        part = plain_dot(own_ref[:, cols], own_taps) + plain_dot(got_ref[:, cols], got_taps)
        if tap == 0:
            total_ref[...] = part
        else:
            total_ref[...] += part
    for at in row_steps():
        lifted, slope = gelu_and_slope(total_ref[at, :])
        hat, inverse = normalized(lifted)
        slope_ref[at, :] = slope.astype(low)
        hat_ref[at, :] = hat.astype(low)
        inverse_ref[at, :] = inverse
        normed = hat * vector(vec_ref, "ln0_gain") + vector(vec_ref, "ln0_bias")
        normed_ref[at, :] = normed.astype(low)
    for at in row_steps():
        encoded = plain_dot(normed_ref[at, :], proj_ref[...]) + vector(vec_ref, "proj0_bias")
        encoded = jnp.where(masked_ref[at, :] > 0, vector(vec_ref, "mask_emb"), encoded)
        inputs_ref[at, :] = encoded.astype(low)


def first_kernel(
    inputs_ref, mixed_ref, out_ref, vec_ref, first_ref, hat_ref, inverse_ref, total_ref
):
    total_ref[...] = plain_dot(mixed_ref[...], out_ref[:, D:])
    for at in row_steps():
        value = inputs_ref[at, :].astype(full) + total_ref[at, :] + vector(vec_ref, "out_bias")
        hat, inverse = normalized(value)
        hat_ref[at, :] = hat.astype(low)
        inverse_ref[at, :] = inverse
        value = hat * vector(vec_ref, "ln1_gain") + vector(vec_ref, "ln1_bias")
        first_ref[at, :] = value.astype(low)


def first_back_kernel(
    d_pre_ref, up_ref, d_ffn_ref, hat_ref, inverse_ref, out_ref, vec_ref,
    d_attn_ref, d_mixed_ref, g_gain_ref, g_shift_ref, g_out_bias_ref, d_first_ref, held_ref, sems,
):
    part = right_dot(d_pre_ref[...], fetched(up_ref, held_ref, sems))

    @pl.when(pl.program_id(0) == 0)
    def _():
        d_first_ref[...] = d_ffn_ref[...].astype(full) + part

    @pl.when(pl.program_id(0) > 0)
    def _():
        d_first_ref[...] += part

    @pl.when(pl.program_id(0) == pl.num_programs(0) - 1)
    def _():
        g_gain = g_shift = g_out_bias = jnp.zeros((1, D), full)
        for at in row_steps():
            grad = d_first_ref[at, :]
            hat = hat_ref[at, :].astype(full)
            g_gain += column_sum(grad * hat)
            g_shift += column_sum(grad)
            grad = normalize_back(grad * vector(vec_ref, "ln1_gain"), hat, inverse_ref[at, :])
            grad = grad.astype(low)
            d_attn_ref[at, :] = grad
            g_out_bias += column_sum(grad.astype(full))
        g_gain_ref[...] = g_gain
        g_shift_ref[...] = g_shift
        g_out_bias_ref[...] = g_out_bias
        d_mixed_ref[...] = right_dot(d_attn_ref[...], out_ref[:, D:]).astype(low)


def first_backward(d_pre, ffn, d_ffn, hat, inverse, vo, vectors):
    def held(*shape):
        return pl.BlockSpec(shape, lambda i: (0, 0))

    return pl.pallas_call(
        first_back_kernel,
        grid=(FF // D,),
        in_specs=[
            pl.BlockSpec((FMB, D), lambda i: (0, i)),
            pl.BlockSpec(memory_space=pltpu.HBM),
            held(FMB, D),
            held(FMB, D),
            held(FMB, 1),
            held(D, 2 * D),
            held(1, VECTOR_TOTAL),
        ],
        out_specs=[held(FMB, D)] * 2 + [held(1, D)] * 3,
        out_shape=[jax.ShapeDtypeStruct((FMB, D), low)] * 2
        + [jax.ShapeDtypeStruct((1, D), full)] * 3,
        scratch_shapes=[
            pltpu.VMEM((FMB, D), full),
            pltpu.VMEM((FF // D, D, D), low),
            pltpu.SemaphoreType.DMA((FF // D,)),
        ],
        compiler_params=pltpu.CompilerParams(vmem_limit_bytes=28 * 1024 * 1024),
        cost_estimate=pl.CostEstimate(flops=1, bytes_accessed=1, transcendentals=0),
        name="first_backward",
    )(d_pre, ffn, d_ffn, hat, inverse, vo, vectors)


def inputs_back_kernel(
    d_qk_ref, d_values_ref, qk_ref, v_ref, d_attn_ref, masked_ref,
    d_encoded_ref, g_mask_ref, g_proj_bias_ref, g_query_ref, g_value_ref, total_ref,
):
    total_ref[...] = right_dot(d_qk_ref[...], qk_ref[...])
    total_ref[...] += right_dot(d_values_ref[...], v_ref[:, :D])
    g_mask = g_proj_bias = g_query = g_value = jnp.zeros((1, D), full)
    for at in row_steps():
        grad = total_ref[at, :] + d_attn_ref[at, :].astype(full)
        masked = masked_ref[at, :] > 0
        g_mask += column_sum(jnp.where(masked, grad, 0.0))
        grad = jnp.where(masked, 0.0, grad).astype(low)
        d_encoded_ref[at, :] = grad
        g_proj_bias += column_sum(grad.astype(full))
        g_query += column_sum(d_qk_ref[at, :D].astype(full))
        g_value += column_sum(d_values_ref[at, :].astype(full))
    g_mask_ref[...] = g_mask
    g_proj_bias_ref[...] = g_proj_bias
    g_query_ref[...] = g_query
    g_value_ref[...] = g_value


def front_back_kernel(
    d_encoded_ref, proj_ref, hat_ref, slope_ref, inverse_ref, vec_ref,
    d_conv_ref, g_gain_ref, g_shift_ref, total_ref,
):
    total_ref[...] = right_dot(d_encoded_ref[...], proj_ref[...])
    g_gain = g_shift = jnp.zeros((1, C), full)
    for at in row_steps():
        grad = total_ref[at, :]
        hat = hat_ref[at, :].astype(full)
        g_gain += column_sum(grad * hat)
        g_shift += column_sum(grad)
        grad = normalize_back(grad * vector(vec_ref, "ln0_gain"), hat, inverse_ref[at, :])
        d_conv_ref[at, :] = (grad * slope_ref[at, :].astype(full)).astype(low)
    g_gain_ref[...] = g_gain
    g_shift_ref[...] = g_shift


def each_pair(rows, each):
    step = 2 * each if rows % (2 * each) == 0 else each
    return [(slice(r, r + step), slice(2 * r, 2 * r + 2 * step)) for r in range(0, rows, step)]


def join_cores(own_ref, got_ref, whole_ref, core, each, width=512):
    cols = own_ref.shape[1]
    for c in range(0, cols, width):
        at = slice(c, min(c + width, cols))
        for lane, whole in each_pair(own_ref.shape[0], each):
            own, got = own_ref[lane, at].astype(full), got_ref[lane, at].astype(full)
            zero = jnp.where(core == 0, own, got)
            one = jnp.where(core == 0, got, own)
            parts = []
            for r in range(0, own.shape[0], each):
                parts += [zero[r : r + each], one[r : r + each]]
            whole_ref[whole, at] = jnp.concatenate(parts, 0).astype(low)


def split_cores(whole_ref, keep_ref, send_ref, core, each, begin=0, width=384):
    cols = whole_ref.shape[1]
    for c in range(0, cols, width):
        at = slice(c, min(c + width, cols))
        to = slice(begin + at.start, begin + at.stop)
        for lane, whole in each_pair(whole_ref.shape[0] // 2, each):
            zero, one = [], []
            for r in range(whole.start, whole.stop, 2 * each):
                zero.append(whole_ref[r : r + each, at])
                one.append(whole_ref[r + each : r + 2 * each, at])
            zero, one = jnp.concatenate(zero, 0), jnp.concatenate(one, 0)
            keep_ref[lane, to] = jnp.where(core == 0, zero, one).astype(low)
            send_ref[lane, to] = jnp.where(core == 0, one, zero).astype(low)


def qkv_kernel(
    each, inputs_ref, qk_own_ref, qk_got_ref, vo_own_ref, vo_got_ref, vec_ref, core_ref,
    qk_ref, vo_ref, qk_rows_ref, values_ref,
):
    core = core_ref[0, 0]
    join_cores(qk_own_ref, qk_got_ref, qk_ref, core, each)
    join_cores(vo_own_ref, vo_got_ref, vo_ref, core, each)
    bias = vector(vec_ref, "qv_bias")
    rows = plain_dot(inputs_ref[...], qk_ref[:, :D]) + bias[:, :D]
    qk_rows_ref[:, :D] = rows.astype(low)
    qk_rows_ref[:, D:] = plain_dot(inputs_ref[...], qk_ref[:, D:]).astype(low)
    rows = plain_dot(inputs_ref[...], vo_ref[:, :D]) + bias[:, D:]
    values_ref[...] = rows.astype(low)


def lanes_kernel(each, up_ref, up_got_ref, down_ref, down_got_ref, out_ref):
    out_ref[0, 0, 0, :each, :] = added(up_ref[0], up_got_ref[0])
    for j in range(FF // D):
        rows = slice(j * each, (j + 1) * each)
        part = added(down_ref[0, rows, :], down_got_ref[0, rows, :])
        out_ref[0, 0, 0, each:, j * D : (j + 1) * D] = part


def add_lanes(each, depth, up, up_got, down, down_got):
    def where(i):
        return (i // (2 * depth), i % 2, (i // 2) % depth, 0, 0)

    up_rows = pl.BlockSpec((1, each, FF), lambda i: (i, 0, 0))
    down_rows = pl.BlockSpec((1, each * FF // D, D), lambda i: (i, 0, 0))
    up, up_got = [t.reshape(4 * depth, each, FF) for t in (up, up_got)]
    down, down_got = [t.reshape(4 * depth, each * FF // D, D) for t in (down, down_got)]
    return pl.pallas_call(
        functools.partial(lanes_kernel, each),
        grid=(4 * depth,),
        in_specs=[up_rows, up_rows, down_rows, down_rows],
        out_specs=pl.BlockSpec((1, 1, 1, 2 * each, FF), where),
        out_shape=jax.ShapeDtypeStruct((2, 2, depth, 2 * each, FF), low),
        compiler_params=pltpu.CompilerParams(vmem_limit_bytes=8 * 1024 * 1024),
        cost_estimate=pl.CostEstimate(flops=1, bytes_accessed=1, transcendentals=0),
        name="add_lanes",
    )(up, up_got, down, down_got)


def heads_grad_kernel(
    each, inputs_ref, mixed_ref, d_qk_ref, d_values_ref, d_attn_ref, core_ref,
    keep_ref, send_ref, turned_ref, total_ref,
):
    core = core_ref[0, 0]
    turned_ref[...] = inputs_ref[...].T
    for begin, rhs in (
        (0, d_qk_ref[:, :D]),
        (D, d_qk_ref[:, D:]),
        (2 * D, d_values_ref[...]),
        (3 * D, d_attn_ref[...]),
    ):
        if begin == 3 * D:
            turned_ref[...] = mixed_ref[...].T
        total_ref[...] = plain_dot(turned_ref[...], rhs)
        split_cores(total_ref, keep_ref, send_ref, core, each, begin)


def misc_grad_kernel(
    rows, each, normed_ref, d_encoded_ref, second_ref, d_proj_ref, own_ref, got_ref, d_conv_ref,
    vectors_ref, section_ref, terms_ref, final_ref, taps_ref,
):
    section = section_ref[0, 0]
    half = C // 2
    terms_ref[:, :D] = plain_dot(normed_ref[...].T, d_encoded_ref[...]).astype(low)
    final_ref[...] = plain_dot(second_ref[...].T, d_proj_ref[...])
    for d in range(C // rows):
        to = slice(d * rows, d * rows + rows)
        terms_ref[to, D : D + PD] = final_ref[d * each : d * each + rows, :].astype(low)
        last = [final_ref[d * each + rows : (d + 1) * each, :]]
        last.append(vectors_ref[d * (rows // 2) : (d + 1) * (rows // 2), :])
        terms_ref[to, D + PD : D + PD + SPARE] = jnp.concatenate(last, 0).astype(low)
    taps_ref[:C, :] = plain_dot(own_ref[...].T, d_conv_ref[...])
    taps_ref[C:, :] = plain_dot(got_ref[...].T, d_conv_ref[...])
    for tap in range(2):
        for side in range(2):
            for r in range(0, half, 2 * rows):
                at = tap * half + r
                own, got = taps_ref[at : at + 2 * rows, :], taps_ref[C + at : C + at + 2 * rows, :]
                value = jnp.where(section == side, own, got).astype(low)
                d = (tap * C + side * half + r) // (2 * rows)
                begin = D + PD + SPARE
                terms_ref[d * rows : (d + 1) * rows, begin : begin + C] = value[:rows]
                terms_ref[d * rows : (d + 1) * rows, begin + C :] = value[rows:]


def local_kernel(kernel, outs, scratch=(), scalars=0, static=(), far_in=(), far_out=()):
    def call(*args):
        near = len(args) - scalars
        held = [(args[i].shape, args[i].dtype) for i in far_in] + [outs[i] for i in far_out]
        first_held = len(args) + len(outs) + len(scratch)

        def run(*refs):
            refs, held_refs, sems = list(refs[:first_held]), refs[first_held:-2], refs[-2:]
            ins = [
                pltpu.make_async_copy(refs[i], held_refs[k], sems[0].at[k])
                for k, i in enumerate(far_in)
            ]
            ends = [
                pltpu.make_async_copy(
                    held_refs[len(far_in) + k], refs[len(args) + i], sems[1].at[k]
                )
                for k, i in enumerate(far_out)
            ]
            for copy in ins:
                copy.start()
            for copy in ins:
                copy.wait()
            for k, i in enumerate(list(far_in) + [len(args) + i for i in far_out]):
                refs[i] = held_refs[k]
            kernel(*static, *refs)
            for copy in ends:
                copy.start()
            for copy in ends:
                copy.wait()

        def space(index, far):
            return pl.BlockSpec(memory_space=pltpu.HBM if index in far else pltpu.VMEM)

        everything = [(a.shape, a.dtype) for a in args] + list(outs) + list(scratch)
        size = sum(math.prod(shape) * jnp.dtype(dtype).itemsize for shape, dtype in everything)
        return pl.pallas_call(
            run,
            out_shape=[jax.ShapeDtypeStruct(shape, dtype) for shape, dtype in outs],
            in_specs=[space(i, far_in) for i in range(near)]
            + [pl.BlockSpec(memory_space=pltpu.SMEM)] * scalars,
            out_specs=[space(i, far_out) for i in range(len(outs))],
            scratch_shapes=[pltpu.VMEM(shape, dtype) for shape, dtype in list(scratch) + held]
            + [pltpu.SemaphoreType.DMA((max(len(far), 1),)) for far in (far_in, far_out)],
            compiler_params=pltpu.CompilerParams(vmem_limit_bytes=56 * 1024 * 1024 if kernel.__name__ in ('front_kernel',) else size + 4 * 1024 * 1024),
            cost_estimate=pl.CostEstimate(flops=1, bytes_accessed=1, transcendentals=0),
            name=kernel.__name__,
        )(*args)

    return call


def fetched(ffn_ref, held_ref, sems):
    step, width = pl.program_id(0), held_ref.shape[2]

    def copy(k):
        source = ffn_ref.at[0, :, k * width : (k + 1) * width]
        return pltpu.make_async_copy(source, held_ref.at[k], sems.at[k])

    for k in range(held_ref.shape[0]):
        @pl.when(step == 0)
        def _():
            copy(k).start()

    for k in range(held_ref.shape[0]):
        @pl.when(step == k)
        def _():
            copy(k).wait()

    return held_ref[step]


def up_kernel(x_ref, ffn_ref, bias_ref, hidden_ref, slope_ref, pre_ref, held_ref, sems):
    pre_ref[...] = plain_dot(x_ref[...], fetched(ffn_ref, held_ref, sems))
    bias = bias_ref[...]
    for at in row_steps(64):
        value, slope = gelu_and_slope(pre_ref[at, :] + bias)
        hidden_ref[at, :] = value.astype(low)
        slope_ref[at, :] = slope.astype(low)


def up_forward(x, ffn, vectors, tile=1024):
    begin = start_of["up_bias"] // tile
    columns = pl.BlockSpec((FMB, tile), lambda i: (0, i))
    return pl.pallas_call(
        up_kernel,
        grid=(FF // tile,),
        in_specs=[
            pl.BlockSpec((FMB, D), lambda i: (0, 0)),
            pl.BlockSpec(memory_space=pltpu.HBM),
            pl.BlockSpec((1, tile), lambda i: (0, begin + i)),
        ],
        out_specs=[columns, columns],
        out_shape=[jax.ShapeDtypeStruct((FMB, FF), low)] * 2,
        scratch_shapes=[
            pltpu.VMEM((FMB, tile), full),
            pltpu.VMEM((FF // tile, D, tile), low),
            pltpu.SemaphoreType.DMA((FF // tile,)),
        ],
        compiler_params=pltpu.CompilerParams(vmem_limit_bytes=22 * 1024 * 1024),
        cost_estimate=pl.CostEstimate(flops=1, bytes_accessed=1, transcendentals=0),
        name="up_forward",
    )(x, ffn, vectors)


def body(
    features,
    conv_weight,
    ln0_gain,
    ln0_bias,
    proj0_weight,
    proj0_bias,
    mask_emb,
    qkv_weight,
    qv_bias,
    out_weight,
    out_bias,
    ln1_gain,
    ln1_bias,
    up_weight,
    up_bias,
    down_weight,
    down_bias,
    ln2_gain,
    ln2_bias,
    final_weight,
    final_bias,
    codebook,
    lengths,
    mask_pos,
    distractors,
    target_ids,
):
    links = Links()
    section = links.y
    core = links.core.reshape(1, 1).astype(jnp.int32)
    place = jnp.stack([links.core, links.y]).reshape(1, 2).astype(jnp.int32)
    devices = 2 * links.per_section
    rows = C // devices

    own_rows = pick(features, section, 0)
    lens = pick(lengths, section, 0)
    positions = pick(mask_pos, section, 0)
    chosen = pick(distractors, section, 0)
    target_rows = pick(target_ids, section, 0)

    each = D // devices
    slot = (rows // 2) * SPARE // SLOTS
    blocks = FF // D
    down_blocks = down_weight.reshape(blocks, each, D).transpose(1, 0, 2).reshape(each, FF)
    ffn_full = lax.all_gather(jnp.stack([up_weight, down_blocks]), BOTH, axis=1, tiled=True)
    heads = Gather(links, jnp.concatenate([qkv_weight, out_weight], axis=1), 2 * D)
    heads.start_z()
    got_rows = links.over_y(pick(features, 1 - section, 0))
    late = (up_bias, proj0_weight, chosen)
    late = after([heads], *late)
    up_bias, proj0_weight, chosen = late
    heads.start_z_rest()
    vector_parts = [
        up_bias,
        ln0_gain,
        ln0_bias,
        proj0_bias,
        mask_emb,
        qv_bias,
        out_bias,
        ln1_gain,
        ln1_bias,
        down_bias,
        ln2_gain,
        ln2_bias,
        final_bias,
    ]
    vector_parts += [vector_parts[0]] * (SLOTS - len(vector_parts))
    vector_part = jnp.stack([jnp.pad(v, (0, slot - v.shape[0])) for v in vector_parts])
    misc = Gather(
        links,
        jnp.concatenate(
            [
                proj0_weight,
                final_weight[:rows],
                jnp.concatenate([final_weight[rows:], vector_part.reshape(rows // 2, SPARE)], 0),
                conv_weight[:rows],
                conv_weight[rows:],
            ],
            axis=1,
        ),
        D + PD + SPARE,
        parts=2,
    )
    misc.start_z()
    drawn = count_distractors(chosen)
    (drawn,) = after([heads, misc], drawn)

    heads.start_first()
    misc.start_z_rest()
    frame_ids = jnp.arange(FMB, dtype=jnp.int32)
    at_frame = positions[:, None] == frame_ids[None, :]
    is_masked = jnp.any(at_frame, axis=0)
    own_frame = (frame_ids[:, None] == frame_ids[None, :]) & is_masked[:, None]
    counts = lax.dot_general(
        at_frame.astype(low), drawn, (((0,), (1,)), ((), ())), preferred_element_type=full
    ) + own_frame.astype(full)
    entries = jnp.arange(codebook.shape[1], dtype=jnp.int32)
    targets = jnp.concatenate(
        [
            plain_dot((target_rows[0][:, None] == entries[None, :]).astype(low), codebook[0]),
            plain_dot((target_rows[1][:, None] == entries[None, :]).astype(low), codebook[1]),
        ],
        axis=1,
    )
    targets = targets * lax.rsqrt(jnp.sum(targets * targets, axis=1, keepdims=True) + unit_eps)
    stops = jnp.cumsum(lens)
    segment = jnp.sum(
        (frame_ids[:, None] >= stops[None, : UTTS - 1]).astype(jnp.int32), axis=1
    )
    masked = is_masked[:, None].astype(full)
    own_pairs = own_rows.reshape(FMB, C)
    counts, targets, got_rows, own_pairs, segment = after(
        [heads, misc], counts, targets, got_rows, own_pairs, segment
    )

    heads.start_second()
    misc.start_first()
    got_pairs = got_rows.reshape(FMB, C)
    (got_pairs,) = after([heads, misc], got_pairs)

    misc.start_second()
    heads.start_core()
    misc.start_core()
    half = C // 2
    (
        inputs, normed, hat_zero, conv_slope, inverse_zero, conv_full, proj_full, vectors, final_full
    ) = local_kernel(
        front_kernel,
        [
            ((FMB, D), low),
            ((FMB, C), low),
            ((FMB, C), low),
            ((FMB, C), low),
            ((FMB, 1), full),
            ((2 * C, C), low),
            ((C, D), low),
            ((1, VECTOR_TOTAL), full),
            ((D, PD), full),
        ],
        [((C, PD + SPARE), low), ((FMB, C), full)],
        scalars=1,
        static=(rows,),
        far_in=(0, 1),
        far_out=(1, 2, 3, 4, 5, 6, 8),
    )(own_pairs, got_pairs, *misc.apart(), masked, place)
    taps = conv_full.reshape(2, 2, half, C)
    own_taps = pick(taps, section, 1).reshape(C, C)
    got_taps = pick(taps, 1 - section, 1).reshape(C, C)
    qk_full, vo_full, qk_rows, value_rows = local_kernel(
        qkv_kernel,
        [((D, 2 * D), low), ((D, 2 * D), low), ((FMB, 2 * D), low), ((FMB, D), low)],
        scalars=1,
        static=(each,),
        far_out=(0,),
    )(inputs, *heads.apart(), vectors, core)
    mixed, logs = attention_forward(qk_rows, value_rows, segment)
    first_low, hat_one, inverse_one = local_kernel(
        first_kernel, [((FMB, D), low), ((FMB, D), low), ((FMB, 1), full)], [((FMB, D), full)],
        far_out=(1, 2),
    )(inputs, mixed, vo_full, vectors)
    hidden_low, slope = up_forward(first_low, ffn_full, vectors)
    grad = {}
    (
        second_low,
        d_proj_low,
        d_ffn_low,
        d_pre_low,
        loss,
        grad["down_bias"],
        grad["ln2_gain"],
        grad["ln2_bias"],
        grad["final_bias"],
        grad["up_bias"],
    ) = middle(
        each,
        hidden_low,
        slope,
        ffn_full,
        first_low,
        final_full,
        *[
            vectors[:, start_of[name] : start_of[name] + size]
            for name, size in VECTORS
            if name in ("down_bias", "ln2_gain", "ln2_bias", "final_bias")
        ],
        targets,
        counts,
        masked,
    )

    loss = jnp.where(jnp.arange(2) == section, loss[0], 0.0)
    loss_got = links.over_y(loss)
    g_down = left_dot(hidden_low, d_ffn_low).astype(low)
    down = Sum(links, *by_core(links, g_down), D // 2)
    down.start_core()
    g_up = left_dot(first_low, d_pre_low).astype(low)
    up = Sum(links, *by_core(links, g_up), FF // 2)
    up.start_core()
    d_attn_low, d_mixed, grad["ln1_gain"], grad["ln1_bias"], grad["out_bias"] = (
        first_backward(d_pre_low, ffn_full, d_ffn_low, hat_one, inverse_one, vo_full, vectors)
    )
    d_mixed, d_attn_low, loss_got = after([down, up], d_mixed, d_attn_low, loss_got)

    lanes = add_lanes(
        each, links.depth, up.keep.reshape(-1, FF), up.got[0], down.keep.reshape(-1, D), down.got[0]
    )
    line = lax.psum_scatter(
        lanes.reshape(-1, FF), ("section", "x"), scatter_dimension=0, tiled=True
    ).reshape(links.depth, 2 * each, FF)
    d_qk, d_values = attention_backward(qk_rows, value_rows, segment, d_mixed, logs)
    keep, send = local_kernel(
        heads_grad_kernel,
        [((D // 2, 4 * D), low)] * 2,
        [((D, FMB), low), ((D, D), full)],
        scalars=1,
        static=(each,),
        far_in=(0, 1),
    )(inputs, mixed, d_qk, d_values, d_attn_low, core)

    heads = Sum(links, keep, send, 2 * D)
    heads.start_core()
    d_encoded, grad["mask_emb"], grad["proj0_bias"], g_query, g_value = local_kernel(
        inputs_back_kernel, [((FMB, D), low)] + [((1, D), full)] * 4, [((FMB, D), full)], far_in=(2, 3)
    )(d_qk, d_values, qk_full, vo_full, d_attn_low, masked)
    grad["qv_bias"] = jnp.concatenate([g_query, g_value], axis=1)
    (d_encoded,) = after([heads], d_encoded)

    heads.start_first()
    d_conv_low, grad["ln0_gain"], grad["ln0_bias"] = local_kernel(
        front_back_kernel,
        [((FMB, C), low), ((1, C), full), ((1, C), full)],
        [((FMB, C), full)],
        far_in=(1, 2, 3, 4),
    )(d_encoded, proj_full, hat_zero, conv_slope, inverse_zero, vectors)
    g_vectors = split_vectors([grad[name] for name, _ in VECTORS], devices, slot)
    g_vectors = g_vectors.transpose(1, 0, 2).reshape(devices * (rows // 2), SPARE)
    (terms,) = local_kernel(
        misc_grad_kernel,
        [((C, D + PD + SPARE + 2 * C), low)],
        [((D, PD), full), ((2 * C, C), full)],
        scalars=1,
        static=(rows, each),
        far_in=(0, 2, 3, 4, 5),
    )(
        normed, d_encoded, second_low, d_proj_low, own_pairs, got_pairs, d_conv_low, g_vectors,
        section.reshape(1, 1).astype(jnp.int32),
    )
    misc = Sum(links, *by_core(links, terms), D + PD + SPARE)
    misc.start_core()
    got_d = right_dot(d_conv_low, got_taps).astype(low).reshape(2 * FMB, half)
    own_d = right_dot(d_conv_low, own_taps).reshape(2 * FMB, half)
    own_d, got_d, line = after([misc, heads], own_d, got_d, line)

    heads.start_second()
    misc.start_first()
    ffn = Line(links, line)
    ffn.start_z()
    (got_d,) = after([heads, misc], got_d)
    got_d = links.over_y(got_d)

    heads.start_z()
    misc.start_second()
    ffn.start_z_rest()
    after([heads, misc])

    heads.start_z_rest()
    misc.start_z()
    after([misc])
    misc.start_z_rest()
    features_grad = in_order(section, own_d, got_d.astype(full), -2)
    loss_each = loss + loss_got
    ffn_sum, heads_sum, misc_sum = ffn.total(), heads.total(), misc.total()
    up_sum = ffn_sum[:each]
    down_sum = jnp.concatenate(jnp.split(ffn_sum[each:], blocks, axis=1), axis=0)
    qkv_sum, out_sum = heads_sum[:, : 3 * D], heads_sum[:, 3 * D :]
    proj_sum = misc_sum[:, :D]
    left, right = misc_sum[:, D : D + PD + SPARE], misc_sum[:, D + PD + SPARE :]
    conv_sum = jnp.concatenate([right[:, :C], right[:, C:]], axis=0)
    final_sum = jnp.concatenate([left[:, :PD], left[: rows // 2, PD:]], axis=0)
    vector_sum = left[rows // 2 :, PD:].reshape(SLOTS, slot)
    share = {}
    for index, (name, size) in enumerate(VECTORS):
        share[name] = vector_sum[index, : size // devices]
    return (
        loss_each,
        features_grad,
        conv_sum,
        share["ln0_gain"],
        share["ln0_bias"],
        proj_sum,
        share["proj0_bias"],
        share["mask_emb"],
        qkv_sum,
        share["qv_bias"],
        out_sum,
        share["out_bias"],
        share["ln1_gain"],
        share["ln1_bias"],
        up_sum,
        share["up_bias"],
        down_sum,
        share["down_bias"],
        share["ln2_gain"],
        share["ln2_bias"],
        final_sum,
        share["final_bias"],
    )


def solution(mesh):
    grid = mesh.devices.reshape(2, -1, 2, 2)
    rows = P(BOTH, None)
    part = P(BOTH)
    weights = (rows, part, part, rows, part, part, rows, part, rows, part, part, part)
    weights += (rows, part, rows, part, part, part, rows, part)
    batch = [P(SPLIT, *[None] * more) for more in (1, 1, 2, 2)]
    return jax.shard_map(
        body,
        mesh=jax.sharding.Mesh(grid, BOTH),
        in_specs=(P(SPLIT, None, "section"),) + weights + (P(), *batch),
        out_specs=(P(SPLIT), P(SPLIT, None, "section")) + weights,
        check_vma=False,
    )
```

```python
import functools
import math

import jax
import jax.numpy as jnp
from jax import lax
from jax.experimental import pallas as pl
from jax.experimental.pallas import tpu as pltpu
from jax.sharding import PartitionSpec as P

D = 768
H = 12
HD = 64
FF = 3072
C = 512
PD = 256
UTTS = 3
PAIR = 2 * HD
FMB = 512
NEG = 100
NMASK = 256
SPARE = 256
SLOTS = 16

SPLIT = ("z", "x", "core")
BOTH = ("section",) + SPLIT
norm_eps = 1e-05
unit_eps = 1e-06
sharpness = 10.0
masked_score = -1000000000.0
precise = lax.Precision.HIGHEST
low = jnp.bfloat16
full = jnp.float32

VECTORS = (
    ("up_bias", FF),
    ("ln0_gain", C),
    ("ln0_bias", C),
    ("proj0_bias", D),
    ("mask_emb", D),
    ("qv_bias", 2 * D),
    ("out_bias", D),
    ("ln1_gain", D),
    ("ln1_bias", D),
    ("down_bias", D),
    ("ln2_gain", D),
    ("ln2_bias", D),
    ("final_bias", PD),
)
VECTOR_TOTAL = sum(size for _, size in VECTORS)
start_of = {name: sum(size for _, size in VECTORS[:i]) for i, (name, _) in enumerate(VECTORS)}
QV_START = start_of["qv_bias"]


def plain_dot(left_side, right_side):
    return jnp.dot(left_side, right_side, preferred_element_type=full)


def left_dot(left_side, right_side):
    return lax.dot_general(
        left_side, right_side, (((0,), (0,)), ((), ())), preferred_element_type=full
    )


def right_dot(left_side, right_side):
    return lax.dot_general(
        left_side, right_side, (((1,), (1,)), ((), ())), preferred_element_type=full
    )


def gelu_and_slope(x):
    size = jnp.abs(x)
    bell = jnp.exp(-0.5 * x * x)
    t = 1.0 / (1.0 + 0.23164189 * size)
    poly = t * (0.127414796 + t * (-0.142248368 + t * (0.7107068705 + t * (-0.7265760135 + t * 0.5307027145))))
    tail = poly * bell
    below = jnp.where(x >= 0, 1.0 - tail, tail)
    return x * below, below + x * (0.3989422804 * bell)


class Links:
    def __init__(self):
        self.depth = lax.axis_size("z")
        self.per_section = 4 * self.depth
        self.core = lax.axis_index("core")
        self.x = lax.axis_index("x")
        self.z = lax.axis_index("z")
        self.y = lax.axis_index("section")
        self.sizes, self.upper = [], []
        size, place = self.depth, self.z
        while size > 1:
            self.sizes.append(size)
            self.upper.append((place >= size // 2).astype(jnp.int32))
            place = jnp.where(place >= size // 2, size - 1 - place, place)
            size //= 2

    def move(self, value, where):
        pairs = []
        for y in range(2):
            for z in range(self.depth):
                for x in range(2):
                    for core in range(2):
                        ty, tz, tx, tcore = where(y, z, x, core)
                        pairs.append(
                            (
                                y * self.per_section + z * 4 + x * 2 + core,
                                ty * self.per_section + tz * 4 + tx * 2 + tcore,
                            )
                        )
        return lax.ppermute(value, BOTH, pairs)

    def over_x(self, value):
        return self.move(value, lambda y, z, x, core: (y, z, 1 - x, core))

    def over_y(self, value):
        return self.move(value, lambda y, z, x, core: (1 - y, z, x, core))

    def over_core(self, value):
        return self.move(value, lambda y, z, x, core: (y, z, x, 1 - core))

    def over_both(self, value):
        return self.move(value, lambda y, z, x, core: (1 - y, z, 1 - x, core))

    def along_z(self, value, steps):
        return self.move(value, lambda y, z, x, core: (y, (z + steps) % self.depth, x, core))

    def over_z(self, value, size):
        def where(y, z, x, core):
            return (y, z - z % size + size - 1 - z % size, x, core)

        return self.move(value, where)


def pick(value, index, axis):
    axis = axis % value.ndim
    return lax.squeeze(lax.dynamic_slice_in_dim(value, index, 1, axis), (axis,))


def in_order(index, own, got, axis):
    axis = axis % own.ndim
    own, got = jnp.expand_dims(own, axis), jnp.expand_dims(got, axis)
    shape = own.shape[:axis] + (2,) + own.shape[axis + 1 :]
    return jnp.where(lax.broadcasted_iota(jnp.int32, shape, axis) == index, own, got)


def in_line(uppers, own, got):
    shape = (own.shape[0], 2) + own.shape[1:]
    turn = (
        lax.broadcasted_iota(jnp.int32, shape, 0) + lax.broadcasted_iota(jnp.int32, shape, 1)
    ) % 2
    line = jnp.where(turn == uppers[-1], jnp.expand_dims(own, 1), jnp.expand_dims(got, 1))
    line = line.reshape((-1,) + own.shape[1:])
    for _ in range(2, len(uppers)):
        line = jnp.concatenate([line[:, 0], jnp.flip(line[:, 1], 0)], axis=0)
    return line


class Gather:
    def __init__(self, links, line, cut, parts=1):
        self.links, self.line, self.cut, self.parts = links, line, cut, parts
        self.got = []

    def start_z(self):
        self.got = [self.links.over_z(self.line, self.links.sizes[0])]

    def start_z_rest(self):
        links = self.links
        for step in range(1, len(links.sizes)):
            self.line = in_order(links.upper[step - 1], self.line, self.got[0], 0)
            self.got = [links.over_z(self.line, links.sizes[step])]

    def start_first(self):
        links = self.links
        line = in_line(links.upper, self.line, self.got[0])
        self.first, self.second = line[..., : self.cut], line[..., self.cut :]
        if self.parts > 1:
            shape = self.second.shape
            self.second = self.second.reshape(shape[:2] + (self.parts, -1)).swapaxes(1, 2)
            self.second = self.second.reshape(shape[0], -1, shape[2] // self.parts)
        self.got = [links.over_x(self.first), links.over_y(self.second)]

    def start_second(self):
        links = self.links
        self.first = in_order(links.x, self.first, self.got[0], -2)
        self.second = in_order(links.y, self.second, self.got[1], -3)
        self.got = [links.over_y(self.first), links.over_x(self.second)]

    def start_core(self):
        links = self.links
        self.lanes = [
            in_order(links.y, self.first, self.got[0], -4),
            in_order(links.x, self.second, self.got[1], -2),
        ]
        self.lanes = lax.optimization_barrier(self.lanes)
        self.got = [links.over_core(lane) for lane in self.lanes]

    def whole(self):
        core = self.links.core
        return [
            in_order(core, own, got, -2).reshape(-1, own.shape[-1])
            for own, got in zip(self.lanes, self.got)
        ]

    def apart(self):
        lanes = [x for pair in zip(self.lanes, self.got) for x in pair]
        return [x.reshape(-1, x.shape[-1]) for x in lanes]


class Line:
    def __init__(self, links, line):
        self.links, self.line = links, line

    def start_z(self):
        self.start_line(self.line)

    def start_line(self, line):
        links = self.links
        for size in links.sizes[:-1]:
            line = jnp.stack([line[: size // 2], jnp.flip(line[size // 2 :], 0)], axis=1)
        self.line = line
        self.got = [links.over_z(pick(line, 1 - links.upper[-1], 0), links.sizes[-1])]

    def start_z_rest(self):
        links = self.links
        for step in range(len(links.sizes) - 2, -1, -1):
            self.line = added(pick(self.line, links.upper[step + 1], 0), self.got[0])
            away = pick(self.line, 1 - links.upper[step], 0)
            self.got = [links.over_z(away, links.sizes[step])]

    def total(self):
        return pick(self.line, self.links.upper[0], 0).astype(full) + self.got[0].astype(full)


class Sum(Line):
    def __init__(self, links, keep, send, cut):
        self.links, self.cut = links, cut
        self.grid = (2, links.depth, 2, -1, keep.shape[-1])
        self.keep, self.send = keep.reshape(self.grid), send
        self.got = []

    def start_core(self):
        self.got = [self.links.over_core(self.send)]

    def start_first(self):
        links = self.links
        lane = added(self.keep, self.got[0].reshape(self.grid))
        self.first, self.second = lane[..., : self.cut], lane[..., self.cut :]
        self.got = [
            links.over_x(pick(self.first, 1 - links.x, -3)),
            links.over_y(pick(self.second, 1 - links.y, -5)),
        ]

    def start_plane(self):
        links = self.links
        lane = added(self.keep, self.got[0].reshape(self.grid))

        def part(y, x):
            return pick(pick(lane, x, -3), y, 0)

        self.line = part(links.y, links.x)
        self.got = [
            links.over_x(part(links.y, 1 - links.x)),
            links.over_y(part(1 - links.y, links.x)),
            links.over_both(part(1 - links.y, 1 - links.x)),
        ]

    def line_of(self):
        links = self.links
        if len(self.got) == 3:
            return total_of(self.line, self.got).astype(low)
        first = added(pick(self.first, links.y, -4), self.got[0])
        second = added(pick(self.second, links.x, -3), self.got[1])
        return jnp.concatenate([first, second], -1)

    def start_straight_z(self):
        links, line = self.links, self.line_of()
        self.line = pick(line, links.z, 0)
        self.got = [
            links.along_z(pick(line, (links.z + k) % links.depth, 0), k)
            for k in range(1, links.depth)
        ]

    def straight_total(self):
        return total_of(self.line, self.got)

    def start_second(self):
        links = self.links
        self.first = added(pick(self.first, links.x, -3), self.got[0])
        self.second = added(pick(self.second, links.y, -5), self.got[1])
        self.got = [
            links.over_y(pick(self.first, 1 - links.y, -4)),
            links.over_x(pick(self.second, 1 - links.x, -3)),
        ]

    def start_z(self):
        self.start_line(self.line_of())


def by_core(links, terms):
    lanes = terms.reshape(links.per_section, 2, -1, terms.shape[-1])
    return [
        pick(lanes, core, 1).reshape(-1, terms.shape[-1]) for core in (links.core, 1 - links.core)
    ]


def total_of(own, others):
    out = own.astype(full)
    for got in others:
        out = out + got.astype(full)
    return out


def added(own, got):
    return (own.astype(full) + got.astype(full)).astype(low)


def after(moves, *values):
    bound = lax.optimization_barrier((tuple(tuple(m.got) for m in moves), values))
    for move, got in zip(moves, bound[0]):
        move.got = list(got)
    return bound[1]


def owner_of(columns, part):
    factor = -(-(1 << 20) // part)
    assert all((n * factor) >> 20 == n // part for n in range(columns))
    lane = lax.broadcasted_iota(jnp.int32, (1, columns), 1)
    return lax.shift_right_logical(lane * factor, 20)


def spread_parts(rows, parts_ref, out_ref):
    start = 0
    devices = C // rows
    slot = (rows // 2) * SPARE // SLOTS
    each_row = SPARE // slot
    shape = (devices, C)
    across = lax.broadcasted_iota(jnp.int32, shape, 1)
    first = lax.broadcasted_iota(jnp.int32, shape, 0) * rows + rows // 2
    held = [
        plain_dot(jnp.where(across == first + k, 1.0, 0.0).astype(low), parts_ref[:, PD:]).astype(low)
        for k in range(rows // 2)
    ]
    for index, (_, size) in enumerate(VECTORS):
        part = size // devices
        owner = owner_of(size, part)
        place = lax.broadcasted_iota(jnp.int32, (1, size), 1) - owner * part
        lanes = jnp.where(lax.broadcasted_iota(jnp.int32, (slot, size), 0) == place, 1.0, 0.0)
        at = lax.broadcasted_iota(jnp.int32, (devices, size), 0) == owner
        begin = (index % each_row) * slot
        mine = held[index // each_row][:, begin : begin + slot]
        out_ref[:, start : start + size] = jnp.sum(
            jnp.where(at, plain_dot(mine, lanes.astype(low)), 0.0), axis=0, keepdims=True
        )
        start += size


def split_kernel(devices, *refs):
    out_ref = refs[-1]
    slot = out_ref.shape[2]
    for index, (_, size) in enumerate(VECTORS):
        part = size // devices
        owner = owner_of(size, part)
        place = lax.broadcasted_iota(jnp.int32, (1, size), 1) - owner * part
        lanes = jnp.where(lax.broadcasted_iota(jnp.int32, (slot, size), 0) == place, 1.0, 0.0)
        lanes = lanes.astype(low)
        rows = lax.broadcasted_iota(jnp.int32, (devices, size), 0) == owner
        values = refs[index][...]
        high = values.astype(low)
        rest = (values - high.astype(full)).astype(low)
        out_ref[index] = right_dot(
            jnp.where(rows, high.astype(full), 0.0).astype(low), lanes
        ) + right_dot(jnp.where(rows, rest.astype(full), 0.0).astype(low), lanes)
    for index in range(len(VECTORS), SLOTS):
        out_ref[index] = jnp.zeros((devices, slot), full)


def split_vectors(vectors, devices, slot):
    return pl.pallas_call(
        functools.partial(split_kernel, devices),
        out_shape=jax.ShapeDtypeStruct((SLOTS, devices, slot), full),
        compiler_params=pltpu.CompilerParams(vmem_limit_bytes=8 * 1024 * 1024),
        name="split_vectors",
    )(*vectors)


def count_kernel(chosen_ref, count_ref):
    rows = 64
    for block in range(FMB // rows):
        frames = block * rows + lax.broadcasted_iota(jnp.int32, (rows, NMASK), 0)

        def add_one(j, seen):
            return seen + jnp.where(frames == chosen_ref[pl.ds(j, 1), :], 1.0, 0.0)

        seen = lax.fori_loop(0, NEG, add_one, jnp.zeros((rows, NMASK), full), unroll=10)
        count_ref[pl.ds(block * rows, rows), :] = seen.astype(low)


def count_distractors(chosen):
    return pl.pallas_call(
        count_kernel,
        out_shape=jax.ShapeDtypeStruct((FMB, NMASK), low),
        in_specs=[pl.BlockSpec(memory_space=pltpu.VMEM)],
        out_specs=pl.BlockSpec(memory_space=pltpu.VMEM),
        cost_estimate=pl.CostEstimate(flops=1, bytes_accessed=1, transcendentals=0),
    )(chosen.T)


def head_lanes(rows, which):
    lane = lax.broadcasted_iota(jnp.int32, (rows, PAIR), 1)
    return (lane < HD) if which == 0 else (lane >= HD)
def fill_mask(row_ref, col_ref, mask_ref):
    mask_ref[...] = jnp.where(col_ref[...] == row_ref[...], 0.0, masked_score)
def spare_lanes(which):
    lane = lax.broadcasted_iota(jnp.int32, (FMB, PAIR), 1)
    return lane - HD if which == 0 else jnp.where(lane >= HD, -1, lane)


def lane_value(spare, columns):
    value = jnp.zeros((FMB, PAIR), full)
    for place, column in columns:
        value = jnp.where(spare == place, column, value)
    return value


def score_sides(q_ref, k_ref, col_ref, which):
    spare = spare_lanes(which)
    segment = col_ref[...]
    same = [(u, jnp.where(segment == u, 1.0, 0.0)) for u in range(UTTS)]
    keys = [(u, 1.0 - value) for u, value in same]
    queries = [(u, masked_score * value) for u, value in same]
    scaled = q_ref[...] * jnp.asarray(1.0 / math.sqrt(HD), low)
    keys = jnp.where(spare < 0, k_ref[...], lane_value(spare, keys).astype(low))
    queries = jnp.where(spare < 0, scaled, lane_value(spare, queries).astype(low))
    return keys, queries


def attention_kernel(col_ref, q_ref, k_ref, v_ref, mixed_ref, log_ref):
    parts, logs = [], []
    for which in range(2):
        keys, queries = score_sides(q_ref, k_ref, col_ref, which)
        scores = right_dot(queries, keys)
        top = jnp.max(scores, axis=1, keepdims=True)
        shares = jnp.exp(scores - top)
        total = jnp.sum(shares, axis=1, keepdims=True)
        parts.append(plain_dot(shares.astype(low), v_ref[...]) * (1.0 / total))
        logs.append(top + jnp.log(total))
    mixed_ref[...] = jnp.where(spare_lanes(0) < 0, parts[0], parts[1]).astype(low)
    log_ref[0] = jnp.concatenate(logs + [jnp.zeros((FMB, 6), full)], 1).T


def attention_forward(qk, values, seg):
    pairs = H // 2

    def spec(first):
        return pl.BlockSpec((FMB, PAIR), lambda i: (0, i + first))

    return pl.pallas_call(
        attention_kernel,
        grid=(pairs,),
        in_specs=[pl.BlockSpec((FMB, 1), lambda i: (0, 0)), spec(0), spec(pairs), spec(0)],
        out_specs=[spec(0), pl.BlockSpec((1, 8, FMB), lambda i: (i, 0, 0))],
        out_shape=[
            jax.ShapeDtypeStruct((FMB, D), low),
            jax.ShapeDtypeStruct((pairs, 8, FMB), full),
        ],
        compiler_params=pltpu.CompilerParams(vmem_limit_bytes=14 * 1024 * 1024),
        cost_estimate=pl.CostEstimate(flops=1, bytes_accessed=1, transcendentals=0),
        name="attention_forward",
    )(seg.reshape(FMB, 1), qk, qk, values)


def attention_back_kernel(row_ref, col_ref, q_ref, k_ref, v_ref, dm_ref, log_ref, out_ref, d_values_ref, mask_ref):
    i = pl.program_id(0)
    @pl.when(i == 0)
    def _():
        fill_mask(row_ref, col_ref, mask_ref)
    queries = q_ref[...] * jnp.asarray(1.0/math.sqrt(HD), low)
    d_mixed = dm_ref[...]
    keys_t = (k_ref[...] * jnp.asarray(1.0/math.sqrt(HD), low)).T
    d_keys = d_values = None
    d_queries = []
    for which in range(2):
        lanes = head_lanes(FMB, which)
        keys = jnp.where(lanes, k_ref[...], 0).astype(low)
        values = jnp.where(lanes, v_ref[...], 0).astype(low)
        shares = jnp.exp(right_dot(keys, queries) + mask_ref[...] - log_ref[0, which:which+1, :])
        d_shares = right_dot(values, d_mixed)
        inner = jnp.sum(shares * d_shares, axis=0, keepdims=True)
        d_scores = (shares * (d_shares - inner)).astype(low)
        dv = plain_dot(shares.astype(low), d_mixed)
        dk = plain_dot(d_scores, queries)
        d_queries.append(plain_dot(keys_t[which*HD:(which+1)*HD], d_scores))
        if which == 0:
            d_values, d_keys = dv, dk
        else:
            d_values, d_keys = jnp.where(lanes, dv, d_values), jnp.where(lanes, dk, d_keys)
    out_ref[:, pl.ds(pl.multiple_of(i*PAIR, PAIR), PAIR)] = jnp.concatenate(d_queries, 0).T.astype(low)
    out_ref[:, pl.ds(pl.multiple_of(D + i*PAIR, PAIR), PAIR)] = d_keys.astype(low)
    d_values_ref[...] = d_values.astype(low)
def attention_backward(qk, values, seg, d_mixed, logs):
    pairs = H//2
    spec = lambda off: pl.BlockSpec((FMB, PAIR), lambda i: (0, i+off))
    return pl.pallas_call(attention_back_kernel, grid=(pairs,),
        in_specs=[pl.BlockSpec((1,FMB), lambda i:(0,0)), pl.BlockSpec((FMB,1), lambda i:(0,0)), spec(0), spec(pairs), spec(0), spec(0), pl.BlockSpec((1,8,FMB), lambda i:(i,0,0))],
        out_specs=[pl.BlockSpec((FMB,2*D), lambda i:(0,0)), spec(0)],
        out_shape=[jax.ShapeDtypeStruct((FMB,2*D),low), jax.ShapeDtypeStruct((FMB,D),low)],
        scratch_shapes=[pltpu.VMEM((FMB,FMB),full)],
        compiler_params=pltpu.CompilerParams(vmem_limit_bytes=56 * 1024 * 1024),
        cost_estimate=pl.CostEstimate(flops=1, bytes_accessed=1, transcendentals=0),
        name="attention_backward")(seg.reshape(1,FMB), seg.reshape(FMB,1), qk, qk, values, d_mixed, logs)


def column_sum(value):
    return jnp.sum(value, axis=0, keepdims=True)
def three_dots(dot, left, right):
    left_high, right_high = left.astype(low), right.astype(low)
    left_rest = (left - left_high.astype(full)).astype(low)
    right_rest = (right - right_high.astype(full)).astype(low)
    return (
        dot(left_high, right_high) + dot(left_high, right_rest) + dot(left_rest, right_high)
    )


def middle_kernel(each, hidden_ref, slope_ref, blocks_ref, first_ref, final_ref, down_bias_ref, gain_ref, shift_ref, final_bias_ref,
                  targets_ref, counts_ref, masked_ref,
                  second_ref, d_proj_ref, d_ffn_ref, d_pre_ref, loss_ref, g_down_bias_ref, g_gain_ref, g_shift_ref, g_final_bias_ref, g_up_bias_ref,
                  res_ref, inv_ref, proj_ref, down_ref, d_second_ref, held_ref, sem):
    rows = 128
    steps = FMB // rows
    blocks = FF // D
    copy = pltpu.make_async_copy(blocks_ref.at[1], held_ref, sem)
    copy.start()
    copy.wait()
    for r in range(0, D, 2 * each):
        pair = [held_ref[r : r + 2 * each, j * D : (j + 1) * D].astype(full) for j in range(blocks)]
        for k in range(2):
            part = jnp.concatenate([p[k * each : (k + 1) * each] for p in pair], 0).astype(low)
            begin = (r + k * each) * blocks
            down_ref[begin : begin + blocks * each, :] = part
    res_ref[...] = plain_dot(hidden_ref[...], down_ref[...])
    for r in range(steps):
        at = slice(r*rows, (r+1)*rows)
        value = first_ref[at, :].astype(full) + res_ref[at, :] + down_bias_ref[...]
        center = value - jnp.mean(value, axis=1, keepdims=True)
        inverse = lax.rsqrt(jnp.mean(center*center, axis=1, keepdims=True) + norm_eps)
        hat = center * inverse
        res_ref[at, :] = hat
        inv_ref[at, :] = inverse
        second_ref[at, :] = (hat * gain_ref[...] + shift_ref[...]).astype(low)
    proj_ref[...] = plain_dot(second_ref[...], final_ref[...].astype(low)) + final_bias_ref[...]
    loss = jnp.zeros((1, 1), full)
    g_final_bias = jnp.zeros((1, PD), full)
    for r in range(steps):
        at = slice(r*rows, (r+1)*rows)
        value = proj_ref[at, :]
        inverse = lax.rsqrt(jnp.sum(value*value, axis=1, keepdims=True) + unit_eps)
        unit = value * inverse
        agreement = sharpness * three_dots(right_dot, unit, targets_ref[...])
        counts = counts_ref[at, :]
        masked = masked_ref[at, :] > 0
        drawn = counts > 0
        own = (lax.broadcasted_iota(jnp.int32, (rows, FMB), 0) + r*rows) == lax.broadcasted_iota(jnp.int32, (rows, FMB), 1)
        highest = jnp.max(jnp.where(drawn, agreement, masked_score), axis=1, keepdims=True)
        weights = counts * jnp.exp(jnp.where(drawn, agreement - highest, 0.0))
        total = jnp.where(masked, jnp.sum(weights, axis=1, keepdims=True), 1.0)
        own_score = jnp.sum(jnp.where(own, agreement, 0.0), axis=1, keepdims=True)
        loss += column_sum(jnp.where(masked, highest + jnp.log(total) - own_score, 0.0))
        d_agreement = jnp.where(masked, weights * (1.0 / total) - jnp.where(own, 1.0, 0.0), 0.0) * (sharpness / NMASK)
        d_unit = three_dots(plain_dot, d_agreement, targets_ref[...])
        d_proj = (inverse * (d_unit - unit * jnp.sum(d_unit*unit, axis=1, keepdims=True))).astype(low)
        d_proj_ref[at, :] = d_proj
        g_final_bias += column_sum(d_proj.astype(full))
    loss_ref[...] = loss * (1.0 / NMASK)
    g_final_bias_ref[...] = g_final_bias
    d_second_ref[...] = right_dot(d_proj_ref[...], final_ref[...].astype(low))
    g_gain = g_shift = g_down_bias = jnp.zeros((1, D), full)
    for r in range(steps):
        at = slice(r*rows, (r+1)*rows)
        grad = d_second_ref[at, :]
        hat = res_ref[at, :]
        g_gain += column_sum(grad * hat)
        g_shift += column_sum(grad)
        grad = grad * gain_ref[...]
        grad = inv_ref[at, :] * (grad - jnp.mean(grad, axis=1, keepdims=True) - hat * jnp.mean(grad*hat, axis=1, keepdims=True))
        d_ffn_ref[at, :] = grad.astype(low)
        g_down_bias += column_sum(grad.astype(low).astype(full))
    g_gain_ref[...] = g_gain
    g_shift_ref[...] = g_shift
    g_down_bias_ref[...] = g_down_bias
    for j in range(blocks):
        part = right_dot(d_ffn_ref[...], down_ref[j*D:(j+1)*D, :]) * slope_ref[:, j*D:(j+1)*D].astype(full)
        part = part.astype(low)
        d_pre_ref[:, j*D:(j+1)*D] = part
        g_up_bias_ref[:, j*D:(j+1)*D] = column_sum(part.astype(full))
def middle(each, hidden, slope, down, first_low, final, down_bias, gain, shift, final_bias, targets, counts, masked):
    def out(shape, dtype): return jax.ShapeDtypeStruct(shape, dtype)
    return pl.pallas_call(functools.partial(middle_kernel, each),
        grid=(1,),
        in_specs=[pl.BlockSpec(memory_space=pltpu.VMEM)] * 2 + [pl.BlockSpec(memory_space=pltpu.HBM)] + [pl.BlockSpec(memory_space=pltpu.VMEM)] * 9,
        out_specs=[pl.BlockSpec(memory_space=pltpu.VMEM)] * 10,
        out_shape=[out((FMB,D),low), out((FMB,PD),low), out((FMB,D),low), out((FMB,FF),low), out((1,1),full),
                   out((1,D),full), out((1,D),full), out((1,D),full), out((1,PD),full), out((1,FF),full)],
        scratch_shapes=[pltpu.VMEM((FMB,D),full), pltpu.VMEM((FMB,1),full), pltpu.VMEM((FMB,PD),full), pltpu.VMEM((FF,D),low), pltpu.VMEM((FMB,D),full), pltpu.VMEM((D,FF),low), pltpu.SemaphoreType.DMA(())],
        compiler_params=pltpu.CompilerParams(vmem_limit_bytes=34*1024*1024),
        cost_estimate=pl.CostEstimate(flops=1, bytes_accessed=1, transcendentals=0),
        name="middle")(hidden, slope, down, first_low, final, down_bias, gain, shift, final_bias, targets, counts, masked)


def normalized(value):
    center = value - jnp.mean(value, axis=1, keepdims=True)
    inverse = lax.rsqrt(jnp.mean(center * center, axis=1, keepdims=True) + norm_eps)
    return center * inverse, inverse


def normalize_back(grad, hat, inverse):
    shift = jnp.mean(grad, axis=1, keepdims=True)
    return inverse * (grad - shift - hat * jnp.mean(grad * hat, axis=1, keepdims=True))


def vector(ref, name):
    start = 0
    for known, size in VECTORS:
        if known == name:
            return ref[:, start : start + size]
        start += size


def row_steps(rows=128):
    return [slice(r, r + rows) for r in range(0, FMB, rows)]


def join_rows(own_ref, got_ref, whole_ref, core, rows, to=slice(None), at=slice(None)):
    for value in range(2):
        @pl.when(core == value)
        def _():
            for r in range(0, own_ref.shape[0], rows):
                for c, ref in enumerate((own_ref, got_ref)):
                    begin = 2 * r + ((value + c) % 2) * rows
                    part = ref[r : r + rows, at].astype(whole_ref.dtype)
                    whole_ref[begin : begin + rows, to] = part


def front_kernel(
    rows, own_ref, got_ref, left_own_ref, left_got_ref, right_own_ref, right_got_ref, masked_ref,
    place_ref,
    inputs_ref, normed_ref, hat_ref, slope_ref, inverse_ref, taps_ref, proj_ref, vec_ref,
    final_ref, parts_ref, total_ref,
):
    core, section = place_ref[0, 0], place_ref[0, 1]
    half = C // 2
    join_rows(right_own_ref, right_got_ref, taps_ref, core, 2 * rows)
    join_rows(left_own_ref, left_got_ref, proj_ref, core, rows, at=slice(0, D))
    more = slice(D, D + PD + SPARE)
    join_rows(left_own_ref, left_got_ref, parts_ref, core, rows, at=more)
    spread_parts(rows, parts_ref, vec_ref)
    for d in range(C // rows):
        at = slice(d * rows, (d + 1) * rows)
        head, tail = parts_ref[at, :PD], parts_ref[d * rows : d * rows + rows // 2, PD:]
        to = d * (rows + rows // 2)
        final_ref[to : to + rows, :] = head.astype(full)
        final_ref[to + rows : to + rows + rows // 2, :] = tail.astype(full)
    for tap in range(2):
        cols = slice(tap * half, (tap + 1) * half)
        own_taps = taps_ref[pl.ds(pl.multiple_of(tap * C + section * half, half), half), :]
        got_taps = taps_ref[pl.ds(pl.multiple_of(tap * C + (1 - section) * half, half), half), :]
        part = plain_dot(own_ref[:, cols], own_taps) + plain_dot(got_ref[:, cols], got_taps)
        if tap == 0:
            total_ref[...] = part
        else:
            total_ref[...] += part
    for at in row_steps():
        lifted, slope = gelu_and_slope(total_ref[at, :])
        hat, inverse = normalized(lifted)
        slope_ref[at, :] = slope.astype(low)
        hat_ref[at, :] = hat.astype(low)
        inverse_ref[at, :] = inverse
        normed = hat * vector(vec_ref, "ln0_gain") + vector(vec_ref, "ln0_bias")
        normed_ref[at, :] = normed.astype(low)
    for at in row_steps():
        encoded = plain_dot(normed_ref[at, :], proj_ref[...]) + vector(vec_ref, "proj0_bias")
        encoded = jnp.where(masked_ref[at, :] > 0, vector(vec_ref, "mask_emb"), encoded)
        inputs_ref[at, :] = encoded.astype(low)


def first_kernel(
    inputs_ref, mixed_ref, out_ref, vec_ref, first_ref, hat_ref, inverse_ref, total_ref
):
    total_ref[...] = plain_dot(mixed_ref[...], out_ref[:, D:])
    for at in row_steps():
        value = inputs_ref[at, :].astype(full) + total_ref[at, :] + vector(vec_ref, "out_bias")
        hat, inverse = normalized(value)
        hat_ref[at, :] = hat.astype(low)
        inverse_ref[at, :] = inverse
        value = hat * vector(vec_ref, "ln1_gain") + vector(vec_ref, "ln1_bias")
        first_ref[at, :] = value.astype(low)


def first_back_kernel(
    d_pre_ref, up_ref, d_ffn_ref, hat_ref, inverse_ref, out_ref, vec_ref,
    d_attn_ref, d_mixed_ref, g_gain_ref, g_shift_ref, g_out_bias_ref, d_first_ref, held_ref, sems,
):
    part = right_dot(d_pre_ref[...], fetched(up_ref, held_ref, sems))

    @pl.when(pl.program_id(0) == 0)
    def _():
        d_first_ref[...] = d_ffn_ref[...].astype(full) + part

    @pl.when(pl.program_id(0) > 0)
    def _():
        d_first_ref[...] += part

    @pl.when(pl.program_id(0) == pl.num_programs(0) - 1)
    def _():
        g_gain = g_shift = g_out_bias = jnp.zeros((1, D), full)
        for at in row_steps():
            grad = d_first_ref[at, :]
            hat = hat_ref[at, :].astype(full)
            g_gain += column_sum(grad * hat)
            g_shift += column_sum(grad)
            grad = normalize_back(grad * vector(vec_ref, "ln1_gain"), hat, inverse_ref[at, :])
            grad = grad.astype(low)
            d_attn_ref[at, :] = grad
            g_out_bias += column_sum(grad.astype(full))
        g_gain_ref[...] = g_gain
        g_shift_ref[...] = g_shift
        g_out_bias_ref[...] = g_out_bias
        d_mixed_ref[...] = right_dot(d_attn_ref[...], out_ref[:, D:]).astype(low)


def first_backward(d_pre, ffn, d_ffn, hat, inverse, vo, vectors):
    def held(*shape):
        return pl.BlockSpec(shape, lambda i: (0, 0))

    return pl.pallas_call(
        first_back_kernel,
        grid=(FF // D,),
        in_specs=[
            pl.BlockSpec((FMB, D), lambda i: (0, i)),
            pl.BlockSpec(memory_space=pltpu.HBM),
            held(FMB, D),
            held(FMB, D),
            held(FMB, 1),
            held(D, 2 * D),
            held(1, VECTOR_TOTAL),
        ],
        out_specs=[held(FMB, D)] * 2 + [held(1, D)] * 3,
        out_shape=[jax.ShapeDtypeStruct((FMB, D), low)] * 2
        + [jax.ShapeDtypeStruct((1, D), full)] * 3,
        scratch_shapes=[
            pltpu.VMEM((FMB, D), full),
            pltpu.VMEM((FF // D, D, D), low),
            pltpu.SemaphoreType.DMA((FF // D,)),
        ],
        compiler_params=pltpu.CompilerParams(vmem_limit_bytes=28 * 1024 * 1024),
        cost_estimate=pl.CostEstimate(flops=1, bytes_accessed=1, transcendentals=0),
        name="first_backward",
    )(d_pre, ffn, d_ffn, hat, inverse, vo, vectors)


def inputs_back_kernel(
    d_qk_ref, d_values_ref, qk_ref, v_ref, d_attn_ref, masked_ref,
    d_encoded_ref, g_mask_ref, g_proj_bias_ref, g_query_ref, g_value_ref, total_ref,
):
    total_ref[...] = right_dot(d_qk_ref[...], qk_ref[...])
    total_ref[...] += right_dot(d_values_ref[...], v_ref[:, :D])
    g_mask = g_proj_bias = g_query = g_value = jnp.zeros((1, D), full)
    for at in row_steps():
        grad = total_ref[at, :] + d_attn_ref[at, :].astype(full)
        masked = masked_ref[at, :] > 0
        g_mask += column_sum(jnp.where(masked, grad, 0.0))
        grad = jnp.where(masked, 0.0, grad).astype(low)
        d_encoded_ref[at, :] = grad
        g_proj_bias += column_sum(grad.astype(full))
        g_query += column_sum(d_qk_ref[at, :D].astype(full))
        g_value += column_sum(d_values_ref[at, :].astype(full))
    g_mask_ref[...] = g_mask
    g_proj_bias_ref[...] = g_proj_bias
    g_query_ref[...] = g_query
    g_value_ref[...] = g_value


def front_back_kernel(
    d_encoded_ref, proj_ref, hat_ref, slope_ref, inverse_ref, vec_ref,
    d_conv_ref, g_gain_ref, g_shift_ref, total_ref,
):
    total_ref[...] = right_dot(d_encoded_ref[...], proj_ref[...])
    g_gain = g_shift = jnp.zeros((1, C), full)
    for at in row_steps():
        grad = total_ref[at, :]
        hat = hat_ref[at, :].astype(full)
        g_gain += column_sum(grad * hat)
        g_shift += column_sum(grad)
        grad = normalize_back(grad * vector(vec_ref, "ln0_gain"), hat, inverse_ref[at, :])
        d_conv_ref[at, :] = (grad * slope_ref[at, :].astype(full)).astype(low)
    g_gain_ref[...] = g_gain
    g_shift_ref[...] = g_shift


def each_pair(rows, each):
    step = 2 * each if rows % (2 * each) == 0 else each
    return [(slice(r, r + step), slice(2 * r, 2 * r + 2 * step)) for r in range(0, rows, step)]


def join_cores(own_ref, got_ref, whole_ref, core, each, width=512):
    cols = own_ref.shape[1]
    for c in range(0, cols, width):
        at = slice(c, min(c + width, cols))
        for lane, whole in each_pair(own_ref.shape[0], each):
            own, got = own_ref[lane, at].astype(full), got_ref[lane, at].astype(full)
            zero = jnp.where(core == 0, own, got)
            one = jnp.where(core == 0, got, own)
            parts = []
            for r in range(0, own.shape[0], each):
                parts += [zero[r : r + each], one[r : r + each]]
            whole_ref[whole, at] = jnp.concatenate(parts, 0).astype(low)


def split_cores(whole_ref, keep_ref, send_ref, core, each, begin=0, width=384):
    cols = whole_ref.shape[1]
    for c in range(0, cols, width):
        at = slice(c, min(c + width, cols))
        to = slice(begin + at.start, begin + at.stop)
        for lane, whole in each_pair(whole_ref.shape[0] // 2, each):
            zero, one = [], []
            for r in range(whole.start, whole.stop, 2 * each):
                zero.append(whole_ref[r : r + each, at])
                one.append(whole_ref[r + each : r + 2 * each, at])
            zero, one = jnp.concatenate(zero, 0), jnp.concatenate(one, 0)
            keep_ref[lane, to] = jnp.where(core == 0, zero, one).astype(low)
            send_ref[lane, to] = jnp.where(core == 0, one, zero).astype(low)


def qkv_kernel(
    each, inputs_ref, qk_own_ref, qk_got_ref, vo_own_ref, vo_got_ref, vec_ref, core_ref,
    qk_ref, vo_ref, qk_rows_ref, values_ref,
):
    core = core_ref[0, 0]
    join_cores(qk_own_ref, qk_got_ref, qk_ref, core, each)
    join_cores(vo_own_ref, vo_got_ref, vo_ref, core, each)
    bias = vector(vec_ref, "qv_bias")
    rows = plain_dot(inputs_ref[...], qk_ref[:, :D]) + bias[:, :D]
    qk_rows_ref[:, :D] = rows.astype(low)
    qk_rows_ref[:, D:] = plain_dot(inputs_ref[...], qk_ref[:, D:]).astype(low)
    rows = plain_dot(inputs_ref[...], vo_ref[:, :D]) + bias[:, D:]
    values_ref[...] = rows.astype(low)


def lanes_kernel(each, up_ref, up_got_ref, down_ref, down_got_ref, out_ref):
    out_ref[0, 0, 0, :each, :] = added(up_ref[0], up_got_ref[0])
    for j in range(FF // D):
        rows = slice(j * each, (j + 1) * each)
        part = added(down_ref[0, rows, :], down_got_ref[0, rows, :])
        out_ref[0, 0, 0, each:, j * D : (j + 1) * D] = part


def add_lanes(each, depth, up, up_got, down, down_got):
    def where(i):
        return (i // (2 * depth), i % 2, (i // 2) % depth, 0, 0)

    up_rows = pl.BlockSpec((1, each, FF), lambda i: (i, 0, 0))
    down_rows = pl.BlockSpec((1, each * FF // D, D), lambda i: (i, 0, 0))
    up, up_got = [t.reshape(4 * depth, each, FF) for t in (up, up_got)]
    down, down_got = [t.reshape(4 * depth, each * FF // D, D) for t in (down, down_got)]
    return pl.pallas_call(
        functools.partial(lanes_kernel, each),
        grid=(4 * depth,),
        in_specs=[up_rows, up_rows, down_rows, down_rows],
        out_specs=pl.BlockSpec((1, 1, 1, 2 * each, FF), where),
        out_shape=jax.ShapeDtypeStruct((2, 2, depth, 2 * each, FF), low),
        compiler_params=pltpu.CompilerParams(vmem_limit_bytes=8 * 1024 * 1024),
        cost_estimate=pl.CostEstimate(flops=1, bytes_accessed=1, transcendentals=0),
        name="add_lanes",
    )(up, up_got, down, down_got)


def heads_grad_kernel(
    each, inputs_ref, mixed_ref, d_qk_ref, d_values_ref, d_attn_ref, core_ref,
    keep_ref, send_ref, turned_ref, total_ref,
):
    core = core_ref[0, 0]
    turned_ref[...] = inputs_ref[...].T
    for begin, rhs in (
        (0, d_qk_ref[:, :D]),
        (D, d_qk_ref[:, D:]),
        (2 * D, d_values_ref[...]),
        (3 * D, d_attn_ref[...]),
    ):
        if begin == 3 * D:
            turned_ref[...] = mixed_ref[...].T
        total_ref[...] = plain_dot(turned_ref[...], rhs)
        split_cores(total_ref, keep_ref, send_ref, core, each, begin)


def misc_grad_kernel(
    rows, each, normed_ref, d_encoded_ref, second_ref, d_proj_ref, own_ref, got_ref, d_conv_ref,
    vectors_ref, section_ref, terms_ref, final_ref, taps_ref,
):
    section = section_ref[0, 0]
    half = C // 2
    terms_ref[:, :D] = plain_dot(normed_ref[...].T, d_encoded_ref[...]).astype(low)
    final_ref[...] = plain_dot(second_ref[...].T, d_proj_ref[...])
    for d in range(C // rows):
        to = slice(d * rows, d * rows + rows)
        terms_ref[to, D : D + PD] = final_ref[d * each : d * each + rows, :].astype(low)
        last = [final_ref[d * each + rows : (d + 1) * each, :]]
        last.append(vectors_ref[d * (rows // 2) : (d + 1) * (rows // 2), :])
        terms_ref[to, D + PD : D + PD + SPARE] = jnp.concatenate(last, 0).astype(low)
    taps_ref[:C, :] = plain_dot(own_ref[...].T, d_conv_ref[...])
    taps_ref[C:, :] = plain_dot(got_ref[...].T, d_conv_ref[...])
    for tap in range(2):
        for side in range(2):
            for r in range(0, half, 2 * rows):
                at = tap * half + r
                own, got = taps_ref[at : at + 2 * rows, :], taps_ref[C + at : C + at + 2 * rows, :]
                value = jnp.where(section == side, own, got).astype(low)
                d = (tap * C + side * half + r) // (2 * rows)
                begin = D + PD + SPARE
                terms_ref[d * rows : (d + 1) * rows, begin : begin + C] = value[:rows]
                terms_ref[d * rows : (d + 1) * rows, begin + C :] = value[rows:]


def local_kernel(kernel, outs, scratch=(), scalars=0, static=(), far_in=(), far_out=()):
    def call(*args):
        near = len(args) - scalars
        held = [(args[i].shape, args[i].dtype) for i in far_in] + [outs[i] for i in far_out]
        first_held = len(args) + len(outs) + len(scratch)

        def run(*refs):
            refs, held_refs, sems = list(refs[:first_held]), refs[first_held:-2], refs[-2:]
            ins = [
                pltpu.make_async_copy(refs[i], held_refs[k], sems[0].at[k])
                for k, i in enumerate(far_in)
            ]
            ends = [
                pltpu.make_async_copy(
                    held_refs[len(far_in) + k], refs[len(args) + i], sems[1].at[k]
                )
                for k, i in enumerate(far_out)
            ]
            for copy in ins:
                copy.start()
            for copy in ins:
                copy.wait()
            for k, i in enumerate(list(far_in) + [len(args) + i for i in far_out]):
                refs[i] = held_refs[k]
            kernel(*static, *refs)
            for copy in ends:
                copy.start()
            for copy in ends:
                copy.wait()

        def space(index, far):
            return pl.BlockSpec(memory_space=pltpu.HBM if index in far else pltpu.VMEM)

        everything = [(a.shape, a.dtype) for a in args] + list(outs) + list(scratch)
        size = sum(math.prod(shape) * jnp.dtype(dtype).itemsize for shape, dtype in everything)
        return pl.pallas_call(
            run,
            out_shape=[jax.ShapeDtypeStruct(shape, dtype) for shape, dtype in outs],
            in_specs=[space(i, far_in) for i in range(near)]
            + [pl.BlockSpec(memory_space=pltpu.SMEM)] * scalars,
            out_specs=[space(i, far_out) for i in range(len(outs))],
            scratch_shapes=[pltpu.VMEM(shape, dtype) for shape, dtype in list(scratch) + held]
            + [pltpu.SemaphoreType.DMA((max(len(far), 1),)) for far in (far_in, far_out)],
            compiler_params=pltpu.CompilerParams(vmem_limit_bytes=56 * 1024 * 1024 if kernel.__name__ in ('front_kernel',) else size + 4 * 1024 * 1024),
            cost_estimate=pl.CostEstimate(flops=1, bytes_accessed=1, transcendentals=0),
            name=kernel.__name__,
        )(*args)

    return call


def fetched(ffn_ref, held_ref, sems):
    step, width = pl.program_id(0), held_ref.shape[2]

    def copy(k):
        source = ffn_ref.at[0, :, k * width : (k + 1) * width]
        return pltpu.make_async_copy(source, held_ref.at[k], sems.at[k])

    for k in range(held_ref.shape[0]):
        @pl.when(step == 0)
        def _():
            copy(k).start()

    for k in range(held_ref.shape[0]):
        @pl.when(step == k)
        def _():
            copy(k).wait()

    return held_ref[step]


def up_kernel(x_ref, ffn_ref, bias_ref, hidden_ref, slope_ref, pre_ref, held_ref, sems):
    pre_ref[...] = plain_dot(x_ref[...], fetched(ffn_ref, held_ref, sems))
    bias = bias_ref[...]
    for at in row_steps(64):
        value, slope = gelu_and_slope(pre_ref[at, :] + bias)
        hidden_ref[at, :] = value.astype(low)
        slope_ref[at, :] = slope.astype(low)


def up_forward(x, ffn, vectors, tile=1024):
    begin = start_of["up_bias"] // tile
    columns = pl.BlockSpec((FMB, tile), lambda i: (0, i))
    return pl.pallas_call(
        up_kernel,
        grid=(FF // tile,),
        in_specs=[
            pl.BlockSpec((FMB, D), lambda i: (0, 0)),
            pl.BlockSpec(memory_space=pltpu.HBM),
            pl.BlockSpec((1, tile), lambda i: (0, begin + i)),
        ],
        out_specs=[columns, columns],
        out_shape=[jax.ShapeDtypeStruct((FMB, FF), low)] * 2,
        scratch_shapes=[
            pltpu.VMEM((FMB, tile), full),
            pltpu.VMEM((FF // tile, D, tile), low),
            pltpu.SemaphoreType.DMA((FF // tile,)),
        ],
        compiler_params=pltpu.CompilerParams(vmem_limit_bytes=46 * 1024 * 1024),
        cost_estimate=pl.CostEstimate(flops=1, bytes_accessed=1, transcendentals=0),
        name="up_forward",
    )(x, ffn, vectors)


def body(
    features,
    conv_weight,
    ln0_gain,
    ln0_bias,
    proj0_weight,
    proj0_bias,
    mask_emb,
    qkv_weight,
    qv_bias,
    out_weight,
    out_bias,
    ln1_gain,
    ln1_bias,
    up_weight,
    up_bias,
    down_weight,
    down_bias,
    ln2_gain,
    ln2_bias,
    final_weight,
    final_bias,
    codebook,
    lengths,
    mask_pos,
    distractors,
    target_ids,
):
    links = Links()
    section = links.y
    core = links.core.reshape(1, 1).astype(jnp.int32)
    place = jnp.stack([links.core, links.y]).reshape(1, 2).astype(jnp.int32)
    devices = 2 * links.per_section
    rows = C // devices

    own_rows = pick(features, section, 0)
    lens = pick(lengths, section, 0)
    positions = pick(mask_pos, section, 0)
    chosen = pick(distractors, section, 0)
    target_rows = pick(target_ids, section, 0)

    each = D // devices
    slot = (rows // 2) * SPARE // SLOTS
    blocks = FF // D
    down_blocks = down_weight.reshape(blocks, each, D).transpose(1, 0, 2).reshape(each, FF)
    ffn_full = lax.all_gather(jnp.stack([up_weight, down_blocks]), BOTH, axis=1, tiled=True)
    heads = Gather(links, jnp.concatenate([qkv_weight, out_weight], axis=1), 2 * D)
    heads.start_z()
    got_rows = links.over_y(pick(features, 1 - section, 0))
    late = (up_bias, proj0_weight, chosen)
    late = after([heads], *late)
    up_bias, proj0_weight, chosen = late
    heads.start_z_rest()
    vector_parts = [
        up_bias,
        ln0_gain,
        ln0_bias,
        proj0_bias,
        mask_emb,
        qv_bias,
        out_bias,
        ln1_gain,
        ln1_bias,
        down_bias,
        ln2_gain,
        ln2_bias,
        final_bias,
    ]
    vector_parts += [vector_parts[0]] * (SLOTS - len(vector_parts))
    vector_part = jnp.stack([jnp.pad(v, (0, slot - v.shape[0])) for v in vector_parts])
    misc = Gather(
        links,
        jnp.concatenate(
            [
                proj0_weight,
                final_weight[:rows],
                jnp.concatenate([final_weight[rows:], vector_part.reshape(rows // 2, SPARE)], 0),
                conv_weight[:rows],
                conv_weight[rows:],
            ],
            axis=1,
        ),
        D + PD + SPARE,
        parts=2,
    )
    misc.start_z()
    drawn = count_distractors(chosen)
    (drawn,) = after([heads, misc], drawn)

    heads.start_first()
    misc.start_z_rest()
    frame_ids = jnp.arange(FMB, dtype=jnp.int32)
    at_frame = positions[:, None] == frame_ids[None, :]
    is_masked = jnp.any(at_frame, axis=0)
    own_frame = (frame_ids[:, None] == frame_ids[None, :]) & is_masked[:, None]
    counts = lax.dot_general(
        at_frame.astype(low), drawn, (((0,), (1,)), ((), ())), preferred_element_type=full
    ) + own_frame.astype(full)
    entries = jnp.arange(codebook.shape[1], dtype=jnp.int32)
    targets = jnp.concatenate(
        [
            plain_dot((target_rows[0][:, None] == entries[None, :]).astype(low), codebook[0]),
            plain_dot((target_rows[1][:, None] == entries[None, :]).astype(low), codebook[1]),
        ],
        axis=1,
    )
    targets = targets * lax.rsqrt(jnp.sum(targets * targets, axis=1, keepdims=True) + unit_eps)
    stops = jnp.cumsum(lens)
    segment = jnp.sum(
        (frame_ids[:, None] >= stops[None, : UTTS - 1]).astype(jnp.int32), axis=1
    )
    masked = is_masked[:, None].astype(full)
    own_pairs = own_rows.reshape(FMB, C)
    counts, targets, got_rows, own_pairs, segment = after(
        [heads, misc], counts, targets, got_rows, own_pairs, segment
    )

    heads.start_second()
    misc.start_first()
    got_pairs = got_rows.reshape(FMB, C)
    (got_pairs,) = after([heads, misc], got_pairs)

    misc.start_second()
    heads.start_core()
    misc.start_core()
    half = C // 2
    (
        inputs, normed, hat_zero, conv_slope, inverse_zero, conv_full, proj_full, vectors, final_full
    ) = local_kernel(
        front_kernel,
        [
            ((FMB, D), low),
            ((FMB, C), low),
            ((FMB, C), low),
            ((FMB, C), low),
            ((FMB, 1), full),
            ((2 * C, C), low),
            ((C, D), low),
            ((1, VECTOR_TOTAL), full),
            ((D, PD), full),
        ],
        [((C, PD + SPARE), low), ((FMB, C), full)],
        scalars=1,
        static=(rows,),
        far_in=(0, 1),
        far_out=(1, 2, 3, 4, 5, 6, 8),
    )(own_pairs, got_pairs, *misc.apart(), masked, place)
    taps = conv_full.reshape(2, 2, half, C)
    own_taps = pick(taps, section, 1).reshape(C, C)
    got_taps = pick(taps, 1 - section, 1).reshape(C, C)
    qk_full, vo_full, qk_rows, value_rows = local_kernel(
        qkv_kernel,
        [((D, 2 * D), low), ((D, 2 * D), low), ((FMB, 2 * D), low), ((FMB, D), low)],
        scalars=1,
        static=(each,),
        far_out=(0,),
    )(inputs, *heads.apart(), vectors, core)
    mixed, logs = attention_forward(qk_rows, value_rows, segment)
    first_low, hat_one, inverse_one = local_kernel(
        first_kernel, [((FMB, D), low), ((FMB, D), low), ((FMB, 1), full)], [((FMB, D), full)],
        far_out=(1, 2),
    )(inputs, mixed, vo_full, vectors)
    hidden_low, slope = up_forward(first_low, ffn_full, vectors)
    grad = {}
    (
        second_low,
        d_proj_low,
        d_ffn_low,
        d_pre_low,
        loss,
        grad["down_bias"],
        grad["ln2_gain"],
        grad["ln2_bias"],
        grad["final_bias"],
        grad["up_bias"],
    ) = middle(
        each,
        hidden_low,
        slope,
        ffn_full,
        first_low,
        final_full,
        *[
            vectors[:, start_of[name] : start_of[name] + size]
            for name, size in VECTORS
            if name in ("down_bias", "ln2_gain", "ln2_bias", "final_bias")
        ],
        targets,
        counts,
        masked,
    )

    loss = jnp.where(jnp.arange(2) == section, loss[0], 0.0)
    loss_got = links.over_y(loss)
    g_down = left_dot(hidden_low, d_ffn_low).astype(low)
    down = Sum(links, *by_core(links, g_down), D // 2)
    down.start_core()
    g_up = left_dot(first_low, d_pre_low).astype(low)
    up = Sum(links, *by_core(links, g_up), FF // 2)
    up.start_core()
    d_attn_low, d_mixed, grad["ln1_gain"], grad["ln1_bias"], grad["out_bias"] = (
        first_backward(d_pre_low, ffn_full, d_ffn_low, hat_one, inverse_one, vo_full, vectors)
    )
    d_mixed, d_attn_low, loss_got = after([down, up], d_mixed, d_attn_low, loss_got)

    lanes = add_lanes(
        each, links.depth, up.keep.reshape(-1, FF), up.got[0], down.keep.reshape(-1, D), down.got[0]
    )
    line = lax.psum_scatter(
        lanes.reshape(-1, FF), ("section", "x"), scatter_dimension=0, tiled=True
    ).reshape(links.depth, 2 * each, FF)
    d_qk, d_values = attention_backward(qk_rows, value_rows, segment, d_mixed, logs)
    keep, send = local_kernel(
        heads_grad_kernel,
        [((D // 2, 4 * D), low)] * 2,
        [((D, FMB), low), ((D, D), full)],
        scalars=1,
        static=(each,),
        far_in=(0, 1),
    )(inputs, mixed, d_qk, d_values, d_attn_low, core)

    heads = Sum(links, keep, send, 2 * D)
    heads.start_core()
    d_encoded, grad["mask_emb"], grad["proj0_bias"], g_query, g_value = local_kernel(
        inputs_back_kernel, [((FMB, D), low)] + [((1, D), full)] * 4, [((FMB, D), full)], far_in=(2, 3)
    )(d_qk, d_values, qk_full, vo_full, d_attn_low, masked)
    grad["qv_bias"] = jnp.concatenate([g_query, g_value], axis=1)
    (d_encoded,) = after([heads], d_encoded)

    heads.start_first()
    d_conv_low, grad["ln0_gain"], grad["ln0_bias"] = local_kernel(
        front_back_kernel,
        [((FMB, C), low), ((1, C), full), ((1, C), full)],
        [((FMB, C), full)],
        far_in=(1, 2, 3, 4),
    )(d_encoded, proj_full, hat_zero, conv_slope, inverse_zero, vectors)
    g_vectors = split_vectors([grad[name] for name, _ in VECTORS], devices, slot)
    g_vectors = g_vectors.transpose(1, 0, 2).reshape(devices * (rows // 2), SPARE)
    (terms,) = local_kernel(
        misc_grad_kernel,
        [((C, D + PD + SPARE + 2 * C), low)],
        [((D, PD), full), ((2 * C, C), full)],
        scalars=1,
        static=(rows, each),
        far_in=(0, 2, 3, 4, 5),
    )(
        normed, d_encoded, second_low, d_proj_low, own_pairs, got_pairs, d_conv_low, g_vectors,
        section.reshape(1, 1).astype(jnp.int32),
    )
    misc = Sum(links, *by_core(links, terms), D + PD + SPARE)
    misc.start_core()
    got_d = right_dot(d_conv_low, got_taps).astype(low).reshape(2 * FMB, half)
    own_d = right_dot(d_conv_low, own_taps).reshape(2 * FMB, half)
    own_d, got_d, line = after([misc, heads], own_d, got_d, line)

    heads.start_second()
    misc.start_first()
    ffn = Line(links, line)
    ffn.start_z()
    (got_d,) = after([heads, misc], got_d)
    got_d = links.over_y(got_d)

    heads.start_z()
    misc.start_second()
    ffn.start_z_rest()
    after([heads, misc])

    heads.start_z_rest()
    misc.start_z()
    after([misc])
    misc.start_z_rest()
    features_grad = in_order(section, own_d, got_d.astype(full), -2)
    loss_each = loss + loss_got
    ffn_sum, heads_sum, misc_sum = ffn.total(), heads.total(), misc.total()
    up_sum = ffn_sum[:each]
    down_sum = jnp.concatenate(jnp.split(ffn_sum[each:], blocks, axis=1), axis=0)
    qkv_sum, out_sum = heads_sum[:, : 3 * D], heads_sum[:, 3 * D :]
    proj_sum = misc_sum[:, :D]
    left, right = misc_sum[:, D : D + PD + SPARE], misc_sum[:, D + PD + SPARE :]
    conv_sum = jnp.concatenate([right[:, :C], right[:, C:]], axis=0)
    final_sum = jnp.concatenate([left[:, :PD], left[: rows // 2, PD:]], axis=0)
    vector_sum = left[rows // 2 :, PD:].reshape(SLOTS, slot)
    share = {}
    for index, (name, size) in enumerate(VECTORS):
        share[name] = vector_sum[index, : size // devices]
    return (
        loss_each,
        features_grad,
        conv_sum,
        share["ln0_gain"],
        share["ln0_bias"],
        proj_sum,
        share["proj0_bias"],
        share["mask_emb"],
        qkv_sum,
        share["qv_bias"],
        out_sum,
        share["out_bias"],
        share["ln1_gain"],
        share["ln1_bias"],
        up_sum,
        share["up_bias"],
        down_sum,
        share["down_bias"],
        share["ln2_gain"],
        share["ln2_bias"],
        final_sum,
        share["final_bias"],
    )


def solution(mesh):
    grid = mesh.devices.reshape(2, -1, 2, 2)
    rows = P(BOTH, None)
    part = P(BOTH)
    weights = (rows, part, part, rows, part, part, rows, part, rows, part, part, part)
    weights += (rows, part, rows, part, part, part, rows, part)
    batch = [P(SPLIT, *[None] * more) for more in (1, 1, 2, 2)]
    return jax.shard_map(
        body,
        mesh=jax.sharding.Mesh(grid, BOTH),
        in_specs=(P(SPLIT, None, "section"),) + weights + (P(), *batch),
        out_specs=(P(SPLIT), P(SPLIT, None, "section")) + weights,
        check_vma=False,
    )
```
